32 devices in a mesh: groups: 2 (over x), experts: 16 (over z, y, core).
Axes of the slice: x: 2, y: 2, z: 4, core: 2. Of those that a mesh axis runs over, the one named last changes fastest.
Arguments:
- queries: bfloat16 [128, 576, 64], P(('groups', 'experts')), parts along dimension 0, may hold values from -21 to 21
- cache: bfloat16 [128, 576, 4096], P(('groups', 'experts')), parts along dimension 0, may hold values from -6 to 6
- cache_len: int32 [128], P(('groups', 'experts')), parts along dimension 0, may hold values from 2 to 4096, as said below
- residual_in: bfloat16 [128, 7168], P(('groups', 'experts')), parts along dimension 0, may hold values from -24 to 24
- w_absorb: bfloat16 [64, 512, 128], P('experts'), may hold values from -0.5 to 0.5
- w_out: bfloat16 [8192, 7168], P('experts'), may hold values from -0.0625 to 0.0625
- norm_gain: float32 [7168], replicated, may hold values from 0.1 to 1.9
- expert_ids: int32 [128, 2], P('groups'), parts along dimension 0, may hold values from 0 to 1, as said below
- route_gates: float32 [128, 2], P(('groups', 'experts')), parts along dimension 0, may hold values from 0.3 to 1.5
- w_gate: bfloat16 [7168, 4096], P(None, 'experts'), may hold values from -0.0625 to 0.0625
- w_up: bfloat16 [7168, 4096], P(None, 'experts'), may hold values from -0.0625 to 0.0625
- w_down: bfloat16 [4096, 7168], P('experts'), may hold values from -0.125 to 0.125
Outputs:
- attended: bfloat16 [128, 7168], P(('groups', 'experts')), parts along dimension 0
- expert_out: bfloat16 [128, 7168], P(('groups', 'experts')), parts along dimension 0
The draws below stay inside these ranges and needn't reach their ends.
There are 2 independent parts, one for each index of `groups`. The reference program is written for one: setup_inputs(seed, part) draws one part's arguments, and reference() takes and returns one part's arrays. A program takes and returns all parts, laid end to end along the dimension named above; an argument that names none is the same for every part. Nothing has to cross between parts.
Inputs may be any that keep to these rules, and one draw needn't show every extreme that they name: `expert_ids`: each row names 2 different experts; one expert, the same for all rows of a draw, is named by every row. `cache_len`: some request has exactly 4096 valid positions.
All inputs are finite; a program needn't handle non-finite values.
Results may differ from the reference program's by a relative error of at most 0.0097.
Values may be sent and summed in bfloat16 or wider, within the bound.
No kernel may reach another device: no remote copies, remote signals or barrier semaphores. Data moves between devices by JAX's collectives and lax.ppermute only.
A program may use at most 128 MiB of HBM per device.

```python
import jax
import jax.numpy as jnp
from jax import lax

D = 7168
KVR = 512
ROPE = 64
VH = 128
QK = 192
FF = 2048
TOP = 2
LMAX = 4096
HEADS = 64
ROWS = 64
EXPERTS = 2


def draw_cache(key, part):
    key = jax.random.fold_in(key, 1)
    base = jnp.clip(jax.random.normal(key, (ROWS, KVR + ROPE, LMAX), jnp.float32), -6.0, 6.0)
    return base.astype(jnp.bfloat16)


def draw_queries(key, part):
    key = jax.random.fold_in(key, 2)
    base = 2.0 * jnp.clip(jax.random.normal(key, (ROWS, KVR + ROPE, HEADS), jnp.float32), -6.0, 6.0)
    return base.astype(jnp.bfloat16)


def draw_residual_in(key, part):
    key = jax.random.fold_in(key, 3)
    keys = jax.random.split(key, 3)
    row_scale = 10.0 ** jax.random.uniform(keys[0], (ROWS, 1), jnp.float32, -0.5, 0.5)
    col_scale = 10.0 ** jax.random.uniform(keys[1], (1, D), jnp.float32, -0.5, 0.5)
    base = jnp.clip(jax.random.normal(keys[2], (ROWS, D), jnp.float32), -6.0, 6.0)
    return (0.4 * base * row_scale * col_scale).astype(jnp.bfloat16)


def draw_cache_len(key, part):
    key = jax.random.fold_in(key, 4)
    keys = jax.random.split(key, 3)
    first = jax.random.randint(keys[0], (ROWS,), 0, LMAX - 1)
    second = jax.random.randint(keys[1], (ROWS,), 0, LMAX - 1)
    lengths = 2 + first * second // (LMAX - 2)
    longest = jax.random.randint(keys[2], (), 0, ROWS)
    lengths = jnp.where(jnp.arange(ROWS) == longest, LMAX, lengths)
    return lengths.astype(jnp.int32)


def draw_expert_ids(key, part):
    key = jax.random.fold_in(key, 5)
    keys = jax.random.split(key, 2)
    hottest = jax.random.randint(keys[0], (), 0, EXPERTS)
    column = jnp.arange(EXPERTS, dtype=jnp.int32)[None, :]
    ranking = jax.random.randint(keys[1], (ROWS, EXPERTS), 0, 1 << 20) * EXPERTS + column
    ranking = jnp.where(column == hottest, -1, ranking)
    return jnp.argsort(ranking, axis=-1, stable=True)[:, :TOP].astype(jnp.int32)


def block_levels(own_key, shape, cuts, smallest, top_value):
    loudness = 1.0
    for axis_at, parts in cuts:
        draws = jax.random.uniform(jax.random.fold_in(jax.random.fold_in(own_key, 6), axis_at), (parts,), jnp.float32, smallest / len(cuts), top_value / len(cuts))
        loudness = loudness * jnp.repeat(jnp.exp(draws), shape[axis_at] // parts).reshape((-1,) + (1,) * (len(shape) - 1 - axis_at))
    return loudness


def bell_draw(rng, extent, deviation, bound, cuts=(), kind=jnp.bfloat16):
    array = jax.random.normal(rng, extent, jnp.float32) * deviation
    if len(cuts) > 0:
        array = block_levels(rng, extent, cuts, -0.22, 0.18) * array
    return jnp.clip(array, min=-bound, max=bound).astype(kind)


def setup_inputs(seed: int = 0, part: int = 0) -> dict:
    seeds = jax.random.split(jax.random.key(seed), 13)
    part_splits = jax.random.split(jax.random.fold_in(seeds[12], part), 13)
    return {
        "queries": draw_queries(jax.random.fold_in(jax.random.fold_in(seeds[12], part), 71), part),
        "cache": draw_cache(jax.random.fold_in(jax.random.fold_in(seeds[12], part), 71), part),
        "cache_len": draw_cache_len(jax.random.fold_in(jax.random.fold_in(seeds[12], part), 71), part),
        "residual_in": draw_residual_in(jax.random.fold_in(jax.random.fold_in(seeds[12], part), 71), part),
        "w_absorb": bell_draw(seeds[4], (HEADS, KVR, VH), VH ** -0.5, 0.5, ((0, 16),)),
        "w_out": bell_draw(seeds[5], (HEADS * VH, D), (HEADS * VH) ** -0.5, 0.0625, ((0, 16),)),
        "norm_gain": jnp.clip(1.0 + 0.18 * jax.random.normal(seeds[6], (D,), jnp.float32), 0.1, 1.9),
        "expert_ids": draw_expert_ids(jax.random.fold_in(jax.random.fold_in(seeds[12], part), 71), part),
        "route_gates": jnp.clip(0.3 + 1.2 * jax.random.uniform(part_splits[8], (ROWS, TOP), jnp.float32) ** block_levels(part_splits[8], (ROWS, TOP), ((0, 16),), -0.2, 0.2), 0.3, 1.5),
        "w_gate": bell_draw(seeds[9], (D, EXPERTS * FF), D ** -0.5, 0.0625, ((1, 16),)),
        "w_up": bell_draw(seeds[10], (D, EXPERTS * FF), D ** -0.5, 0.0625, ((1, 16),)),
        "w_down": bell_draw(seeds[11], (EXPERTS * FF, D), FF ** -0.5, 0.125, ((0, 16),)),
    }


def reference(queries, cache, cache_len, residual_in, w_absorb, w_out, norm_gain, expert_ids, route_gates, w_gate, w_up, w_down):
    score_scale = QK ** (-0.5)
    positions = jnp.arange(LMAX, dtype=jnp.int32)

    def attend_row(row_data):
        query_row, key_block, length = row_data
        scores = jnp.dot(query_row.T, key_block, preferred_element_type=jnp.float32) * score_scale
        scores = jnp.where(positions[None, :] < length, scores, -jnp.inf)
        soft_w = jax.nn.softmax(scores, axis=-1).astype(jnp.bfloat16)
        latent_row = jnp.dot(soft_w, key_block[:KVR].T, preferred_element_type=jnp.float32)
        return latent_row.astype(jnp.bfloat16)
    latent = lax.map(attend_row, (queries, cache, cache_len))
    head_values = jnp.einsum('rhc,hcv->rhv', latent.astype(jnp.float32), w_absorb.astype(jnp.float32)).astype(jnp.bfloat16)
    attention = jnp.dot(head_values.reshape(ROWS, HEADS * VH), w_out, preferred_element_type=jnp.float32)
    attended = (residual_in.astype(jnp.float32) + attention).astype(jnp.bfloat16)
    widened = attended.astype(jnp.float32)
    inverse = lax.rsqrt(lax.optimization_barrier(jnp.mean(widened * widened, axis=-1, keepdims=True)) + 1e-06)
    normed = (widened * inverse * norm_gain).astype(jnp.bfloat16)
    gate_proj = jnp.dot(normed, w_gate, preferred_element_type=jnp.float32)
    up_proj = jnp.dot(normed, w_up, preferred_element_type=jnp.float32)
    activated = (jax.nn.silu(gate_proj) * up_proj).astype(jnp.bfloat16)
    expert_all = jnp.einsum('ref,efd->erd', activated.reshape(ROWS, EXPERTS, FF).astype(jnp.float32), w_down.reshape(EXPERTS, FF, D).astype(jnp.float32))
    expert_iota = jnp.arange(EXPERTS, dtype=jnp.int32)
    mixing = lax.optimization_barrier(jnp.sum(route_gates[:, :, None] * (expert_ids[:, :, None] == expert_iota[None, None, :]).astype(jnp.float32), axis=1))
    expert_out = jnp.einsum('re,erd->rd', mixing, expert_all, precision=lax.Precision.HIGHEST)
    return (attended, expert_out.astype(jnp.bfloat16))
```

```python
import jax
import jax.numpy as jnp
from jax import lax
from jax.sharding import PartitionSpec as P

QK = 192
FF = 2048


def rms_scale(stream, norm_gain):
    widened = stream.astype(jnp.float32)
    inverse = lax.rsqrt(jnp.mean(widened * widened, axis=-1, keepdims=True) + 1e-06)
    return (widened * inverse * norm_gain).astype(jnp.bfloat16)


def shards(
    queries,
    cache,
    cache_len,
    residual_in,
    w_absorb,
    w_out,
    norm_gain,
    expert_ids,
    route_gates,
    w_gate,
    w_up,
    w_down,
):
    devices = lax.axis_size("experts")
    rank_here = lax.axis_index("experts")
    own_rows = queries.shape[0]
    all_rows = expert_ids.shape[0]
    latent_rank = w_absorb.shape[1]
    width = residual_in.shape[1]
    split_ways = FF // w_gate.shape[1]
    gates_all = lax.all_gather(route_gates, "experts", axis=0, tiled=True)
    expert_here = rank_here // split_ways
    mixing = jnp.sum(
        gates_all * (expert_ids == expert_here).astype(jnp.float32), axis=1, keepdims=True
    )
    positions = lax.broadcasted_iota(jnp.int32, (1, 1, cache.shape[2]), 2)
    scores = jnp.einsum(
        "rch,rcp->rhp", queries, cache, preferred_element_type=jnp.float32
    ) * QK ** (-0.5)
    scores = jnp.where(positions < cache_len[:, None, None], scores, -jnp.inf)
    soft_w = jax.nn.softmax(scores, axis=-1).astype(jnp.bfloat16)
    latent = jnp.einsum(
        "rhp,rcp->rhc", soft_w, cache[:, :latent_rank, :], preferred_element_type=jnp.float32
    ).astype(jnp.bfloat16)
    by_head = lax.all_to_all(latent, "experts", split_axis=1, concat_axis=0, tiled=True)
    head_values = jnp.einsum(
        "rhc,hcv->rhv", by_head, w_absorb, preferred_element_type=jnp.float32
    ).astype(jnp.bfloat16)
    head_term = jnp.dot(
        head_values.reshape(all_rows, -1), w_out, preferred_element_type=jnp.float32
    ).astype(jnp.bfloat16)
    terms = lax.all_to_all(
        head_term.reshape(devices, own_rows, width), "experts", split_axis=0, concat_axis=0, tiled=True
    )
    summed = jnp.sum(terms.astype(jnp.float32), axis=0)
    attended = (residual_in.astype(jnp.float32) + summed).astype(jnp.bfloat16)
    attended_all = lax.all_gather(attended, "experts", axis=0, tiled=True)
    normed_all = rms_scale(attended_all, norm_gain)
    gate_proj = jnp.dot(normed_all, w_gate, preferred_element_type=jnp.float32)
    up_proj = jnp.dot(normed_all, w_up, preferred_element_type=jnp.float32)
    activated = (jax.nn.silu(gate_proj) * up_proj).astype(jnp.bfloat16)
    partials = jnp.dot(activated, w_down, preferred_element_type=jnp.float32)
    sent = (partials * mixing).astype(jnp.bfloat16).reshape(devices, own_rows, width)
    returned = lax.all_to_all(sent, "experts", split_axis=0, concat_axis=0, tiled=True)
    expert_out = jnp.sum(returned.astype(jnp.float32), axis=0)
    return (attended, expert_out.astype(jnp.bfloat16))


def solution(mesh):
    placed = (
        P(("groups", "experts"), None, None),
        P(("groups", "experts"), None, None),
        P(("groups", "experts")),
        P(("groups", "experts"), None),
        P("experts", None, None),
        P("experts", None),
        P(),
        P("groups", None),
        P(("groups", "experts"), None),
        P(None, "experts"),
        P(None, "experts"),
        P("experts", None),
    )
    return jax.shard_map(
        shards,
        mesh=mesh,
        in_specs=placed,
        out_specs=(P(("groups", "experts"), None), P(("groups", "experts"), None)),
        check_vma=False,
    )
```

```python
import jax
import jax.numpy as jnp
from jax import lax
from jax.experimental import pallas as pl
from jax.experimental.pallas import tpu as pltpu
from jax.sharding import PartitionSpec as P

QK = 192
FF = 2048
BLOCK = 512
LANES = 128


def attend_kernel(
    len_ref, queries_ref, cache_ref, latent_ref, held, scores, summed, arrived
):
    own_rows, _, heads = queries_ref.shape
    rank = latent_ref.shape[2]

    def block_copy(row, block):
        return pltpu.make_async_copy(
            cache_ref.at[row, :, pl.ds(pl.multiple_of(block * BLOCK, BLOCK), BLOCK)],
            held.at[row, block],
            arrived.at[row, block],
        )

    counts = [(len_ref[row] + BLOCK - 1) // BLOCK for row in range(own_rows)]
    for row in range(own_rows):

        def begin(block, _, row=row):
            block_copy(row, block).start()
            return 0

        lax.fori_loop(0, counts[row], begin, 0)
    for row in range(own_rows):
        length = len_ref[row]
        query = queries_ref[row].T
        column = lax.broadcasted_iota(jnp.int32, (heads, BLOCK), 1)

        def score(block, highest, row=row, length=length, query=query):
            block_copy(row, block).wait()
            found = jnp.dot(
                query, held[row, block], preferred_element_type=jnp.float32
            ) * QK ** (-0.5)
            found = jnp.where(column + block * BLOCK < length, found, -jnp.inf)
            scores[block] = found
            for at in range(0, BLOCK, LANES):
                highest = jnp.maximum(highest, found[:, at : at + LANES])
            return highest

        highest = lax.fori_loop(
            0, counts[row], score, jnp.full((heads, LANES), -jnp.inf, jnp.float32)
        )
        highest = jnp.max(highest, axis=1, keepdims=True)
        summed[...] = jnp.zeros_like(summed)

        def weigh(block, total, row=row, highest=highest):
            weight = jnp.exp(scores[block] - highest)
            summed[...] += lax.dot_general(
                weight.astype(jnp.bfloat16),
                held[row, block, :rank, :],
                (((1,), (1,)), ((), ())),
                preferred_element_type=jnp.float32,
            )
            for at in range(0, BLOCK, LANES):
                total = total + weight[:, at : at + LANES]
            return total

        total = lax.fori_loop(
            0, counts[row], weigh, jnp.zeros((heads, LANES), jnp.float32)
        )
        total = jnp.sum(total, axis=1, keepdims=True)
        latent_ref[row] = (summed[...] / total).astype(latent_ref.dtype)


def attend(queries, cache, cache_len, rank):
    own_rows, depth, heads = queries.shape
    blocks = cache.shape[2] // BLOCK
    return pl.pallas_call(
        attend_kernel,
        out_shape=jax.ShapeDtypeStruct((own_rows, heads, rank), jnp.bfloat16),
        in_specs=[
            pl.BlockSpec(memory_space=pltpu.SMEM),
            pl.BlockSpec(memory_space=pltpu.VMEM),
            pl.BlockSpec(memory_space=pl.ANY),
        ],
        out_specs=pl.BlockSpec(memory_space=pltpu.VMEM),
        scratch_shapes=[
            pltpu.VMEM((own_rows, blocks, depth, BLOCK), jnp.bfloat16),
            pltpu.VMEM((blocks, heads, BLOCK), jnp.float32),
            pltpu.VMEM((heads, rank), jnp.float32),
            pltpu.SemaphoreType.DMA((own_rows, blocks)),
        ],
        compiler_params=pltpu.CompilerParams(vmem_limit_bytes=32 * 2**20),
        cost_estimate=pl.CostEstimate(
            flops=2 * own_rows * heads * cache.shape[2] * (depth + rank),
            bytes_accessed=2 * cache.size,
            transcendentals=own_rows * heads * cache.shape[2],
        ),
        name="attend",
    )(cache_len, queries, cache)


def swap(array, distance):
    pairs = [(at, at ^ distance) for at in range(lax.axis_size("experts"))]
    return lax.ppermute(array, "experts", pairs)


def add(ours, theirs):
    return (ours.astype(jnp.float32) + theirs.astype(jnp.float32)).astype(jnp.bfloat16)


def shards(
    queries,
    cache,
    cache_len,
    residual_in,
    w_absorb,
    w_out,
    norm_gain,
    expert_ids,
    route_gates,
    w_gate,
    w_up,
    w_down,
):
    devices = lax.axis_size("experts")
    rank_here = lax.axis_index("experts")
    own_rows = queries.shape[0]
    all_rows = expert_ids.shape[0]
    half, quarter = all_rows // 2, all_rows // 4
    far = devices // 4
    split_ways = FF // w_gate.shape[1]

    latent = attend(queries, cache, cache_len, w_absorb.shape[1])
    by_head = lax.all_to_all(latent, "experts", split_axis=1, concat_axis=0, tiled=True)
    head_values = jnp.einsum(
        "rhc,hcv->rhv", by_head, w_absorb, preferred_element_type=jnp.float32
    ).astype(jnp.bfloat16)
    slot = jnp.arange(all_rows, dtype=jnp.int32) // own_rows
    distance = slot // (2 * far) + slot // far % 2 * 2 + slot % far * 4
    source = (rank_here ^ distance) * own_rows + jnp.arange(all_rows) % own_rows
    order = (source[:, None] == jnp.arange(all_rows)[None, :]).astype(jnp.bfloat16)
    relative = jnp.dot(
        order, head_values.reshape(all_rows, -1), preferred_element_type=jnp.float32
    ).astype(jnp.bfloat16)

    term = jnp.dot(relative, w_out, preferred_element_type=jnp.float32).astype(jnp.bfloat16)
    term = add(term[:half], swap(term[half:], 1))
    term = add(term[:quarter], swap(term[quarter:], 2))
    blocks = [term[at * own_rows : (at + 1) * own_rows] for at in range(far)]
    blocks = [blocks[0]] + [swap(blocks[at], 4 * at) for at in range(1, far)]
    attention = sum(block.astype(jnp.float32) for block in blocks)
    attended = (residual_in.astype(jnp.float32) + attention).astype(jnp.bfloat16)
    widened = attended.astype(jnp.float32)
    inverse = lax.rsqrt(jnp.mean(widened * widened, axis=-1, keepdims=True) + 1e-06)
    normed = (widened * inverse * norm_gain).astype(jnp.bfloat16)

    normed = jnp.concatenate([normed] + [swap(normed, 4 * at) for at in range(1, far)])
    normed = jnp.concatenate([normed, swap(normed, 2)])
    normed = jnp.concatenate([normed, swap(normed, 1)])
    gate_proj = jnp.dot(normed, w_gate, preferred_element_type=jnp.float32)
    up_proj = jnp.dot(normed, w_up, preferred_element_type=jnp.float32)
    activated = (jax.nn.silu(gate_proj) * up_proj).astype(jnp.bfloat16)
    term = jnp.dot(activated, w_down, preferred_element_type=jnp.float32).astype(jnp.bfloat16)

    term = add(term[:half], swap(term[half:], 1))
    own_ids = lax.dynamic_slice_in_dim(expert_ids, rank_here * own_rows, own_rows, 0)
    expert_out = 0.0
    for at in range(devices // 2):
        block = term[at * own_rows : (at + 1) * own_rows]
        distance = at // far * 2 + at % far * 4
        block = swap(block, distance) if distance else block
        expert = (rank_here ^ distance) // split_ways
        mixing = jnp.sum(
            route_gates * (own_ids == expert).astype(jnp.float32), axis=1, keepdims=True
        )
        expert_out = expert_out + mixing * block.astype(jnp.float32)
    return (attended, expert_out.astype(jnp.bfloat16))


def solution(mesh):
    placed = (
        P(("groups", "experts"), None, None),
        P(("groups", "experts"), None, None),
        P(("groups", "experts")),
        P(("groups", "experts"), None),
        P("experts", None, None),
        P("experts", None),
        P(),
        P("groups", None),
        P(("groups", "experts"), None),
        P(None, "experts"),
        P(None, "experts"),
        P("experts", None),
    )
    return jax.shard_map(
        shards,
        mesh=mesh,
        in_specs=placed,
        out_specs=(P(("groups", "experts"), None), P(("groups", "experts"), None)),
        check_vma=False,
    )
```

```python
import functools

import jax
import jax.numpy as jnp
from jax import lax
from jax.experimental import pallas as pl
from jax.experimental.pallas import tpu as pltpu
from jax.sharding import PartitionSpec as P

QK = 192
FF = 2048
BLOCK = 512
GROUP = 4
LANES = 128
TILE = 256
MIB = 2**20


def in_groups(count, step):
    whole = count // GROUP

    def body(at, _):
        step(at * GROUP, GROUP)
        return 0

    lax.fori_loop(0, whole, body, 0)
    pl.when((count & 2) != 0)(lambda: step(whole * GROUP, 2))
    pl.when((count & 1) != 0)(lambda: step(count - 1, 1))


def lane_tiles(array):
    return [array[:, at : at + LANES] for at in range(0, array.shape[1], LANES)]


def attend_kernel(
    info_ref,
    queries_ref,
    cache_ref,
    near_ref,
    across_ref,
    held,
    scores,
    highest,
    total,
    summed,
    staged,
    arrived,
):
    own_rows, heads, _ = queries_ref.shape
    devices, _, rank = staged.shape
    own_heads = heads // devices

    def block_copy(row, block):
        return pltpu.make_async_copy(
            cache_ref.at[row, :, pl.ds(pl.multiple_of(block * BLOCK, BLOCK), BLOCK)],
            held.at[row, block],
            arrived.at[row, block],
        )

    counts = [(info_ref[row] + BLOCK - 1) // BLOCK for row in range(own_rows)]
    for row in range(own_rows):

        def begin(block, _, row=row):
            block_copy(row, block).start()
            return 0

        lax.fori_loop(0, counts[row], begin, 0)
    column = lax.broadcasted_iota(jnp.int32, (heads, BLOCK), 1)
    for row in range(own_rows):
        length = info_ref[row]
        query = queries_ref[row]
        highest[...] = jnp.full_like(highest, -jnp.inf)
        total[...] = jnp.zeros_like(total)
        summed[...] = jnp.zeros_like(summed)

        def score(first, many, row=row, length=length, query=query):
            for block in [first + at for at in range(many)]:
                block_copy(row, block).wait()
            tops = []
            for block in [first + at for at in range(many)]:
                found = jnp.dot(
                    query, held[row, block], preferred_element_type=jnp.float32
                ) * QK ** (-0.5)
                found = jnp.where(column + block * BLOCK < length, found, -jnp.inf)
                scores[block] = found
                tops.append(functools.reduce(jnp.maximum, lane_tiles(found)))
            highest[...] = functools.reduce(jnp.maximum, tops, highest[...])

        in_groups(counts[row], score)
        top = jnp.max(highest[...], axis=1, keepdims=True)

        def lift(first, many, top=top):
            sums = []
            for block in [first + at for at in range(many)]:
                weight = jnp.exp(scores[block] - top)
                scores[block] = weight
                sums.append(sum(lane_tiles(weight)))
            total[...] += sum(sums)

        in_groups(counts[row], lift)
        inverse = 1.0 / jnp.sum(total[...], axis=1, keepdims=True)

        def gather(first, many, row=row, inverse=inverse):
            terms = []
            for block in [first + at for at in range(many)]:
                weight = (scores[block] * inverse).astype(jnp.bfloat16)
                terms.append(
                    lax.dot_general(
                        weight,
                        held[row, block, :rank, :],
                        (((1,), (1,)), ((), ())),
                        preferred_element_type=jnp.float32,
                    )
                )
            summed[...] += sum(terms)

        in_groups(counts[row], gather)
        latent = summed[...]
        for device in range(devices):
            staged[device, row * own_heads : (row + 1) * own_heads, :] = latent[
                device * own_heads : (device + 1) * own_heads
            ]
    here = info_ref[own_rows]
    for at in range(devices // 2):
        near_ref[at] = staged[here ^ (2 * at)].astype(near_ref.dtype)
        across_ref[at] = staged[here ^ (2 * at + 1)].astype(across_ref.dtype)


def attend(queries, cache, cache_len, rank_here, devices, rank):
    own_rows, depth, heads = queries.shape
    blocks = cache.shape[2] // BLOCK
    packed = own_rows * heads // devices
    info = jnp.concatenate([cache_len, rank_here.astype(jnp.int32)[None]])
    part = jax.ShapeDtypeStruct((devices // 2, packed, rank), jnp.bfloat16)
    return pl.pallas_call(
        attend_kernel,
        out_shape=(part, part),
        in_specs=[
            pl.BlockSpec(memory_space=pltpu.SMEM),
            pl.BlockSpec(memory_space=pltpu.VMEM),
            pl.BlockSpec(memory_space=pl.ANY),
        ],
        out_specs=(pl.BlockSpec(memory_space=pltpu.VMEM),) * 2,
        scratch_shapes=[
            pltpu.VMEM((own_rows, blocks, depth, BLOCK), jnp.bfloat16),
            pltpu.VMEM((blocks, heads, BLOCK), jnp.float32),
            pltpu.VMEM((heads, LANES), jnp.float32),
            pltpu.VMEM((heads, LANES), jnp.float32),
            pltpu.VMEM((heads, rank), jnp.float32),
            pltpu.VMEM((devices, packed, rank), jnp.float32),
            pltpu.SemaphoreType.DMA((own_rows, blocks)),
        ],
        compiler_params=pltpu.CompilerParams(vmem_limit_bytes=48 * MIB),
        cost_estimate=pl.CostEstimate(
            flops=own_rows * heads * cache.shape[2] * (depth + rank),
            bytes_accessed=cache.size,
            transcendentals=own_rows * heads * cache.shape[2],
        ),
        name="attend",
    )(info, jnp.swapaxes(queries, 1, 2), cache)


def column_copies(source, target, semaphores, parts):
    width = source.shape[1] // parts
    return [
        pltpu.make_async_copy(
            source.at[:, at * width : (at + 1) * width],
            target.at[:, at * width : (at + 1) * width],
            semaphores.at[at],
        )
        for at in range(parts)
    ]


def row_copies(source, target, semaphores, parts):
    depth = source.shape[0] // parts
    return [
        pltpu.make_async_copy(
            source.at[at * depth : (at + 1) * depth, :],
            target.at[at * depth : (at + 1) * depth, :],
            semaphores.at[at],
        )
        for at in range(parts)
    ]


PARTS = 4


def project_kernel(own_rows, far, *refs):
    *pieces, absorb_ref, w_ref, keep_ref, send_ref, joined, held, arrived = refs
    copies = column_copies(w_ref, held, arrived, PARTS)
    for copy in copies:
        copy.start()
    packed = 2 * pieces[0].shape[0]
    joined[0 : packed // 2, :] = pieces[0][...]
    joined[packed // 2 : packed, :] = pieces[1][...]
    for at, piece in enumerate(pieces[2:], 1):
        joined[at * packed : (at + 1) * packed, :] = piece[...]
    own_heads = absorb_ref.shape[0]
    half, width = keep_ref.shape
    rows = 2 * half
    shape = (rows, joined.shape[0])
    row = lax.broadcasted_iota(jnp.int32, shape, 0)
    place = lax.broadcasted_iota(jnp.int32, shape, 1)
    turn = own_rows.bit_length() - 1
    far_bits = far.bit_length() - 1
    request, slot = row & (own_rows - 1), row >> turn
    far_at, slot = slot & (far - 1), slot >> far_bits
    source = (far_at << 3) + ((slot & 1) << 2) + ((slot >> 1 & 1) << 1) + (slot >> 2)
    values = []
    for head in range(own_heads):
        wanted = ((source << turn) + request) * own_heads + head
        choice = (place == wanted).astype(jnp.float32).astype(jnp.bfloat16)
        latent = jnp.dot(choice, joined[...], preferred_element_type=jnp.float32)
        value = jnp.dot(
            latent.astype(jnp.bfloat16), absorb_ref[head], preferred_element_type=jnp.float32
        )
        values.append(value.astype(jnp.bfloat16))
    values = jnp.concatenate(values, axis=1)
    for part in range(PARTS):
        copies[part].wait()
        for at in range(part * width // PARTS, (part + 1) * width // PARTS, TILE):
            term = jnp.dot(values, held[:, at : at + TILE], preferred_element_type=jnp.float32)
            keep_ref[:, at : at + TILE] = term[:half]
            send_ref[:, at : at + TILE] = term[half:].astype(send_ref.dtype)


def project(pieces, w_absorb, w_out, own_rows, rows, far):
    depth, width = w_out.shape
    rank = w_absorb.shape[1]
    joined = sum(piece.shape[0] for piece in pieces)
    return pl.pallas_call(
        functools.partial(project_kernel, own_rows, far),
        out_shape=(
            jax.ShapeDtypeStruct((rows // 2, width), jnp.float32),
            jax.ShapeDtypeStruct((rows // 2, width), jnp.bfloat16),
        ),
        in_specs=[pl.BlockSpec(memory_space=pltpu.VMEM)] * (len(pieces) + 1)
        + [pl.BlockSpec(memory_space=pl.ANY)],
        out_specs=(pl.BlockSpec(memory_space=pltpu.VMEM),) * 2,
        scratch_shapes=[
            pltpu.VMEM((joined, rank), jnp.bfloat16),
            pltpu.VMEM((depth, width), jnp.bfloat16),
            pltpu.SemaphoreType.DMA((PARTS,)),
        ],
        compiler_params=pltpu.CompilerParams(vmem_limit_bytes=24 * MIB),
        cost_estimate=pl.CostEstimate(
            flops=2 * rows * depth * width, bytes_accessed=2 * depth * width, transcendentals=0
        ),
        name="project",
    )(*pieces, w_absorb, w_out)


def expert_kernel(
    far_rows,
    first_own,
    first_other,
    second_own,
    second_other,
    gate_ref,
    up_ref,
    down_ref,
    keep_ref,
    send_ref,
    gate_held,
    up_held,
    down_held,
    gate_arrived,
    up_arrived,
    down_arrived,
):
    gate_copies = row_copies(gate_ref, gate_held, gate_arrived, PARTS)
    up_copies = row_copies(up_ref, up_held, up_arrived, PARTS)
    down_copies = column_copies(down_ref, down_held, down_arrived, PARTS)
    for part in range(PARTS):
        gate_copies[part].start()
        up_copies[part].start()
    for part in range(PARTS):
        down_copies[part].start()
    half, width = keep_ref.shape
    depth = width // PARTS
    side = width // 2

    def arrange(array):
        eighths = [array[at * far_rows : (at + 1) * far_rows] for at in range(8)]
        return jnp.concatenate([eighths[at] for at in (0, 2, 1, 3, 4, 6, 5, 7)], axis=0)

    gates, ups = [], []
    for part in range(PARTS):
        own, other = (
            (first_own, first_other) if part < PARTS // 2 else (second_own, second_other)
        )
        at = part * depth % side
        tokens = jnp.concatenate(
            [own[:, at : at + depth], other[:, at : at + depth]], axis=0
        )
        span = slice(part * depth, (part + 1) * depth)
        gate_copies[part].wait()
        gates.append(jnp.dot(tokens, gate_held[span, :], preferred_element_type=jnp.float32))
        up_copies[part].wait()
        ups.append(jnp.dot(tokens, up_held[span, :], preferred_element_type=jnp.float32))
    middle = PARTS // 2
    gate = sum(gates[:middle]) + arrange(sum(gates[middle:]))
    up = sum(ups[:middle]) + arrange(sum(ups[middle:]))
    active = (gate / (1.0 + jnp.exp(-gate)) * up).astype(jnp.bfloat16)
    for part in range(PARTS):
        down_copies[part].wait()
        for at in range(part * depth, (part + 1) * depth, TILE):
            term = jnp.dot(
                active, down_held[:, at : at + TILE], preferred_element_type=jnp.float32
            )
            keep_ref[:, at : at + TILE] = term[:half]
            send_ref[:, at : at + TILE] = term[half:].astype(send_ref.dtype)


def run_expert(tokens, w_gate, w_up, w_down, far_rows):
    half, side = tokens[0].shape
    width, hidden = w_gate.shape
    return pl.pallas_call(
        functools.partial(expert_kernel, far_rows),
        out_shape=(
            jax.ShapeDtypeStruct((half, width), jnp.float32),
            jax.ShapeDtypeStruct((half, width), jnp.bfloat16),
        ),
        in_specs=[pl.BlockSpec(memory_space=pltpu.VMEM)] * 4
        + [pl.BlockSpec(memory_space=pl.ANY)] * 3,
        out_specs=(pl.BlockSpec(memory_space=pltpu.VMEM),) * 2,
        scratch_shapes=[
            pltpu.VMEM((width, hidden), jnp.bfloat16),
            pltpu.VMEM((width, hidden), jnp.bfloat16),
            pltpu.VMEM((hidden, width), jnp.bfloat16),
            pltpu.SemaphoreType.DMA((PARTS,)),
            pltpu.SemaphoreType.DMA((PARTS,)),
            pltpu.SemaphoreType.DMA((PARTS,)),
        ],
        compiler_params=pltpu.CompilerParams(vmem_limit_bytes=24 * MIB),
        cost_estimate=pl.CostEstimate(
            flops=12 * half * hidden * width,
            bytes_accessed=6 * hidden * width,
            transcendentals=2 * half * hidden,
        ),
        name="expert",
    )(*tokens, w_gate, w_up, w_down)


def swap(array, distance):
    pairs = [(at, at ^ distance) for at in range(lax.axis_size("experts"))]
    return lax.ppermute(array, "experts", pairs)


def join(ours, theirs, distance):
    return ours + swap(theirs.astype(jnp.bfloat16), distance).astype(jnp.float32)


def halve(keep, send, far):
    half, width = keep.shape
    whole = join(keep, send, 1)
    first, second = whole[:, : width // 2], whole[:, width // 2 :]
    second = second.reshape(2, 2, half // 4, width // 2)
    first = join(first[: half // 2], first[half // 2 :], 2)
    second = join(second[:, 0], second[:, 1], 4)
    first = join(first[: half // 4], first[half // 4 :], 4)
    second = join(second[0], second[1], 2)
    own_rows = half // 4 // far
    found = []
    for at in range(far):
        span = slice(at * own_rows, (at + 1) * own_rows)
        if at == 0:
            found.append((first[span], second[span]))
        else:
            found.append(
                tuple(
                    swap(side[span].astype(jnp.bfloat16), 8 * at).astype(jnp.float32)
                    for side in (first, second)
                )
            )
    return found


def shards(
    queries,
    cache,
    cache_len,
    residual_in,
    w_absorb,
    w_out,
    norm_gain,
    expert_ids,
    route_gates,
    w_gate,
    w_up,
    w_down,
):
    devices = lax.axis_size("experts")
    rank_here = lax.axis_index("experts")
    own_rows = queries.shape[0]
    all_rows = expert_ids.shape[0]
    width = residual_in.shape[1]
    far = devices // 8
    split_ways = FF // w_gate.shape[1]
    assert split_ways == 8

    near, across = attend(
        queries, cache, cache_len, rank_here, devices, w_absorb.shape[1]
    )
    other = swap(across, 1)
    pieces = [near[0], other[0]]
    for at in range(1, devices // 2):
        pieces.append(swap(jnp.concatenate([near[at], other[at]]), 2 * at))
    keep, send = project(pieces, w_absorb, w_out, own_rows, all_rows, far)

    found = halve(keep, send, far)
    residual = residual_in.astype(jnp.float32)
    attended = jnp.concatenate(
        [
            residual[:, : width // 2] + sum(one[0] for one in found),
            residual[:, width // 2 :] + sum(one[1] for one in found),
        ],
        axis=1,
    ).astype(jnp.bfloat16)
    widened = attended.astype(jnp.float32)
    inverse = lax.rsqrt(jnp.mean(widened * widened, axis=-1, keepdims=True) + 1e-06)
    normed = (widened * inverse * norm_gain).astype(jnp.bfloat16)

    normed = jnp.concatenate([normed] + [swap(normed, 8 * at) for at in range(1, far)])
    first, second = normed[:, : width // 2], normed[:, width // 2 :]
    first = jnp.concatenate([first, swap(first, 4)])
    second = jnp.concatenate([second, swap(second, 2)])
    first = jnp.concatenate([first, swap(first, 2)])
    second = jnp.concatenate([second, swap(second, 4)])
    tokens = (first, swap(first, 1), second, swap(second, 1))
    keep, send = run_expert(tokens, w_gate, w_up, w_down, far * own_rows)

    found = halve(keep, send, far)
    own_ids = lax.dynamic_slice_in_dim(expert_ids, rank_here * own_rows, own_rows, 0)
    sides = [0.0, 0.0]
    for at, one in enumerate(found):
        expert = (rank_here ^ (8 * at)) // split_ways
        mixing = jnp.sum(
            route_gates * (own_ids == expert).astype(jnp.float32), axis=1, keepdims=True
        )
        sides = [side + mixing * block for side, block in zip(sides, one)]
    expert_out = jnp.concatenate(sides, axis=1)
    return (attended, expert_out.astype(jnp.bfloat16))


def solution(mesh):
    placed = (
        P(("groups", "experts"), None, None),
        P(("groups", "experts"), None, None),
        P(("groups", "experts")),
        P(("groups", "experts"), None),
        P("experts", None, None),
        P("experts", None),
        P(),
        P("groups", None),
        P(("groups", "experts"), None),
        P(None, "experts"),
        P(None, "experts"),
        P("experts", None),
    )
    return jax.shard_map(
        shards,
        mesh=mesh,
        in_specs=placed,
        out_specs=(P(("groups", "experts"), None), P(("groups", "experts"), None)),
        check_vma=False,
    )
```

```python
import functools

import jax
import jax.numpy as jnp
from jax import lax
from jax.experimental import pallas as pl
from jax.experimental.pallas import tpu as pltpu
from jax.sharding import PartitionSpec as P

QK = 192
FF = 2048
BLOCK = 512
GROUP = 4
LANES = 128
TILE = 256
MIB = 2**20


def lane_tiles(array):
    return [array[:, at : at + LANES] for at in range(0, array.shape[1], LANES)]


def attend_kernel(
    len_ref,
    queries_ref,
    cache_ref,
    latent_ref,
    length,
    queries,
    held,
    scores,
    highest,
    sums,
    inverse,
    summed,
    staged,
    item_row,
    item_block,
    length_arrived,
    queries_arrived,
    arrived,
):
    own_rows, heads, _ = queries.shape
    devices, _, rank = staged.shape
    own_heads = heads // devices
    blocks = held.shape[1]

    length_copy = pltpu.make_async_copy(len_ref, length, length_arrived)
    length_copy.start()
    queries_copy = pltpu.make_async_copy(queries_ref, queries, queries_arrived)
    queries_copy.start()

    def block_copy(row, block):
        return pltpu.make_async_copy(
            cache_ref.at[row, :, pl.ds(pl.multiple_of(block * BLOCK, BLOCK), BLOCK)],
            held.at[row, block],
            arrived.at[row, block],
        )

    length_copy.wait()
    items = 0
    for row in range(own_rows):
        count = (length[row] + BLOCK - 1) // BLOCK

        def begin(block, first, row=row):
            block_copy(row, block).start()
            item_row[first + block] = row
            item_block[first + block] = block
            return first

        lax.fori_loop(0, count, begin, items)
        items = items + count
    for at in range(GROUP - 1):
        item_row[items + at] = own_rows - 1
        item_block[items + at] = item_block[items - 1]
    groups = (items + GROUP - 1) // GROUP

    def members(group):
        return [
            (group * GROUP + at, item_row[group * GROUP + at], item_block[group * GROUP + at])
            for at in range(GROUP)
        ]

    highest[...] = jnp.full_like(highest, -jnp.inf)
    sums[...] = jnp.zeros_like(sums)
    summed[...] = jnp.zeros_like(summed)
    queries_copy.wait()
    column = lax.broadcasted_iota(jnp.int32, (heads, BLOCK), 1)

    def score(group, _):
        inside = members(group)
        for at, row, block in inside:
            pl.when(at < items)(lambda row=row, block=block: block_copy(row, block).wait())
        for at, row, block in inside:
            found = jnp.dot(
                queries[row], held[row, block], preferred_element_type=jnp.float32
            ) * QK ** (-0.5)
            found = jnp.where(column + block * BLOCK < length[row], found, -jnp.inf)
            scores[row, block] = found
            highest[row, block] = functools.reduce(jnp.maximum, lane_tiles(found))
        return 0

    lax.fori_loop(0, groups, score, 0)
    tops = [jnp.max(highest[row], axis=0) for row in range(own_rows)]
    for row in range(own_rows):
        top = jnp.max(tops[row], axis=1, keepdims=True)
        highest[row, 0] = jnp.broadcast_to(top, (heads, LANES))

    def lift(group, _):
        for at, row, block in members(group):
            top = highest[row, 0][:, :1]
            pl.when(at < items)(lambda row=row, block=block, top=top: lift_one(row, block, top))
        return 0

    def lift_one(row, block, top):
        weight = jnp.exp(scores[row, block] - top)
        scores[row, block] = weight
        sums[row, block] = sum(lane_tiles(weight))

    lax.fori_loop(0, groups, lift, 0)
    for row in range(own_rows):
        total = jnp.sum(jnp.sum(sums[row], axis=0), axis=1, keepdims=True)
        inverse[row] = jnp.broadcast_to(1.0 / total, (heads, LANES))

    def gather(group, _):
        terms = []
        for at, row, block in members(group):
            live = jnp.where(at < items, 1.0, 0.0)
            weight = scores[row, block] * (inverse[row][:, :1] * live)
            terms.append(
                lax.dot_general(
                    weight.astype(jnp.bfloat16),
                    held[row, block, :rank, :],
                    (((1,), (1,)), ((), ())),
                    preferred_element_type=jnp.float32,
                )
            )
        for (at, row, block), term in zip(members(group), terms):
            summed[row] += term
        return 0

    lax.fori_loop(0, groups, gather, 0)
    for row in range(own_rows):
        latent = summed[row]
        for device in range(devices):
            staged[device, row * own_heads : (row + 1) * own_heads, :] = latent[
                device * own_heads : (device + 1) * own_heads
            ]
    latent_ref[...] = staged[...].astype(latent_ref.dtype)


def attend(queries, cache, cache_len, devices, rank):
    own_rows, depth, heads = queries.shape
    blocks = cache.shape[2] // BLOCK
    packed = own_rows * heads // devices
    listed = own_rows * blocks + GROUP
    return pl.pallas_call(
        attend_kernel,
        out_shape=jax.ShapeDtypeStruct((devices, packed, rank), jnp.bfloat16),
        in_specs=[pl.BlockSpec(memory_space=pltpu.HBM)] * 3,
        out_specs=pl.BlockSpec(memory_space=pltpu.VMEM),
        scratch_shapes=[
            pltpu.SMEM((own_rows,), jnp.int32),
            pltpu.VMEM((own_rows, heads, depth), jnp.bfloat16),
            pltpu.VMEM((own_rows, blocks, depth, BLOCK), jnp.bfloat16),
            pltpu.VMEM((own_rows, blocks, heads, BLOCK), jnp.float32),
            pltpu.VMEM((own_rows, blocks, heads, LANES), jnp.float32),
            pltpu.VMEM((own_rows, blocks, heads, LANES), jnp.float32),
            pltpu.VMEM((own_rows, heads, LANES), jnp.float32),
            pltpu.VMEM((own_rows, heads, rank), jnp.float32),
            pltpu.VMEM((devices, packed, rank), jnp.float32),
            pltpu.SMEM((listed,), jnp.int32),
            pltpu.SMEM((listed,), jnp.int32),
            pltpu.SemaphoreType.DMA,
            pltpu.SemaphoreType.DMA,
            pltpu.SemaphoreType.DMA((own_rows, blocks)),
        ],
        compiler_params=pltpu.CompilerParams(vmem_limit_bytes=55 * MIB),
        cost_estimate=pl.CostEstimate(
            flops=own_rows * heads * cache.shape[2] * (depth + rank),
            bytes_accessed=cache.size,
            transcendentals=own_rows * heads * cache.shape[2],
        ),
        name="attend",
    )(cache_len, jnp.swapaxes(queries, 1, 2), cache)


def project_kernel(own_rows, far, here_ref, joined_ref, absorb_ref, w_ref, keep_ref, send_ref):
    own_heads = absorb_ref.shape[0]
    half, width = keep_ref.shape
    shape = (2 * half, joined_ref.shape[0])
    row = lax.broadcasted_iota(jnp.int32, shape, 0)
    place = lax.broadcasted_iota(jnp.int32, shape, 1)
    turn = own_rows.bit_length() - 1
    far_bits = far.bit_length() - 1
    request, slot = row & (own_rows - 1), row >> turn
    far_at, slot = slot & (far - 1), slot >> far_bits
    distance = (far_at << 3) + ((slot & 1) << 2) + ((slot >> 1 & 1) << 1) + (slot >> 2)
    device = distance ^ here_ref[0]
    values = []
    for head in range(own_heads):
        wanted = ((device << turn) + request) * own_heads + head
        choice = (place == wanted).astype(jnp.float32).astype(jnp.bfloat16)
        latent = jnp.dot(choice, joined_ref[...], preferred_element_type=jnp.float32)
        value = jnp.dot(
            latent.astype(jnp.bfloat16), absorb_ref[head], preferred_element_type=jnp.float32
        )
        values.append(value.astype(jnp.bfloat16))
    values = jnp.concatenate(values, axis=1)
    for at in range(0, width, TILE):
        term = jnp.dot(values, w_ref[:, at : at + TILE], preferred_element_type=jnp.float32)
        keep_ref[:, at : at + TILE] = term[:half]
        send_ref[:, at : at + TILE] = term[half:].astype(send_ref.dtype)


def project(here, joined, w_absorb, w_out, own_rows, rows, far):
    depth, width = w_out.shape
    return pl.pallas_call(
        functools.partial(project_kernel, own_rows, far),
        out_shape=(
            jax.ShapeDtypeStruct((rows // 2, width), jnp.float32),
            jax.ShapeDtypeStruct((rows // 2, width), jnp.bfloat16),
        ),
        in_specs=[pl.BlockSpec(memory_space=pltpu.SMEM)]
        + [pl.BlockSpec(memory_space=pltpu.VMEM)] * 3,
        out_specs=(pl.BlockSpec(memory_space=pltpu.VMEM),) * 2,
        compiler_params=pltpu.CompilerParams(vmem_limit_bytes=24 * MIB),
        cost_estimate=pl.CostEstimate(
            flops=2 * rows * depth * width, bytes_accessed=2 * depth * width, transcendentals=0
        ),
        name="project",
    )(here, joined, w_absorb, w_out)


def expert_kernel(own_ref, other_ref, gate_ref, up_ref, down_ref, keep_ref, send_ref):
    half, width = keep_ref.shape
    depth = width // 4
    gate, up = 0.0, 0.0
    for at in range(0, width, depth):
        tokens = jnp.concatenate(
            [own_ref[:, at : at + depth], other_ref[:, at : at + depth]], axis=0
        )
        gate = gate + jnp.dot(
            tokens, gate_ref[at : at + depth, :], preferred_element_type=jnp.float32
        )
        up = up + jnp.dot(
            tokens, up_ref[at : at + depth, :], preferred_element_type=jnp.float32
        )
    active = (gate / (1.0 + jnp.exp(-gate)) * up).astype(jnp.bfloat16)
    for at in range(0, width, TILE):
        term = jnp.dot(active, down_ref[:, at : at + TILE], preferred_element_type=jnp.float32)
        keep_ref[:, at : at + TILE] = term[:half]
        send_ref[:, at : at + TILE] = term[half:].astype(send_ref.dtype)


def run_expert(own, other, w_gate, w_up, w_down):
    half, width = own.shape
    hidden = w_gate.shape[1]
    return pl.pallas_call(
        expert_kernel,
        out_shape=(
            jax.ShapeDtypeStruct((half, width), jnp.float32),
            jax.ShapeDtypeStruct((half, width), jnp.bfloat16),
        ),
        in_specs=[pl.BlockSpec(memory_space=pltpu.VMEM)] * 5,
        out_specs=(pl.BlockSpec(memory_space=pltpu.VMEM),) * 2,
        compiler_params=pltpu.CompilerParams(vmem_limit_bytes=24 * MIB),
        cost_estimate=pl.CostEstimate(
            flops=12 * half * hidden * width,
            bytes_accessed=6 * hidden * width,
            transcendentals=2 * half * hidden,
        ),
        name="expert",
    )(own, other, w_gate, w_up, w_down)


def swap(array, distance):
    pairs = [(at, at ^ distance) for at in range(lax.axis_size("experts"))]
    return lax.ppermute(array, "experts", pairs)


def wide(array):
    return array.astype(jnp.float32)


def collect(keep, send):
    half = keep.shape[0]
    step = half // 4
    whole = keep + wide(swap(send, 1))
    parts = [whole[at : at + step] for at in range(0, half, step)]
    total = parts[0]
    for part, distance in ((3, 6), (1, 4), (2, 2)):
        total = total + wide(swap(parts[part].astype(jnp.bfloat16), distance))
    return total


def shards(
    queries,
    cache,
    cache_len,
    residual_in,
    w_absorb,
    w_out,
    norm_gain,
    expert_ids,
    route_gates,
    w_gate,
    w_up,
    w_down,
):
    devices = lax.axis_size("experts")
    rank_here = lax.axis_index("experts")
    own_rows = queries.shape[0]
    all_rows = expert_ids.shape[0]
    far = devices // 8
    split_ways = FF // w_gate.shape[1]
    assert split_ways == 8

    latent = attend(queries, cache, cache_len, devices, w_absorb.shape[1])
    joined = lax.all_to_all(latent, "experts", split_axis=0, concat_axis=0, tiled=True)
    joined = joined.reshape(-1, joined.shape[-1])
    here = rank_here.astype(jnp.int32)[None]
    keep, send = project(here, joined, w_absorb, w_out, own_rows, all_rows, far)

    total = collect(keep, send)
    total = jnp.concatenate([total[:own_rows] + wide(residual_in), total[own_rows:]])
    sent = total.astype(jnp.bfloat16)
    for at in range(1, far):
        block = swap(sent, 8 * at)
        total = total + wide(
            jnp.concatenate(
                [block[(to ^ at) * own_rows : ((to ^ at) + 1) * own_rows] for to in range(far)]
            )
        )
    stream = total.astype(jnp.bfloat16)
    attended = stream[:own_rows]
    widened = wide(stream)
    inverse = lax.rsqrt(jnp.mean(widened * widened, axis=-1, keepdims=True) + 1e-06)
    normed = (widened * inverse * norm_gain).astype(jnp.bfloat16)

    other = {distance: swap(normed, distance) for distance in (6, 4, 2)}
    own = jnp.concatenate([normed, other[4], other[2], other[6]])
    keep, send = run_expert(own, swap(own, 1), w_gate, w_up, w_down)

    total = collect(keep, send)
    own_ids = lax.dynamic_slice_in_dim(expert_ids, rank_here * own_rows, own_rows, 0)
    expert_out = 0.0
    for at in range(far):
        block = total[at * own_rows : (at + 1) * own_rows]
        block = wide(swap(block.astype(jnp.bfloat16), 8 * at)) if at else block
        expert = (rank_here ^ (8 * at)) // split_ways
        mixing = jnp.sum(
            route_gates * (own_ids == expert).astype(jnp.float32), axis=1, keepdims=True
        )
        expert_out = expert_out + mixing * block
    return (attended, expert_out.astype(jnp.bfloat16))


def solution(mesh):
    placed = (
        P(("groups", "experts"), None, None),
        P(("groups", "experts"), None, None),
        P(("groups", "experts")),
        P(("groups", "experts"), None),
        P("experts", None, None),
        P("experts", None),
        P(),
        P("groups", None),
        P(("groups", "experts"), None),
        P(None, "experts"),
        P(None, "experts"),
        P("experts", None),
    )
    return jax.shard_map(
        shards,
        mesh=mesh,
        in_specs=placed,
        out_specs=(P(("groups", "experts"), None), P(("groups", "experts"), None)),
        check_vma=False,
    )
```

```python
import functools

import jax
import jax.numpy as jnp
from jax import lax
from jax.experimental import pallas as pl
from jax.experimental.pallas import tpu as pltpu
from jax.sharding import PartitionSpec as P

QK = 192
FF = 2048
BLOCK = 512
GROUP = 4
LANES = 128
TILE = 256
PARTS = 4
MIB = 2**20


def lane_tiles(array):
    return [array[:, at : at + LANES] for at in range(0, array.shape[1], LANES)]


def attend_kernel(
    len_ref,
    queries_ref,
    cache_ref,
    latent_ref,
    length,
    queries,
    held,
    products,
    highest,
    sums,
    factors,
    staged,
    item_row,
    item_block,
    length_arrived,
    queries_arrived,
    arrived,
):
    own_rows, heads, _ = queries.shape
    devices, _, rank = staged.shape
    own_heads = heads // devices
    blocks = held.shape[1]

    length_copy = pltpu.make_async_copy(len_ref, length, length_arrived)
    length_copy.start()
    queries_copy = pltpu.make_async_copy(queries_ref, queries, queries_arrived)
    queries_copy.start()

    def block_copy(row, block):
        return pltpu.make_async_copy(
            cache_ref.at[row, :, pl.ds(pl.multiple_of(block * BLOCK, BLOCK), BLOCK)],
            held.at[row, block],
            arrived.at[row, block],
        )

    highest[...] = jnp.full_like(highest, -jnp.inf)
    sums[...] = jnp.zeros_like(sums)
    length_copy.wait()
    items = 0
    counts = []
    for row in range(own_rows):
        count = (length[row] + BLOCK - 1) // BLOCK

        def begin(block, first, row=row):
            block_copy(row, block).start()
            item_row[first + block] = row
            item_block[first + block] = block
            return first

        lax.fori_loop(0, count, begin, items)
        counts.append(count)
        items = items + count
    for at in range(GROUP - 1):
        item_row[items + at] = own_rows - 1
        item_block[items + at] = item_block[items - 1]
    groups = (items + GROUP - 1) // GROUP
    queries_copy.wait()
    column = lax.broadcasted_iota(jnp.int32, (heads, BLOCK), 1)

    def visit(group, _):
        inside = [
            (group * GROUP + at, item_row[group * GROUP + at], item_block[group * GROUP + at])
            for at in range(GROUP)
        ]
        for at, row, block in inside:
            pl.when(at < items)(lambda row=row, block=block: block_copy(row, block).wait())
        found = []
        for _, row, block in inside:
            score = jnp.dot(
                queries[row], held[row, block], preferred_element_type=jnp.float32
            ) * QK ** (-0.5)
            found.append(
                jnp.where(column + block * BLOCK < length[row], score, -jnp.inf)
            )
        tops = [
            jnp.max(functools.reduce(jnp.maximum, lane_tiles(score)), axis=1, keepdims=True)
            for score in found
        ]
        weights = [jnp.exp(score - top) for score, top in zip(found, tops)]
        for (_, row, block), top, weight in zip(inside, tops, weights):
            highest[row, block] = jnp.broadcast_to(top, (heads, LANES))
            sums[row, block] = sum(lane_tiles(weight))
            products[row, block] = lax.dot_general(
                weight.astype(jnp.bfloat16),
                held[row, block, :rank, :],
                (((1,), (1,)), ((), ())),
                preferred_element_type=jnp.float32,
            )
        return 0

    lax.fori_loop(0, groups, visit, 0)
    for row in range(own_rows):
        factor = jnp.exp(highest[row] - jnp.max(highest[row], axis=0, keepdims=True))
        total = jnp.sum(jnp.sum(sums[row] * factor, axis=0), axis=1, keepdims=True)
        factors[row] = factor * (1.0 / total)[None]
    for row in range(own_rows):

        def merge(block, latent, row=row):
            return latent + products[row, block] * factors[row, block][:, :1]

        latent = lax.fori_loop(
            0, counts[row], merge, jnp.zeros((heads, rank), jnp.float32)
        )
        for device in range(devices):
            staged[device, row * own_heads : (row + 1) * own_heads, :] = latent[
                device * own_heads : (device + 1) * own_heads
            ]
    latent_ref[...] = staged[...].astype(latent_ref.dtype)


def attend(queries, cache, cache_len, devices, rank):
    own_rows, depth, heads = queries.shape
    blocks = cache.shape[2] // BLOCK
    packed = own_rows * heads // devices
    listed = own_rows * blocks + GROUP
    return pl.pallas_call(
        attend_kernel,
        out_shape=jax.ShapeDtypeStruct((devices, packed, rank), jnp.bfloat16),
        in_specs=[pl.BlockSpec(memory_space=pl.ANY)] * 3,
        out_specs=pl.BlockSpec(memory_space=pltpu.VMEM),
        scratch_shapes=[
            pltpu.SMEM((own_rows,), jnp.int32),
            pltpu.VMEM((own_rows, heads, depth), jnp.bfloat16),
            pltpu.VMEM((own_rows, blocks, depth, BLOCK), jnp.bfloat16),
            pltpu.VMEM((own_rows, blocks, heads, rank), jnp.float32),
            pltpu.VMEM((own_rows, blocks, heads, LANES), jnp.float32),
            pltpu.VMEM((own_rows, blocks, heads, LANES), jnp.float32),
            pltpu.VMEM((own_rows, blocks, heads, LANES), jnp.float32),
            pltpu.VMEM((devices, packed, rank), jnp.float32),
            pltpu.SMEM((listed,), jnp.int32),
            pltpu.SMEM((listed,), jnp.int32),
            pltpu.SemaphoreType.DMA,
            pltpu.SemaphoreType.DMA,
            pltpu.SemaphoreType.DMA((own_rows, blocks)),
        ],
        compiler_params=pltpu.CompilerParams(vmem_limit_bytes=58 * MIB),
        cost_estimate=pl.CostEstimate(
            flops=own_rows * heads * cache.shape[2] * (depth + rank),
            bytes_accessed=cache.size,
            transcendentals=own_rows * heads * cache.shape[2],
        ),
        name="attend",
    )(cache_len, jnp.swapaxes(queries, 1, 2), cache)


def store_sides(term, at, keeps, sends):
    half, side = keeps[0].shape
    keep, send, at = keeps[at // side], sends[at // side], at % side
    keep[:, at : at + TILE] = term[:half]
    send[:, at : at + TILE] = term[half:].astype(send.dtype)


def side_shapes(half, width):
    return tuple(
        jax.ShapeDtypeStruct((half, width // 2), kind)
        for kind in (jnp.float32, jnp.bfloat16)
        for _ in range(2)
    )


def project_kernel(
    own_rows,
    far,
    here_ref,
    joined_ref,
    absorb_ref,
    residual_ref,
    w_ref,
    first_keep,
    second_keep,
    first_send,
    second_send,
    held,
    arrived,
):
    own_heads = absorb_ref.shape[0]
    half, side = first_keep.shape
    width = 2 * side
    part_width = width // PARTS
    copies = [
        pltpu.make_async_copy(
            w_ref.at[:, part * part_width : (part + 1) * part_width],
            held.at[:, part * part_width : (part + 1) * part_width],
            arrived.at[part],
        )
        for part in range(PARTS)
    ]
    for copy in copies:
        copy.start()
    shape = (2 * half, joined_ref.shape[0])
    row = lax.broadcasted_iota(jnp.int32, shape, 0)
    place = lax.broadcasted_iota(jnp.int32, shape, 1)
    turn = own_rows.bit_length() - 1
    far_bits = far.bit_length() - 1
    request, slot = row & (own_rows - 1), row >> turn
    far_at, slot = slot & (far - 1), slot >> far_bits
    distance = (far_at << 3) + ((slot & 1) << 2) + ((slot >> 1 & 1) << 1) + (slot >> 2)
    device = distance ^ here_ref[0]
    values = []
    for head in range(own_heads):
        wanted = ((device << turn) + request) * own_heads + head
        choice = (place == wanted).astype(jnp.float32).astype(jnp.bfloat16)
        latent = jnp.dot(choice, joined_ref[...], preferred_element_type=jnp.float32)
        value = jnp.dot(
            latent.astype(jnp.bfloat16), absorb_ref[head], preferred_element_type=jnp.float32
        )
        values.append(value.astype(jnp.bfloat16))
    values = jnp.concatenate(values, axis=1)
    for part in range(PARTS):
        copies[part].wait()
        for at in range(part * part_width, (part + 1) * part_width, TILE):
            term = jnp.dot(values, held[:, at : at + TILE], preferred_element_type=jnp.float32)
            store_sides(term, at, (first_keep, second_keep), (first_send, second_send))
    for at, keep in ((0, first_keep), (side, second_keep)):
        residual = residual_ref[:, at : at + side].astype(jnp.float32)
        keep[:own_rows, :] = keep[:own_rows, :] + residual


def project(here, joined, w_absorb, residual_in, w_out, rows, far):
    depth, width = w_out.shape
    own_rows = residual_in.shape[0]
    return pl.pallas_call(
        functools.partial(project_kernel, own_rows, far),
        out_shape=side_shapes(rows // 2, width),
        in_specs=[pl.BlockSpec(memory_space=pltpu.SMEM)]
        + [pl.BlockSpec(memory_space=pltpu.VMEM)] * 3
        + [pl.BlockSpec(memory_space=pl.ANY)],
        out_specs=(pl.BlockSpec(memory_space=pltpu.VMEM),) * 4,
        scratch_shapes=[
            pltpu.VMEM((depth, width), jnp.bfloat16),
            pltpu.SemaphoreType.DMA((PARTS,)),
        ],
        compiler_params=pltpu.CompilerParams(vmem_limit_bytes=55 * MIB),
        cost_estimate=pl.CostEstimate(
            flops=2 * rows * depth * width, bytes_accessed=2 * depth * width, transcendentals=0
        ),
        name="project",
    )(here, joined, w_absorb, residual_in, w_out)


def expert_kernel(
    first_own,
    first_other,
    second_own,
    second_other,
    gain_ref,
    gate_ref,
    up_ref,
    down_ref,
    first_keep,
    second_keep,
    first_send,
    second_send,
):
    half, side = first_own.shape
    width = 2 * side
    depth = width // PARTS
    streams = ((first_own, second_own), (first_other, second_other))
    inverses = []
    for stream in streams:
        squares = 0.0
        for ref in stream:
            for at in range(0, side, depth):
                piece = ref[:, at : at + depth].astype(jnp.float32)
                squares = squares + sum(lane_tiles(piece * piece))
        mean = jnp.sum(squares, axis=1, keepdims=True) / width
        inverses.append(lax.rsqrt(mean + 1e-06))
    gate, up = 0.0, 0.0
    for part in range(PARTS):
        at, place = part * depth, part * depth % side
        gain = gain_ref[:, at : at + depth]
        tokens = jnp.concatenate(
            [
                (
                    stream[at // side][:, place : place + depth].astype(jnp.float32)
                    * inverse
                    * gain
                ).astype(jnp.bfloat16)
                for stream, inverse in zip(streams, inverses)
            ],
            axis=0,
        )
        gate = gate + jnp.dot(
            tokens, gate_ref[at : at + depth, :], preferred_element_type=jnp.float32
        )
        up = up + jnp.dot(
            tokens, up_ref[at : at + depth, :], preferred_element_type=jnp.float32
        )
    active = (gate / (1.0 + jnp.exp(-gate)) * up).astype(jnp.bfloat16)
    for at in range(0, width, TILE):
        term = jnp.dot(active, down_ref[:, at : at + TILE], preferred_element_type=jnp.float32)
        store_sides(term, at, (first_keep, second_keep), (first_send, second_send))


def run_expert(streams, norm_gain, w_gate, w_up, w_down):
    half, side = streams[0].shape
    hidden = w_gate.shape[1]
    return pl.pallas_call(
        expert_kernel,
        out_shape=side_shapes(half, 2 * side),
        in_specs=[pl.BlockSpec(memory_space=pltpu.VMEM)] * 8,
        out_specs=(pl.BlockSpec(memory_space=pltpu.VMEM),) * 4,
        compiler_params=pltpu.CompilerParams(vmem_limit_bytes=24 * MIB),
        cost_estimate=pl.CostEstimate(
            flops=24 * half * hidden * side,
            bytes_accessed=12 * hidden * side,
            transcendentals=2 * half * hidden,
        ),
        name="expert",
    )(*streams, norm_gain[None], w_gate, w_up, w_down)


def swap(array, distance):
    pairs = [(at, at ^ distance) for at in range(lax.axis_size("experts"))]
    return lax.ppermute(array, "experts", pairs)


def wide(array):
    return array.astype(jnp.float32)


def collect(keep, send):
    half = keep.shape[0]
    step = half // 4
    whole = keep + wide(swap(send, 1))
    parts = [whole[at : at + step] for at in range(0, half, step)]
    total = parts[0]
    for part, distance in ((3, 6), (1, 4), (2, 2)):
        total = total + wide(swap(parts[part].astype(jnp.bfloat16), distance))
    return total


def exchange(total, far):
    own_rows = total.shape[0] // far
    sent = total.astype(jnp.bfloat16)
    for at in range(1, far):
        block = swap(sent, 8 * at)
        total = total + wide(
            jnp.concatenate(
                [block[(to ^ at) * own_rows : ((to ^ at) + 1) * own_rows] for to in range(far)]
            )
        )
    return total.astype(jnp.bfloat16)


def spread(stream):
    other = {distance: swap(stream, distance) for distance in (6, 4, 2)}
    own = jnp.concatenate([stream, other[4], other[2], other[6]])
    return own, swap(own, 1)


def shards(
    queries,
    cache,
    cache_len,
    residual_in,
    w_absorb,
    w_out,
    norm_gain,
    expert_ids,
    route_gates,
    w_gate,
    w_up,
    w_down,
):
    devices = lax.axis_size("experts")
    rank_here = lax.axis_index("experts")
    own_rows = queries.shape[0]
    all_rows = expert_ids.shape[0]
    far = devices // 8
    split_ways = FF // w_gate.shape[1]
    assert split_ways == 8

    latent = attend(queries, cache, cache_len, devices, w_absorb.shape[1])
    joined = lax.all_to_all(latent, "experts", split_axis=0, concat_axis=0, tiled=True)
    joined = joined.reshape(-1, joined.shape[-1])
    here = rank_here.astype(jnp.int32)[None]
    sides = project(here, joined, w_absorb, residual_in, w_out, all_rows, far)
    attended, streams = [], []
    for at in range(2):
        total = collect(sides[at], sides[at + 2])
        stream = exchange(total, far)
        attended.append(stream[:own_rows])
        streams.extend(spread(stream))
    attended = jnp.concatenate(attended, axis=1)

    sides = run_expert(streams, norm_gain, w_gate, w_up, w_down)
    own_ids = lax.dynamic_slice_in_dim(expert_ids, rank_here * own_rows, own_rows, 0)
    mixings = []
    for at in range(far):
        expert = (rank_here ^ (8 * at)) // split_ways
        mixings.append(
            jnp.sum(
                route_gates * (own_ids == expert).astype(jnp.float32), axis=1, keepdims=True
            )
        )
    expert_out = []
    for at in range(2):
        total = collect(sides[at], sides[at + 2])
        mixed = mixings[0] * total[:own_rows]
        for to in range(1, far):
            block = total[to * own_rows : (to + 1) * own_rows].astype(jnp.bfloat16)
            mixed = mixed + mixings[to] * wide(swap(block, 8 * to))
        expert_out.append(mixed.astype(jnp.bfloat16))
    return (attended, jnp.concatenate(expert_out, axis=1))


def solution(mesh):
    placed = (
        P(("groups", "experts"), None, None),
        P(("groups", "experts"), None, None),
        P(("groups", "experts")),
        P(("groups", "experts"), None),
        P("experts", None, None),
        P("experts", None),
        P(),
        P("groups", None),
        P(("groups", "experts"), None),
        P(None, "experts"),
        P(None, "experts"),
        P("experts", None),
    )
    return jax.shard_map(
        shards,
        mesh=mesh,
        in_specs=placed,
        out_specs=(P(("groups", "experts"), None), P(("groups", "experts"), None)),
        check_vma=False,
    )
```

```python
import functools

import jax
import jax.numpy as jnp
from jax import lax
from jax.experimental import pallas as pl
from jax.experimental.pallas import tpu as pltpu
from jax.sharding import PartitionSpec as P

QK = 192
FF = 2048
BLOCK = 512
GROUP = 4
LANES = 128
TILE = 256
PARTS = 4
MIB = 2**20


def lane_tiles(array):
    return [array[:, at : at + LANES] for at in range(0, array.shape[1], LANES)]


def attend_kernel(
    len_ref,
    queries_ref,
    cache_ref,
    latent_ref,
    length,
    queries,
    held,
    products,
    highest,
    sums,
    factors,
    even,
    odd,
    staged,
    item_row,
    item_block,
    length_arrived,
    queries_arrived,
    arrived,
):
    own_rows, heads, _ = queries.shape
    devices, _, rank = staged.shape
    own_heads = heads // devices
    blocks = held.shape[1]

    length_copy = pltpu.make_async_copy(len_ref, length, length_arrived)
    length_copy.start()
    queries_copy = pltpu.make_async_copy(queries_ref, queries, queries_arrived)
    queries_copy.start()

    def block_copy(row, block):
        return pltpu.make_async_copy(
            cache_ref.at[row, :, pl.ds(pl.multiple_of(block * BLOCK, BLOCK), BLOCK)],
            held.at[row, block],
            arrived.at[row, block],
        )

    highest[...] = jnp.full_like(highest, -jnp.inf)
    sums[...] = jnp.zeros_like(sums)
    length_copy.wait()
    items = 0
    counts = []
    for row in range(own_rows):
        count = (length[row] + BLOCK - 1) // BLOCK

        def begin(block, first, row=row):
            block_copy(row, block).start()
            item_row[first + block] = row
            item_block[first + block] = block
            return first

        lax.fori_loop(0, count, begin, items)
        counts.append(count)
        items = items + count
    for at in range(GROUP - 1):
        item_row[items + at] = own_rows - 1
        item_block[items + at] = item_block[items - 1]
    groups = (items + GROUP - 1) // GROUP
    queries_copy.wait()
    column = lax.broadcasted_iota(jnp.int32, (heads, BLOCK), 1)

    def members(group):
        return [
            (group * GROUP + at, item_row[group * GROUP + at], item_block[group * GROUP + at])
            for at in range(GROUP)
        ]

    def wait(group):
        for at, row, block in members(group):
            pl.when(at < items)(lambda row=row, block=block: block_copy(row, block).wait())

    def score(group, target):
        for to, (_, row, block) in enumerate(members(group)):
            found = jnp.dot(
                queries[row], held[row, block], preferred_element_type=jnp.float32
            ) * QK ** (-0.5)
            target[to] = jnp.where(column + block * BLOCK < length[row], found, -jnp.inf)

    def weigh(group, source):
        inside = members(group)
        tops = [
            jnp.max(
                functools.reduce(jnp.maximum, lane_tiles(source[at])), axis=1, keepdims=True
            )
            for at in range(GROUP)
        ]
        weights = [jnp.exp(source[at] - top) for at, top in enumerate(tops)]
        for (_, row, block), top, weight in zip(inside, tops, weights):
            highest[row, block] = jnp.broadcast_to(top, (heads, LANES))
            sums[row, block] = sum(lane_tiles(weight))
            products[row, block] = lax.dot_general(
                weight.astype(jnp.bfloat16),
                held[row, block, :rank, :],
                (((1,), (1,)), ((), ())),
                preferred_element_type=jnp.float32,
            )

    def step(group, now, later):
        @pl.when(group + 1 < groups)
        def _():
            wait(group + 1)
            score(group + 1, later)
            weigh(group, now)

        @pl.when(group + 1 == groups)
        def _():
            weigh(group, now)

    wait(0)
    score(0, even)

    def two_steps(pair, _):
        step(2 * pair, even, odd)
        step(2 * pair + 1, odd, even)
        return 0

    lax.fori_loop(0, (groups + 1) // 2, two_steps, 0)
    for row in range(own_rows):
        factor = jnp.exp(highest[row] - jnp.max(highest[row], axis=0, keepdims=True))
        total = jnp.sum(jnp.sum(sums[row] * factor, axis=0), axis=1, keepdims=True)
        factors[row] = factor * (1.0 / total)[None]
    for row in range(own_rows):

        def merge(block, latent, row=row):
            return latent + products[row, block] * factors[row, block][:, :1]

        latent = lax.fori_loop(
            0, counts[row], merge, jnp.zeros((heads, rank), jnp.float32)
        )
        for device in range(devices):
            staged[device, row * own_heads : (row + 1) * own_heads, :] = latent[
                device * own_heads : (device + 1) * own_heads
            ]
    latent_ref[...] = staged[...].astype(latent_ref.dtype)


def attend(queries, cache, cache_len, devices, rank):
    own_rows, depth, heads = queries.shape
    blocks = cache.shape[2] // BLOCK
    packed = own_rows * heads // devices
    listed = own_rows * blocks + GROUP
    return pl.pallas_call(
        attend_kernel,
        out_shape=jax.ShapeDtypeStruct((devices, packed, rank), jnp.bfloat16),
        in_specs=[pl.BlockSpec(memory_space=pl.ANY)] * 3,
        out_specs=pl.BlockSpec(memory_space=pltpu.VMEM),
        scratch_shapes=[
            pltpu.SMEM((own_rows,), jnp.int32),
            pltpu.VMEM((own_rows, heads, depth), jnp.bfloat16),
            pltpu.VMEM((own_rows, blocks, depth, BLOCK), jnp.bfloat16),
            pltpu.VMEM((own_rows, blocks, heads, rank), jnp.float32),
            pltpu.VMEM((own_rows, blocks, heads, LANES), jnp.float32),
            pltpu.VMEM((own_rows, blocks, heads, LANES), jnp.float32),
            pltpu.VMEM((own_rows, blocks, heads, LANES), jnp.float32),
            pltpu.VMEM((GROUP, heads, BLOCK), jnp.float32),
            pltpu.VMEM((GROUP, heads, BLOCK), jnp.float32),
            pltpu.VMEM((devices, packed, rank), jnp.float32),
            pltpu.SMEM((listed,), jnp.int32),
            pltpu.SMEM((listed,), jnp.int32),
            pltpu.SemaphoreType.DMA,
            pltpu.SemaphoreType.DMA,
            pltpu.SemaphoreType.DMA((own_rows, blocks)),
        ],
        compiler_params=pltpu.CompilerParams(vmem_limit_bytes=52 * MIB),
        cost_estimate=pl.CostEstimate(
            flops=own_rows * heads * cache.shape[2] * (depth + rank),
            bytes_accessed=cache.size,
            transcendentals=own_rows * heads * cache.shape[2],
        ),
        name="attend",
    )(cache_len, jnp.swapaxes(queries, 1, 2), cache)


def store_term(term, at, keep_ref, send_ref):
    half = keep_ref.shape[0]
    keep_ref[:, at : at + TILE] = term[:half]
    send_ref[:, at : at + TILE] = term[half:].astype(send_ref.dtype)


def term_shapes(half, width):
    return tuple(jax.ShapeDtypeStruct((half, width), kind) for kind in (jnp.float32, jnp.bfloat16))


def project_kernel(
    own_rows, far, here_ref, joined_ref, absorb_ref, residual_ref, w_ref, keep_ref, send_ref
):
    own_heads = absorb_ref.shape[0]
    half, width = keep_ref.shape
    shape = (2 * half, joined_ref.shape[0])
    row = lax.broadcasted_iota(jnp.int32, shape, 0)
    place = lax.broadcasted_iota(jnp.int32, shape, 1)
    turn = own_rows.bit_length() - 1
    far_bits = far.bit_length() - 1
    request, slot = row & (own_rows - 1), row >> turn
    far_at, slot = slot & (far - 1), slot >> far_bits
    distance = (far_at << 3) + ((slot & 1) << 2) + ((slot >> 1 & 1) << 1) + (slot >> 2)
    device = distance ^ here_ref[0]
    values = []
    for head in range(own_heads):
        wanted = ((device << turn) + request) * own_heads + head
        choice = (place == wanted).astype(jnp.float32).astype(jnp.bfloat16)
        latent = jnp.dot(choice, joined_ref[...], preferred_element_type=jnp.float32)
        value = jnp.dot(
            latent.astype(jnp.bfloat16), absorb_ref[head], preferred_element_type=jnp.float32
        )
        values.append(value.astype(jnp.bfloat16))
    values = jnp.concatenate(values, axis=1)
    for at in range(0, width, TILE):
        term = jnp.dot(values, w_ref[:, at : at + TILE], preferred_element_type=jnp.float32)
        store_term(term, at, keep_ref, send_ref)
    keep_ref[:own_rows, :] = keep_ref[:own_rows, :] + residual_ref[...].astype(jnp.float32)


def project(here, joined, w_absorb, residual_in, w_out, rows, far):
    depth, width = w_out.shape
    own_rows = residual_in.shape[0]
    return pl.pallas_call(
        functools.partial(project_kernel, own_rows, far),
        out_shape=term_shapes(rows // 2, width),
        in_specs=[pl.BlockSpec(memory_space=pltpu.SMEM)]
        + [pl.BlockSpec(memory_space=pltpu.VMEM)] * 4,
        out_specs=(pl.BlockSpec(memory_space=pltpu.VMEM),) * 2,
        compiler_params=pltpu.CompilerParams(vmem_limit_bytes=24 * MIB),
        cost_estimate=pl.CostEstimate(
            flops=2 * rows * depth * width, bytes_accessed=2 * depth * width, transcendentals=0
        ),
        name="project",
    )(here, joined, w_absorb, residual_in, w_out)


def expert_kernel(
    own_ref, other_ref, gain_ref, gate_ref, up_ref, down_ref, keep_ref, send_ref
):
    width = own_ref.shape[1]
    depth = width // PARTS
    streams = (own_ref, other_ref)
    inverses = []
    for stream in streams:
        squares = 0.0
        for at in range(0, width, depth):
            piece = stream[:, at : at + depth].astype(jnp.float32)
            squares = squares + sum(lane_tiles(piece * piece))
        mean = jnp.sum(squares, axis=1, keepdims=True) / width
        inverses.append(lax.rsqrt(mean + 1e-06))
    gate, up = 0.0, 0.0
    for at in range(0, width, depth):
        gain = gain_ref[:, at : at + depth]
        tokens = jnp.concatenate(
            [
                (stream[:, at : at + depth].astype(jnp.float32) * inverse * gain).astype(
                    jnp.bfloat16
                )
                for stream, inverse in zip(streams, inverses)
            ],
            axis=0,
        )
        gate = gate + jnp.dot(
            tokens, gate_ref[at : at + depth, :], preferred_element_type=jnp.float32
        )
        up = up + jnp.dot(
            tokens, up_ref[at : at + depth, :], preferred_element_type=jnp.float32
        )
    active = (gate / (1.0 + jnp.exp(-gate)) * up).astype(jnp.bfloat16)
    for at in range(0, width, TILE):
        term = jnp.dot(active, down_ref[:, at : at + TILE], preferred_element_type=jnp.float32)
        store_term(term, at, keep_ref, send_ref)


def run_expert(own, other, norm_gain, w_gate, w_up, w_down):
    half, width = own.shape
    hidden = w_gate.shape[1]
    return pl.pallas_call(
        expert_kernel,
        out_shape=term_shapes(half, width),
        in_specs=[pl.BlockSpec(memory_space=pltpu.VMEM)] * 6,
        out_specs=(pl.BlockSpec(memory_space=pltpu.VMEM),) * 2,
        compiler_params=pltpu.CompilerParams(vmem_limit_bytes=24 * MIB),
        cost_estimate=pl.CostEstimate(
            flops=12 * half * hidden * width,
            bytes_accessed=6 * hidden * width,
            transcendentals=2 * half * hidden,
        ),
        name="expert",
    )(own, other, norm_gain[None], w_gate, w_up, w_down)


def swap(array, distance):
    pairs = [(at, at ^ distance) for at in range(lax.axis_size("experts"))]
    return lax.ppermute(array, "experts", pairs)


def wide(array):
    return array.astype(jnp.float32)


def collect(keep, send):
    half = keep.shape[0]
    step = half // 4
    whole = keep + wide(swap(send, 1))
    parts = [whole[at : at + step] for at in range(0, half, step)]
    total = parts[0]
    for part, distance in ((3, 6), (1, 4), (2, 2)):
        total = total + wide(swap(parts[part].astype(jnp.bfloat16), distance))
    return total


def exchange(total, far):
    own_rows = total.shape[0] // far
    sent = total.astype(jnp.bfloat16)
    for at in range(1, far):
        block = swap(sent, 8 * at)
        total = total + wide(
            jnp.concatenate(
                [block[(to ^ at) * own_rows : ((to ^ at) + 1) * own_rows] for to in range(far)]
            )
        )
    return total.astype(jnp.bfloat16)


def squares():
    devices = lax.axis_size("experts")
    return [
        [core + 2 * y + 4 * near + 8 * far for y in range(2) for near in range(2)]
        for far in range(devices // 8)
        for core in range(2)
    ]


def shards(
    queries,
    cache,
    cache_len,
    residual_in,
    w_absorb,
    w_out,
    norm_gain,
    expert_ids,
    route_gates,
    w_gate,
    w_up,
    w_down,
):
    devices = lax.axis_size("experts")
    rank_here = lax.axis_index("experts")
    own_rows = queries.shape[0]
    all_rows = expert_ids.shape[0]
    far = devices // 8
    split_ways = FF // w_gate.shape[1]
    assert split_ways == 8

    latent = attend(queries, cache, cache_len, devices, w_absorb.shape[1])
    joined = lax.all_to_all(latent, "experts", split_axis=0, concat_axis=0, tiled=True)
    joined = joined.reshape(-1, joined.shape[-1])
    here = rank_here.astype(jnp.int32)[None]
    keep, send = project(here, joined, w_absorb, residual_in, w_out, all_rows, far)
    stream = exchange(collect(keep, send), far)
    attended = stream[:own_rows]

    own = lax.all_gather(stream, "experts", axis=0, tiled=True, axis_index_groups=squares())
    keep, send = run_expert(own, swap(own, 1), norm_gain, w_gate, w_up, w_down)

    total = (keep + wide(swap(send, 1))).astype(jnp.bfloat16)
    total = lax.all_to_all(
        total.reshape(4, far * own_rows, -1),
        "experts",
        split_axis=0,
        concat_axis=0,
        axis_index_groups=squares(),
        tiled=True,
    )
    total = jnp.sum(wide(total), axis=0)
    own_ids = lax.dynamic_slice_in_dim(expert_ids, rank_here * own_rows, own_rows, 0)
    expert_out = 0.0
    for at in range(far):
        block = total[at * own_rows : (at + 1) * own_rows]
        block = wide(swap(block.astype(jnp.bfloat16), 8 * at)) if at else block
        expert = (rank_here ^ (8 * at)) // split_ways
        mixing = jnp.sum(
            route_gates * (own_ids == expert).astype(jnp.float32), axis=1, keepdims=True
        )
        expert_out = expert_out + mixing * block
    return (attended, expert_out.astype(jnp.bfloat16))


def solution(mesh):
    placed = (
        P(("groups", "experts"), None, None),
        P(("groups", "experts"), None, None),
        P(("groups", "experts")),
        P(("groups", "experts"), None),
        P("experts", None, None),
        P("experts", None),
        P(),
        P("groups", None),
        P(("groups", "experts"), None),
        P(None, "experts"),
        P(None, "experts"),
        P("experts", None),
    )
    return jax.shard_map(
        shards,
        mesh=mesh,
        in_specs=placed,
        out_specs=(P(("groups", "experts"), None), P(("groups", "experts"), None)),
        check_vma=False,
    )
```

```python
import functools

import jax
import jax.numpy as jnp
from jax import lax
from jax.experimental import pallas as pl
from jax.experimental.pallas import tpu as pltpu
from jax.sharding import PartitionSpec as P

QK = 192
FF = 2048
BLOCK = 512
GROUP = 4
LANES = 128
TILE = 256
PARTS = 4
SQUARE = (0, 4, 2, 6)
PIECES = len(SQUARE)
MIB = 2**20


def lane_tiles(array):
    return [array[:, at : at + LANES] for at in range(0, array.shape[1], LANES)]


def attend_kernel(
    len_ref,
    queries_ref,
    cache_ref,
    latent_ref,
    length,
    queries,
    held,
    products,
    highest,
    sums,
    factors,
    staged,
    item_row,
    item_block,
    length_arrived,
    queries_arrived,
    arrived,
):
    own_rows, heads, _ = queries.shape
    devices, _, rank = staged.shape
    own_heads = heads // devices
    blocks = held.shape[1]

    length_copy = pltpu.make_async_copy(len_ref, length, length_arrived)
    length_copy.start()
    queries_copy = pltpu.make_async_copy(queries_ref, queries, queries_arrived)
    queries_copy.start()

    def block_copy(row, block):
        return pltpu.make_async_copy(
            cache_ref.at[row, :, pl.ds(pl.multiple_of(block * BLOCK, BLOCK), BLOCK)],
            held.at[row, block],
            arrived.at[row, block],
        )

    for row in range(own_rows):
        block_copy(row, 0).start()
        item_row[row] = row
        item_block[row] = 0
    highest[...] = jnp.full_like(highest, -jnp.inf)
    sums[...] = jnp.zeros_like(sums)
    length_copy.wait()
    items = own_rows
    counts = []
    for row in range(own_rows):
        count = (length[row] + BLOCK - 1) // BLOCK

        def begin(block, first, row=row):
            block_copy(row, block).start()
            item_row[first + block] = row
            item_block[first + block] = block
            return first

        lax.fori_loop(1, count, begin, items - 1)
        counts.append(count)
        items = items + count - 1
    queries_copy.wait()
    column = lax.broadcasted_iota(jnp.int32, (heads, BLOCK), 1)

    def visit(first, many):
        inside = [(item_row[first + at], item_block[first + at]) for at in range(many)]
        for row, block in inside:
            block_copy(row, block).wait()
        found = []
        for row, block in inside:
            score = jnp.dot(
                queries[row], held[row, block], preferred_element_type=jnp.float32
            ) * QK ** (-0.5)
            found.append(
                jnp.where(column + block * BLOCK < length[row], score, -jnp.inf)
            )
        tops = [
            jnp.max(functools.reduce(jnp.maximum, lane_tiles(score)), axis=1, keepdims=True)
            for score in found
        ]
        weights = [jnp.exp(score - top) for score, top in zip(found, tops)]
        for (row, block), top, weight in zip(inside, tops, weights):
            highest[row, block] = jnp.broadcast_to(top, (heads, LANES))
            sums[row, block] = sum(lane_tiles(weight))
            products[row, block] = lax.dot_general(
                weight.astype(jnp.bfloat16),
                held[row, block, :rank, :],
                (((1,), (1,)), ((), ())),
                preferred_element_type=jnp.float32,
            )

    def visit_group(group, _):
        visit(group * GROUP, GROUP)
        return 0

    whole = items // GROUP
    lax.fori_loop(0, whole, visit_group, 0)
    pl.when((items & 2) != 0)(lambda: visit(whole * GROUP, 2))
    pl.when((items & 1) != 0)(lambda: visit(items - 1, 1))
    for row in range(own_rows):
        factor = jnp.exp(highest[row] - jnp.max(highest[row], axis=0, keepdims=True))
        total = jnp.sum(jnp.sum(sums[row] * factor, axis=0), axis=1, keepdims=True)
        factors[row] = factor * (1.0 / total)[None]
    for row in range(own_rows):

        def merge(block, latent, row=row):
            return latent + products[row, block] * factors[row, block][:, :1]

        latent = lax.fori_loop(
            0, counts[row], merge, jnp.zeros((heads, rank), jnp.float32)
        )
        for device in range(devices):
            staged[device, row * own_heads : (row + 1) * own_heads, :] = latent[
                device * own_heads : (device + 1) * own_heads
            ]
    latent_ref[...] = staged[...].astype(latent_ref.dtype)


def attend(queries, cache, cache_len, devices, rank):
    own_rows, depth, heads = queries.shape
    blocks = cache.shape[2] // BLOCK
    packed = own_rows * heads // devices
    listed = own_rows * blocks
    return pl.pallas_call(
        attend_kernel,
        out_shape=jax.ShapeDtypeStruct((devices, packed, rank), jnp.bfloat16),
        in_specs=[pl.BlockSpec(memory_space=pl.ANY)] * 3,
        out_specs=pl.BlockSpec(memory_space=pltpu.VMEM),
        scratch_shapes=[
            pltpu.SMEM((own_rows,), jnp.int32),
            pltpu.VMEM((own_rows, heads, depth), jnp.bfloat16),
            pltpu.VMEM((own_rows, blocks, depth, BLOCK), jnp.bfloat16),
            pltpu.VMEM((own_rows, blocks, heads, rank), jnp.float32),
            pltpu.VMEM((own_rows, blocks, heads, LANES), jnp.float32),
            pltpu.VMEM((own_rows, blocks, heads, LANES), jnp.float32),
            pltpu.VMEM((own_rows, blocks, heads, LANES), jnp.float32),
            pltpu.VMEM((devices, packed, rank), jnp.float32),
            pltpu.SMEM((listed,), jnp.int32),
            pltpu.SMEM((listed,), jnp.int32),
            pltpu.SemaphoreType.DMA,
            pltpu.SemaphoreType.DMA,
            pltpu.SemaphoreType.DMA((own_rows, blocks)),
        ],
        compiler_params=pltpu.CompilerParams(vmem_limit_bytes=55 * MIB),
        cost_estimate=pl.CostEstimate(
            flops=own_rows * heads * cache.shape[2] * (depth + rank),
            bytes_accessed=cache.size,
            transcendentals=own_rows * heads * cache.shape[2],
        ),
        name="attend",
    )(cache_len, jnp.swapaxes(queries, 1, 2), cache)


def store_term(term, at, refs):
    rows = term.shape[0] // len(refs)
    for piece, ref in enumerate(refs):
        ref[:, at : at + TILE] = term[piece * rows : (piece + 1) * rows].astype(ref.dtype)


def term_shapes(rows, width):
    return tuple(
        jax.ShapeDtypeStruct((rows, width), kind)
        for kind in (jnp.float32, jnp.bfloat16)
        for _ in range(PIECES)
    )


def project_kernel(own_rows, far, joined_ref, residual_ref, absorb_ref, w_ref, *pieces):
    own_heads = absorb_ref.shape[0]
    width = w_ref.shape[1]
    shape = (len(pieces) * pieces[0].shape[0], joined_ref.shape[0])
    row = lax.broadcasted_iota(jnp.int32, shape, 0)
    place = lax.broadcasted_iota(jnp.int32, shape, 1)
    turn = own_rows.bit_length() - 1
    far_bits = far.bit_length() - 1
    request, slot = row & (own_rows - 1), row >> turn
    far_at, slot = slot & (far - 1), slot >> far_bits
    distance = (far_at << 3) + ((slot & 1) << 2) + ((slot >> 1 & 1) << 1) + (slot >> 2)
    device = distance ^ lax.axis_index("experts")
    values = []
    for head in range(own_heads):
        wanted = ((device << turn) + request) * own_heads + head
        choice = (place == wanted).astype(jnp.float32).astype(jnp.bfloat16)
        latent = jnp.dot(choice, joined_ref[...], preferred_element_type=jnp.float32)
        value = jnp.dot(
            latent.astype(jnp.bfloat16), absorb_ref[head], preferred_element_type=jnp.float32
        )
        values.append(value.astype(jnp.bfloat16))
    values = jnp.concatenate(values, axis=1)
    for at in range(0, width, TILE):
        term = jnp.dot(values, w_ref[:, at : at + TILE], preferred_element_type=jnp.float32)
        store_term(term, at, pieces)
    residual = residual_ref[...].astype(jnp.float32)
    pieces[0][:own_rows, :] = pieces[0][:own_rows, :] + residual


def project(joined, w_absorb, residual_in, w_out, rows, far):
    depth, width = w_out.shape
    own_rows = residual_in.shape[0]
    return pl.pallas_call(
        functools.partial(project_kernel, own_rows, far),
        out_shape=term_shapes(rows // (2 * PIECES), width),
        in_specs=[pl.BlockSpec(memory_space=pltpu.VMEM)] * 4,
        out_specs=(pl.BlockSpec(memory_space=pltpu.VMEM),) * (2 * PIECES),
        compiler_params=pltpu.CompilerParams(vmem_limit_bytes=24 * MIB),
        cost_estimate=pl.CostEstimate(
            flops=2 * rows * depth * width, bytes_accessed=2 * depth * width, transcendentals=0
        ),
        name="project",
    )(joined, residual_in, w_absorb, w_out)


def expert_kernel(*refs):
    streams, (gain_ref, gate_ref, up_ref, down_ref), pieces = refs[:8], refs[8:12], refs[12:]
    width = gain_ref.shape[1]
    depth = width // PARTS
    inverses = []
    for stream in streams:
        squares = 0.0
        for at in range(0, width, depth):
            piece = stream[:, at : at + depth].astype(jnp.float32)
            squares = squares + sum(lane_tiles(piece * piece))
        mean = jnp.sum(squares, axis=1, keepdims=True) / width
        inverses.append(lax.rsqrt(mean + 1e-06))
    gate, up = 0.0, 0.0
    for at in range(0, width, depth):
        gain = gain_ref[:, at : at + depth]
        tokens = jnp.concatenate(
            [
                stream[:, at : at + depth].astype(jnp.float32) * inverse * gain
                for stream, inverse in zip(streams, inverses)
            ],
            axis=0,
        ).astype(jnp.bfloat16)
        gate = gate + jnp.dot(
            tokens, gate_ref[at : at + depth, :], preferred_element_type=jnp.float32
        )
        up = up + jnp.dot(
            tokens, up_ref[at : at + depth, :], preferred_element_type=jnp.float32
        )
    active = (gate / (1.0 + jnp.exp(-gate)) * up).astype(jnp.bfloat16)
    for at in range(0, width, TILE):
        term = jnp.dot(active, down_ref[:, at : at + TILE], preferred_element_type=jnp.float32)
        store_term(term, at, pieces)


def run_expert(streams, norm_gain, w_gate, w_up, w_down):
    rows, width = streams[0].shape
    hidden = w_gate.shape[1]
    return pl.pallas_call(
        expert_kernel,
        out_shape=term_shapes(rows, width),
        in_specs=[pl.BlockSpec(memory_space=pltpu.VMEM)] * (2 * PIECES + 4),
        out_specs=(pl.BlockSpec(memory_space=pltpu.VMEM),) * (2 * PIECES),
        compiler_params=pltpu.CompilerParams(vmem_limit_bytes=24 * MIB),
        cost_estimate=pl.CostEstimate(
            flops=12 * PIECES * rows * hidden * width,
            bytes_accessed=6 * hidden * width,
            transcendentals=2 * PIECES * rows * hidden,
        ),
        name="expert",
    )(*streams, norm_gain[None], w_gate, w_up, w_down)


def swap(array, distance):
    pairs = [(at, at ^ distance) for at in range(lax.axis_size("experts"))]
    return lax.ppermute(array, "experts", pairs)


def wide(array):
    return array.astype(jnp.float32)


def collect(terms):
    keeps, sends = terms[:PIECES], terms[PIECES:]
    total = 0.0
    for piece in (3, 1, 2, 0):
        part = keeps[piece] + wide(swap(sends[piece], 1))
        if piece:
            part = wide(swap(part.astype(jnp.bfloat16), SQUARE[piece]))
        total = total + part
    return total


def exchange(total, far):
    own_rows = total.shape[0] // far
    sent = total.astype(jnp.bfloat16)
    for at in range(1, far):
        block = swap(sent, 8 * at)
        total = total + wide(
            jnp.concatenate(
                [block[(to ^ at) * own_rows : ((to ^ at) + 1) * own_rows] for to in range(far)]
            )
        )
    return total.astype(jnp.bfloat16)


def spread(stream):
    own = [swap(stream, distance) if distance else stream for distance in SQUARE]
    return own + [swap(piece, 1) for piece in own]


def shards(
    queries,
    cache,
    cache_len,
    residual_in,
    w_absorb,
    w_out,
    norm_gain,
    expert_ids,
    route_gates,
    w_gate,
    w_up,
    w_down,
):
    devices = lax.axis_size("experts")
    rank_here = lax.axis_index("experts")
    own_rows = queries.shape[0]
    all_rows = expert_ids.shape[0]
    far = devices // 8
    split_ways = FF // w_gate.shape[1]
    assert split_ways == 8

    latent = attend(queries, cache, cache_len, devices, w_absorb.shape[1])
    joined = lax.all_to_all(latent, "experts", split_axis=0, concat_axis=0, tiled=True)
    joined = joined.reshape(-1, joined.shape[-1])
    terms = project(joined, w_absorb, residual_in, w_out, all_rows, far)
    stream = exchange(collect(terms), far)
    attended = stream[:own_rows]

    total = collect(run_expert(spread(stream), norm_gain, w_gate, w_up, w_down))
    own_ids = lax.dynamic_slice_in_dim(expert_ids, rank_here * own_rows, own_rows, 0)
    expert_out = 0.0
    for at in range(far):
        block = total[at * own_rows : (at + 1) * own_rows]
        block = wide(swap(block.astype(jnp.bfloat16), 8 * at)) if at else block
        expert = (rank_here ^ (8 * at)) // split_ways
        mixing = jnp.sum(
            route_gates * (own_ids == expert).astype(jnp.float32), axis=1, keepdims=True
        )
        expert_out = expert_out + mixing * block
    return (attended, expert_out.astype(jnp.bfloat16))


def solution(mesh):
    placed = (
        P(("groups", "experts"), None, None),
        P(("groups", "experts"), None, None),
        P(("groups", "experts")),
        P(("groups", "experts"), None),
        P("experts", None, None),
        P("experts", None),
        P(),
        P("groups", None),
        P(("groups", "experts"), None),
        P(None, "experts"),
        P(None, "experts"),
        P("experts", None),
    )
    return jax.shard_map(
        shards,
        mesh=mesh,
        in_specs=placed,
        out_specs=(P(("groups", "experts"), None), P(("groups", "experts"), None)),
        check_vma=False,
    )
```

```python
import functools

import jax
import jax.numpy as jnp
from jax import lax
from jax.experimental import pallas as pl
from jax.experimental.pallas import tpu as pltpu
from jax.sharding import PartitionSpec as P

QK = 192
FF = 2048
BLOCK = 512
GROUP = 4
LANES = 128
TILE = 256
PARTS = 4
SQUARE = (0, 6, 4, 2)
PIECES = len(SQUARE)
MIB = 2**20


def lane_tiles(array):
    return [array[:, at : at + LANES] for at in range(0, array.shape[1], LANES)]


def attend_kernel(
    len_ref,
    queries_ref,
    cache_ref,
    near_ref,
    across_ref,
    length,
    queries,
    held,
    products,
    highest,
    sums,
    factors,
    staged,
    item_row,
    item_block,
    length_arrived,
    queries_arrived,
    arrived,
):
    own_rows, heads, _ = queries.shape
    devices, _, rank = staged.shape
    own_heads = heads // devices
    blocks = held.shape[1]

    length_copy = pltpu.make_async_copy(len_ref, length, length_arrived)
    length_copy.start()
    queries_copy = pltpu.make_async_copy(queries_ref, queries, queries_arrived)
    queries_copy.start()

    def block_copy(row, block):
        return pltpu.make_async_copy(
            cache_ref.at[row, :, pl.ds(pl.multiple_of(block * BLOCK, BLOCK), BLOCK)],
            held.at[row, block],
            arrived.at[row, block],
        )

    for row in range(own_rows):
        block_copy(row, 0).start()
        item_row[row] = row
        item_block[row] = 0
    highest[...] = jnp.full_like(highest, -jnp.inf)
    sums[...] = jnp.zeros_like(sums)
    length_copy.wait()
    items = own_rows
    counts = []
    for row in range(own_rows):
        count = (length[row] + BLOCK - 1) // BLOCK

        def begin(block, first, row=row):
            block_copy(row, block).start()
            item_row[first + block] = row
            item_block[first + block] = block
            return first

        lax.fori_loop(1, count, begin, items - 1)
        counts.append(count)
        items = items + count - 1
    queries_copy.wait()
    column = lax.broadcasted_iota(jnp.int32, (heads, BLOCK), 1)

    def visit(first, many):
        inside = [(item_row[first + at], item_block[first + at]) for at in range(many)]
        for row, block in inside:
            block_copy(row, block).wait()
        found = []
        for row, block in inside:
            score = jnp.dot(
                queries[row], held[row, block], preferred_element_type=jnp.float32
            ) * QK ** (-0.5)
            found.append(
                jnp.where(column + block * BLOCK < length[row], score, -jnp.inf)
            )
        tops = [
            jnp.max(functools.reduce(jnp.maximum, lane_tiles(score)), axis=1, keepdims=True)
            for score in found
        ]
        weights = [jnp.exp(score - top) for score, top in zip(found, tops)]
        for (row, block), top, weight in zip(inside, tops, weights):
            highest[row, block] = jnp.broadcast_to(top, (heads, LANES))
            sums[row, block] = sum(lane_tiles(weight))
            products[row, block] = lax.dot_general(
                weight.astype(jnp.bfloat16),
                held[row, block, :rank, :],
                (((1,), (1,)), ((), ())),
                preferred_element_type=jnp.float32,
            )

    def visit_group(group, _):
        visit(group * GROUP, GROUP)
        return 0

    whole = items // GROUP
    lax.fori_loop(0, whole, visit_group, 0)
    pl.when((items & 2) != 0)(lambda: visit(whole * GROUP, 2))
    pl.when((items & 1) != 0)(lambda: visit(items - 1, 1))
    for row in range(own_rows):
        factor = jnp.exp(highest[row] - jnp.max(highest[row], axis=0, keepdims=True))
        total = jnp.sum(jnp.sum(sums[row] * factor, axis=0), axis=1, keepdims=True)
        factors[row] = factor * (1.0 / total)[None]
    for row in range(own_rows):

        def merge(block, tiles, row=row):
            factor = factors[row, block]
            return tuple(
                tile + product * factor
                for tile, product in zip(tiles, lane_tiles(products[row, block]))
            )

        tiles = lax.fori_loop(
            0,
            counts[row],
            merge,
            (jnp.zeros((heads, LANES), jnp.float32),) * (rank // LANES),
        )
        latent = jnp.concatenate(tiles, axis=1)
        for device in range(devices):
            staged[device, row * own_heads : (row + 1) * own_heads, :] = latent[
                device * own_heads : (device + 1) * own_heads
            ]
    core = lax.axis_index("experts") & 1
    for chip in range(devices // 2):
        near_ref[chip] = staged[2 * chip + core].astype(near_ref.dtype)
        across_ref[chip] = staged[2 * chip + 1 - core].astype(across_ref.dtype)


def attend(queries, cache, cache_len, devices, rank):
    own_rows, depth, heads = queries.shape
    blocks = cache.shape[2] // BLOCK
    packed = own_rows * heads // devices
    listed = own_rows * blocks
    return pl.pallas_call(
        attend_kernel,
        out_shape=(jax.ShapeDtypeStruct((devices // 2, packed, rank), jnp.bfloat16),) * 2,
        in_specs=[pl.BlockSpec(memory_space=pl.ANY)] * 3,
        out_specs=(pl.BlockSpec(memory_space=pltpu.VMEM),) * 2,
        scratch_shapes=[
            pltpu.SMEM((own_rows,), jnp.int32),
            pltpu.VMEM((own_rows, heads, depth), jnp.bfloat16),
            pltpu.VMEM((own_rows, blocks, depth, BLOCK), jnp.bfloat16),
            pltpu.VMEM((own_rows, blocks, heads, rank), jnp.float32),
            pltpu.VMEM((own_rows, blocks, heads, LANES), jnp.float32),
            pltpu.VMEM((own_rows, blocks, heads, LANES), jnp.float32),
            pltpu.VMEM((own_rows, blocks, heads, LANES), jnp.float32),
            pltpu.VMEM((devices, packed, rank), jnp.float32),
            pltpu.SMEM((listed,), jnp.int32),
            pltpu.SMEM((listed,), jnp.int32),
            pltpu.SemaphoreType.DMA,
            pltpu.SemaphoreType.DMA,
            pltpu.SemaphoreType.DMA((own_rows, blocks)),
        ],
        compiler_params=pltpu.CompilerParams(vmem_limit_bytes=55 * MIB),
        cost_estimate=pl.CostEstimate(
            flops=own_rows * heads * cache.shape[2] * (depth + rank),
            bytes_accessed=cache.size,
            transcendentals=own_rows * heads * cache.shape[2],
        ),
        name="attend",
    )(cache_len, jnp.swapaxes(queries, 1, 2), cache)


def store_term(term, at, refs):
    rows = term.shape[0] // len(refs)
    for piece, ref in enumerate(refs):
        ref[:, at : at + TILE] = term[piece * rows : (piece + 1) * rows].astype(ref.dtype)


def term_shapes(rows, width):
    return tuple(
        jax.ShapeDtypeStruct((rows, width), kind)
        for kind in (jnp.float32, jnp.bfloat16)
        for _ in range(PIECES)
    )


def project_kernel(own_rows, far, joined_ref, residual_ref, absorb_ref, w_ref, *pieces):
    own_heads = absorb_ref.shape[0]
    width = w_ref.shape[1]
    shape = (len(pieces) * pieces[0].shape[0], joined_ref.shape[0])
    row = lax.broadcasted_iota(jnp.int32, shape, 0)
    place = lax.broadcasted_iota(jnp.int32, shape, 1)
    turn = own_rows.bit_length() - 1
    far_bits = far.bit_length() - 1
    request, slot = row & (own_rows - 1), row >> turn
    far_at, slot = slot & (far - 1), slot >> far_bits
    distance = (far_at << 3) + ((4 - (slot & 3) & 3) << 1) + (slot >> 2)
    device = distance ^ lax.axis_index("experts")
    device = (device & ~1) + (distance & 1)
    values = []
    for head in range(own_heads):
        wanted = ((device << turn) + request) * own_heads + head
        choice = (place == wanted).astype(jnp.float32).astype(jnp.bfloat16)
        latent = jnp.dot(choice, joined_ref[...], preferred_element_type=jnp.float32)
        value = jnp.dot(
            latent.astype(jnp.bfloat16), absorb_ref[head], preferred_element_type=jnp.float32
        )
        values.append(value.astype(jnp.bfloat16))
    values = jnp.concatenate(values, axis=1)
    for at in range(0, width, TILE):
        term = jnp.dot(values, w_ref[:, at : at + TILE], preferred_element_type=jnp.float32)
        store_term(term, at, pieces)
    residual = residual_ref[...].astype(jnp.float32)
    pieces[0][:own_rows, :] = pieces[0][:own_rows, :] + residual


def project(joined, w_absorb, residual_in, w_out, rows, far):
    depth, width = w_out.shape
    own_rows = residual_in.shape[0]
    return pl.pallas_call(
        functools.partial(project_kernel, own_rows, far),
        out_shape=term_shapes(rows // (2 * PIECES), width),
        in_specs=[pl.BlockSpec(memory_space=pltpu.VMEM)] * 4,
        out_specs=(pl.BlockSpec(memory_space=pltpu.VMEM),) * (2 * PIECES),
        compiler_params=pltpu.CompilerParams(vmem_limit_bytes=24 * MIB),
        cost_estimate=pl.CostEstimate(
            flops=2 * rows * depth * width, bytes_accessed=2 * depth * width, transcendentals=0
        ),
        name="project",
    )(joined, residual_in, w_absorb, w_out)


def expert_kernel(*refs):
    streams, (gain_ref, gate_ref, up_ref, down_ref), pieces = refs[:8], refs[8:12], refs[12:]
    width = gain_ref.shape[1]
    depth = width // PARTS
    inverses = []
    for stream in streams:
        squares = 0.0
        for at in range(0, width, depth):
            piece = stream[:, at : at + depth].astype(jnp.float32)
            squares = squares + sum(lane_tiles(piece * piece))
        mean = jnp.sum(squares, axis=1, keepdims=True) / width
        inverses.append(lax.rsqrt(mean + 1e-06))
    gate, up = 0.0, 0.0
    for at in range(0, width, depth):
        gain = gain_ref[:, at : at + depth]
        tokens = jnp.concatenate(
            [
                stream[:, at : at + depth].astype(jnp.float32) * inverse * gain
                for stream, inverse in zip(streams, inverses)
            ],
            axis=0,
        ).astype(jnp.bfloat16)
        gate = gate + jnp.dot(
            tokens, gate_ref[at : at + depth, :], preferred_element_type=jnp.float32
        )
        up = up + jnp.dot(
            tokens, up_ref[at : at + depth, :], preferred_element_type=jnp.float32
        )
    active = (gate / (1.0 + jnp.exp(-gate)) * up).astype(jnp.bfloat16)
    for at in range(0, width, TILE):
        term = jnp.dot(active, down_ref[:, at : at + TILE], preferred_element_type=jnp.float32)
        store_term(term, at, pieces)


def run_expert(streams, norm_gain, w_gate, w_up, w_down):
    rows, width = streams[0].shape
    hidden = w_gate.shape[1]
    return pl.pallas_call(
        expert_kernel,
        out_shape=term_shapes(rows, width),
        in_specs=[pl.BlockSpec(memory_space=pltpu.VMEM)] * (2 * PIECES + 4),
        out_specs=(pl.BlockSpec(memory_space=pltpu.VMEM),) * (2 * PIECES),
        compiler_params=pltpu.CompilerParams(vmem_limit_bytes=24 * MIB),
        cost_estimate=pl.CostEstimate(
            flops=12 * PIECES * rows * hidden * width,
            bytes_accessed=6 * hidden * width,
            transcendentals=2 * PIECES * rows * hidden,
        ),
        name="expert",
    )(*streams, norm_gain[None], w_gate, w_up, w_down)


def swap(array, distance):
    pairs = [(at, at ^ distance) for at in range(lax.axis_size("experts"))]
    return lax.ppermute(array, "experts", pairs)


def wide(array):
    return array.astype(jnp.float32)


def collect(terms):
    keeps, sends = terms[:PIECES], terms[PIECES:]
    total = 0.0
    for piece in (1, 2, 3, 0):
        part = keeps[piece] + wide(swap(sends[piece], 1))
        if piece:
            part = wide(swap(part.astype(jnp.bfloat16), SQUARE[piece]))
        total = total + part
    return total


def exchange(total, far):
    own_rows = total.shape[0] // far
    sent = total.astype(jnp.bfloat16)
    for at in range(1, far):
        block = swap(sent, 8 * at)
        total = total + wide(
            jnp.concatenate(
                [block[(to ^ at) * own_rows : ((to ^ at) + 1) * own_rows] for to in range(far)]
            )
        )
    return total.astype(jnp.bfloat16)


def spread(stream):
    own = [swap(stream, distance) if distance else stream for distance in SQUARE]
    return own + [swap(piece, 1) for piece in own]


def shards(
    queries,
    cache,
    cache_len,
    residual_in,
    w_absorb,
    w_out,
    norm_gain,
    expert_ids,
    route_gates,
    w_gate,
    w_up,
    w_down,
):
    devices = lax.axis_size("experts")
    rank_here = lax.axis_index("experts")
    own_rows = queries.shape[0]
    all_rows = expert_ids.shape[0]
    far = devices // 8
    split_ways = FF // w_gate.shape[1]
    assert split_ways == 8

    near, across = attend(queries, cache, cache_len, devices, w_absorb.shape[1])
    same_core = [[2 * chip + core for chip in range(devices // 2)] for core in range(2)]
    joined = lax.all_to_all(
        jnp.concatenate([near, swap(across, 1)], axis=1),
        "experts",
        split_axis=0,
        concat_axis=0,
        axis_index_groups=same_core,
        tiled=True,
    )
    joined = joined.reshape(-1, joined.shape[-1])
    terms = project(joined, w_absorb, residual_in, w_out, all_rows, far)
    stream = exchange(collect(terms), far)
    attended = stream[:own_rows]

    total = collect(run_expert(spread(stream), norm_gain, w_gate, w_up, w_down))
    own_ids = lax.dynamic_slice_in_dim(expert_ids, rank_here * own_rows, own_rows, 0)
    expert_out = 0.0
    for at in range(far):
        block = total[at * own_rows : (at + 1) * own_rows]
        block = wide(swap(block.astype(jnp.bfloat16), 8 * at)) if at else block
        expert = (rank_here ^ (8 * at)) // split_ways
        mixing = jnp.sum(
            route_gates * (own_ids == expert).astype(jnp.float32), axis=1, keepdims=True
        )
        expert_out = expert_out + mixing * block
    return (attended, expert_out.astype(jnp.bfloat16))


def solution(mesh):
    placed = (
        P(("groups", "experts"), None, None),
        P(("groups", "experts"), None, None),
        P(("groups", "experts")),
        P(("groups", "experts"), None),
        P("experts", None, None),
        P("experts", None),
        P(),
        P("groups", None),
        P(("groups", "experts"), None),
        P(None, "experts"),
        P(None, "experts"),
        P("experts", None),
    )
    return jax.shard_map(
        shards,
        mesh=mesh,
        in_specs=placed,
        out_specs=(P(("groups", "experts"), None), P(("groups", "experts"), None)),
        check_vma=False,
    )
```

```python
import functools

import jax
import jax.numpy as jnp
from jax import lax
from jax.experimental import pallas as pl
from jax.experimental.pallas import tpu as pltpu
from jax.sharding import PartitionSpec as P

QK = 192
FF = 2048
BLOCK = 512
GROUP = 4
LANES = 128
TILE = 256
PARTS = 4
SQUARE = (0, 6, 4, 2)
PIECES = len(SQUARE)
MIB = 2**20


def lane_tiles(array):
    return [array[:, at : at + LANES] for at in range(0, array.shape[1], LANES)]


def attend_kernel(
    len_ref,
    queries_ref,
    cache_ref,
    latent_ref,
    length,
    queries,
    held,
    products,
    highest,
    sums,
    factors,
    staged,
    item_row,
    item_block,
    length_arrived,
    queries_arrived,
    arrived,
):
    own_rows, heads, _ = queries.shape
    devices, _, rank = staged.shape
    own_heads = heads // devices
    blocks = held.shape[1]

    length_copy = pltpu.make_async_copy(len_ref, length, length_arrived)
    length_copy.start()
    queries_copy = pltpu.make_async_copy(queries_ref, queries, queries_arrived)
    queries_copy.start()

    def block_copy(row, block):
        return pltpu.make_async_copy(
            cache_ref.at[row, :, pl.ds(pl.multiple_of(block * BLOCK, BLOCK), BLOCK)],
            held.at[row, block],
            arrived.at[row, block],
        )

    for row in range(own_rows):
        block_copy(row, 0).start()
        item_row[row] = row
        item_block[row] = 0
    highest[...] = jnp.full_like(highest, -jnp.inf)
    sums[...] = jnp.zeros_like(sums)
    length_copy.wait()
    items = own_rows
    counts = []
    for row in range(own_rows):
        count = (length[row] + BLOCK - 1) // BLOCK

        def begin(block, first, row=row):
            block_copy(row, block).start()
            item_row[first + block] = row
            item_block[first + block] = block
            return first

        lax.fori_loop(1, count, begin, items - 1)
        counts.append(count)
        items = items + count - 1
    queries_copy.wait()
    column = lax.broadcasted_iota(jnp.int32, (heads, BLOCK), 1)

    def visit(first, many):
        inside = [(item_row[first + at], item_block[first + at]) for at in range(many)]
        for row, block in inside:
            block_copy(row, block).wait()
        found = []
        for row, block in inside:
            score = jnp.dot(
                queries[row], held[row, block], preferred_element_type=jnp.float32
            ) * QK ** (-0.5)
            found.append(
                jnp.where(column + block * BLOCK < length[row], score, -jnp.inf)
            )
        tops = [
            jnp.max(functools.reduce(jnp.maximum, lane_tiles(score)), axis=1, keepdims=True)
            for score in found
        ]
        weights = [jnp.exp(score - top) for score, top in zip(found, tops)]
        for (row, block), top, weight in zip(inside, tops, weights):
            highest[row, block] = jnp.broadcast_to(top, (heads, LANES))
            sums[row, block] = sum(lane_tiles(weight))
            products[row, block] = lax.dot_general(
                weight.astype(jnp.bfloat16),
                held[row, block, :rank, :],
                (((1,), (1,)), ((), ())),
                preferred_element_type=jnp.float32,
            )

    def visit_group(group, _):
        visit(group * GROUP, GROUP)
        return 0

    whole = items // GROUP
    lax.fori_loop(0, whole, visit_group, 0)
    pl.when((items & 2) != 0)(lambda: visit(whole * GROUP, 2))
    pl.when((items & 1) != 0)(lambda: visit(items - 1, 1))
    for row in range(own_rows):
        factor = jnp.exp(highest[row] - jnp.max(highest[row], axis=0, keepdims=True))
        total = jnp.sum(jnp.sum(sums[row] * factor, axis=0), axis=1, keepdims=True)
        factors[row] = factor * (1.0 / total)[None]
    for row in range(own_rows):

        def merge(block, tiles, row=row):
            factor = factors[row, block]
            return tuple(
                tile + product * factor
                for tile, product in zip(tiles, lane_tiles(products[row, block]))
            )

        tiles = lax.fori_loop(
            0,
            counts[row],
            merge,
            (jnp.zeros((heads, LANES), jnp.float32),) * (rank // LANES),
        )
        latent = jnp.concatenate(tiles, axis=1)
        for device in range(devices):
            staged[device, row * own_heads : (row + 1) * own_heads, :] = latent[
                device * own_heads : (device + 1) * own_heads
            ]
    latent_ref[...] = staged[...].astype(latent_ref.dtype)


def attend(queries, cache, cache_len, devices, rank):
    own_rows, depth, heads = queries.shape
    blocks = cache.shape[2] // BLOCK
    packed = own_rows * heads // devices
    listed = own_rows * blocks
    return pl.pallas_call(
        attend_kernel,
        out_shape=jax.ShapeDtypeStruct((devices, packed, rank), jnp.bfloat16),
        in_specs=[pl.BlockSpec(memory_space=pl.ANY)] * 3,
        out_specs=pl.BlockSpec(memory_space=pltpu.VMEM),
        scratch_shapes=[
            pltpu.SMEM((own_rows,), jnp.int32),
            pltpu.VMEM((own_rows, heads, depth), jnp.bfloat16),
            pltpu.VMEM((own_rows, blocks, depth, BLOCK), jnp.bfloat16),
            pltpu.VMEM((own_rows, blocks, heads, rank), jnp.float32),
            pltpu.VMEM((own_rows, blocks, heads, LANES), jnp.float32),
            pltpu.VMEM((own_rows, blocks, heads, LANES), jnp.float32),
            pltpu.VMEM((own_rows, blocks, heads, LANES), jnp.float32),
            pltpu.VMEM((devices, packed, rank), jnp.float32),
            pltpu.SMEM((listed,), jnp.int32),
            pltpu.SMEM((listed,), jnp.int32),
            pltpu.SemaphoreType.DMA,
            pltpu.SemaphoreType.DMA,
            pltpu.SemaphoreType.DMA((own_rows, blocks)),
        ],
        compiler_params=pltpu.CompilerParams(vmem_limit_bytes=55 * MIB),
        cost_estimate=pl.CostEstimate(
            flops=own_rows * heads * cache.shape[2] * (depth + rank),
            bytes_accessed=cache.size,
            transcendentals=own_rows * heads * cache.shape[2],
        ),
        name="attend",
    )(cache_len, jnp.swapaxes(queries, 1, 2), cache)


def store_term(term, at, refs):
    rows = term.shape[0] // len(refs)
    for piece, ref in enumerate(refs):
        ref[:, at : at + TILE] = term[piece * rows : (piece + 1) * rows].astype(ref.dtype)


def term_shapes(rows, width):
    return tuple(
        jax.ShapeDtypeStruct((rows, width), kind)
        for kind in (jnp.float32, jnp.bfloat16)
        for _ in range(PIECES)
    )


def project_kernel(own_rows, far, joined_ref, residual_ref, absorb_ref, w_ref, *pieces):
    own_heads = absorb_ref.shape[0]
    width = w_ref.shape[1]
    shape = (len(pieces) * pieces[0].shape[0], joined_ref.shape[0])
    row = lax.broadcasted_iota(jnp.int32, shape, 0)
    place = lax.broadcasted_iota(jnp.int32, shape, 1)
    turn = own_rows.bit_length() - 1
    far_bits = far.bit_length() - 1
    request, slot = row & (own_rows - 1), row >> turn
    far_at, slot = slot & (far - 1), slot >> far_bits
    distance = (far_at << 3) + ((4 - (slot & 3) & 3) << 1) + (slot >> 2)
    device = distance ^ lax.axis_index("experts")
    values = []
    for head in range(own_heads):
        wanted = ((device << turn) + request) * own_heads + head
        choice = (place == wanted).astype(jnp.float32).astype(jnp.bfloat16)
        latent = jnp.dot(choice, joined_ref[...], preferred_element_type=jnp.float32)
        value = jnp.dot(
            latent.astype(jnp.bfloat16), absorb_ref[head], preferred_element_type=jnp.float32
        )
        values.append(value.astype(jnp.bfloat16))
    values = jnp.concatenate(values, axis=1)
    for at in range(0, width, TILE):
        term = jnp.dot(values, w_ref[:, at : at + TILE], preferred_element_type=jnp.float32)
        store_term(term, at, pieces)
    residual = residual_ref[...].astype(jnp.float32)
    pieces[0][:own_rows, :] = pieces[0][:own_rows, :] + residual


def project(joined, w_absorb, residual_in, w_out, rows, far):
    depth, width = w_out.shape
    own_rows = residual_in.shape[0]
    return pl.pallas_call(
        functools.partial(project_kernel, own_rows, far),
        out_shape=term_shapes(rows // (2 * PIECES), width),
        in_specs=[pl.BlockSpec(memory_space=pltpu.VMEM)] * 4,
        out_specs=(pl.BlockSpec(memory_space=pltpu.VMEM),) * (2 * PIECES),
        compiler_params=pltpu.CompilerParams(vmem_limit_bytes=24 * MIB),
        cost_estimate=pl.CostEstimate(
            flops=2 * rows * depth * width, bytes_accessed=2 * depth * width, transcendentals=0
        ),
        name="project",
    )(joined, residual_in, w_absorb, w_out)


def expert_kernel(*refs):
    streams, (gain_ref, gate_ref, up_ref, down_ref), pieces = refs[:8], refs[8:12], refs[12:]
    width = gain_ref.shape[1]
    depth = width // PARTS
    inverses = []
    for stream in streams:
        squares = 0.0
        for at in range(0, width, depth):
            piece = stream[:, at : at + depth].astype(jnp.float32)
            squares = squares + sum(lane_tiles(piece * piece))
        mean = jnp.sum(squares, axis=1, keepdims=True) / width
        inverses.append(lax.rsqrt(mean + 1e-06))
    gate, up = 0.0, 0.0
    for at in range(0, width, depth):
        gain = gain_ref[:, at : at + depth]
        tokens = jnp.concatenate(
            [
                stream[:, at : at + depth].astype(jnp.float32) * inverse * gain
                for stream, inverse in zip(streams, inverses)
            ],
            axis=0,
        ).astype(jnp.bfloat16)
        gate = gate + jnp.dot(
            tokens, gate_ref[at : at + depth, :], preferred_element_type=jnp.float32
        )
        up = up + jnp.dot(
            tokens, up_ref[at : at + depth, :], preferred_element_type=jnp.float32
        )
    active = (gate / (1.0 + jnp.exp(-gate)) * up).astype(jnp.bfloat16)
    for at in range(0, width, TILE):
        term = jnp.dot(active, down_ref[:, at : at + TILE], preferred_element_type=jnp.float32)
        store_term(term, at, pieces)


def run_expert(streams, norm_gain, w_gate, w_up, w_down):
    rows, width = streams[0].shape
    hidden = w_gate.shape[1]
    return pl.pallas_call(
        expert_kernel,
        out_shape=term_shapes(rows, width),
        in_specs=[pl.BlockSpec(memory_space=pltpu.VMEM)] * (2 * PIECES + 4),
        out_specs=(pl.BlockSpec(memory_space=pltpu.VMEM),) * (2 * PIECES),
        compiler_params=pltpu.CompilerParams(vmem_limit_bytes=24 * MIB),
        cost_estimate=pl.CostEstimate(
            flops=12 * PIECES * rows * hidden * width,
            bytes_accessed=6 * hidden * width,
            transcendentals=2 * PIECES * rows * hidden,
        ),
        name="expert",
    )(*streams, norm_gain[None], w_gate, w_up, w_down)


def swap(array, distance):
    pairs = [(at, at ^ distance) for at in range(lax.axis_size("experts"))]
    return lax.ppermute(array, "experts", pairs)


def wide(array):
    return array.astype(jnp.float32)


def collect(terms):
    keeps, sends = terms[:PIECES], terms[PIECES:]
    total = 0.0
    for piece in (1, 2, 3, 0):
        part = keeps[piece] + wide(swap(sends[piece], 1))
        if piece:
            part = wide(swap(part.astype(jnp.bfloat16), SQUARE[piece]))
        total = total + part
    return total


def exchange(total, far):
    own_rows = total.shape[0] // far
    sent = total.astype(jnp.bfloat16)
    for at in range(1, far):
        block = swap(sent, 8 * at)
        total = total + wide(
            jnp.concatenate(
                [block[(to ^ at) * own_rows : ((to ^ at) + 1) * own_rows] for to in range(far)]
            )
        )
    return total.astype(jnp.bfloat16)


def spread(stream):
    own = [swap(stream, distance) if distance else stream for distance in SQUARE]
    return own + [swap(piece, 1) for piece in own]


def shards(
    queries,
    cache,
    cache_len,
    residual_in,
    w_absorb,
    w_out,
    norm_gain,
    expert_ids,
    route_gates,
    w_gate,
    w_up,
    w_down,
):
    devices = lax.axis_size("experts")
    rank_here = lax.axis_index("experts")
    own_rows = queries.shape[0]
    all_rows = expert_ids.shape[0]
    far = devices // 8
    split_ways = FF // w_gate.shape[1]
    assert split_ways == 8

    latent = attend(queries, cache, cache_len, devices, w_absorb.shape[1])
    joined = lax.all_to_all(latent, "experts", split_axis=0, concat_axis=0, tiled=True)
    joined = joined.reshape(-1, joined.shape[-1])
    terms = project(joined, w_absorb, residual_in, w_out, all_rows, far)
    stream = exchange(collect(terms), far)
    attended = stream[:own_rows]

    terms = run_expert(spread(stream), norm_gain, w_gate, w_up, w_down)
    parts = [
        keep + wide(swap(send, 1)) for keep, send in zip(terms[:PIECES], terms[PIECES:])
    ]
    own_ids = lax.dynamic_slice_in_dim(expert_ids, rank_here * own_rows, own_rows, 0)
    sent = {
        distance + 8 * at: part[at * own_rows : (at + 1) * own_rows].astype(jnp.bfloat16)
        for at in reversed(range(far))
        for part, distance in zip(parts, SQUARE)
        if distance + at
    }
    order = list(reversed(sent))
    for earlier, later in zip(order, order[1:]):
        sent[later], sent[earlier] = lax.optimization_barrier((sent[later], sent[earlier]))
    expert_out = 0.0
    for at in reversed(range(far)):
        expert = (rank_here ^ (8 * at)) // split_ways
        mixing = jnp.sum(
            route_gates * (own_ids == expert).astype(jnp.float32), axis=1, keepdims=True
        )
        for part, distance in zip(parts, SQUARE):
            block = part[at * own_rows : (at + 1) * own_rows]
            if distance + at:
                block = wide(swap(sent[distance + 8 * at], distance + 8 * at))
            expert_out = expert_out + mixing * block
    return (attended, expert_out.astype(jnp.bfloat16))


def solution(mesh):
    placed = (
        P(("groups", "experts"), None, None),
        P(("groups", "experts"), None, None),
        P(("groups", "experts")),
        P(("groups", "experts"), None),
        P("experts", None, None),
        P("experts", None),
        P(),
        P("groups", None),
        P(("groups", "experts"), None),
        P(None, "experts"),
        P(None, "experts"),
        P("experts", None),
    )
    return jax.shard_map(
        shards,
        mesh=mesh,
        in_specs=placed,
        out_specs=(P(("groups", "experts"), None), P(("groups", "experts"), None)),
        check_vma=False,
    )
```

```python
import functools

import jax
import jax.numpy as jnp
from jax import lax
from jax.experimental import pallas as pl
from jax.experimental.pallas import tpu as pltpu
from jax.sharding import PartitionSpec as P

QK = 192
FF = 2048
BLOCK = 512
LOWEST = -3e38
GROUP = 4
LANES = 128
TILE = 256
PARTS = 4
SQUARE = (0, 6, 4, 2)
PIECES = len(SQUARE)
MIB = 2**20


def lane_tiles(array):
    return [array[:, at : at + LANES] for at in range(0, array.shape[1], LANES)]


def attend_kernel(
    len_ref,
    queries_ref,
    cache_ref,
    latent_ref,
    length,
    queries,
    held,
    summed,
    highest,
    sums,
    staged,
    item_row,
    item_block,
    length_arrived,
    queries_arrived,
    arrived,
):
    own_rows, heads, _ = queries.shape
    devices, _, rank = staged.shape
    own_heads = heads // devices
    blocks = held.shape[1]

    length_copy = pltpu.make_async_copy(len_ref, length, length_arrived)
    length_copy.start()
    queries_copy = pltpu.make_async_copy(queries_ref, queries, queries_arrived)
    queries_copy.start()

    def block_copy(row, block):
        return pltpu.make_async_copy(
            cache_ref.at[row, :, pl.ds(pl.multiple_of(block * BLOCK, BLOCK), BLOCK)],
            held.at[row, block],
            arrived.at[row, block],
        )

    for row in range(own_rows):
        block_copy(row, 0).start()
        item_row[row] = row
        item_block[row] = 0
    highest[...] = jnp.full_like(highest, LOWEST)
    sums[...] = jnp.zeros_like(sums)
    summed[...] = jnp.zeros_like(summed)
    length_copy.wait()
    items = own_rows
    for row in range(own_rows):
        count = (length[row] + BLOCK - 1) // BLOCK

        def begin(block, first, row=row):
            block_copy(row, block).start()
            item_row[first + block] = row
            item_block[first + block] = block
            return first

        lax.fori_loop(1, count, begin, items - 1)
        items = items + count - 1
    queries_copy.wait()
    column = lax.broadcasted_iota(jnp.int32, (heads, BLOCK), 1)

    def visit(first, many):
        inside = [(item_row[first + at], item_block[first + at]) for at in range(many)]
        for row, block in inside:
            block_copy(row, block).wait()
        found = []
        for row, block in inside:
            score = jnp.dot(
                queries[row], held[row, block], preferred_element_type=jnp.float32
            ) * QK ** (-0.5)
            found.append(
                jnp.where(column + block * BLOCK < length[row], score, -jnp.inf)
            )
        tops = [
            jnp.max(functools.reduce(jnp.maximum, lane_tiles(score)), axis=1, keepdims=True)
            for score in found
        ]
        weights = [jnp.exp(score - top) for score, top in zip(found, tops)]
        terms = [
            lax.dot_general(
                weight.astype(jnp.bfloat16),
                held[row, block, :rank, :],
                (((1,), (1,)), ((), ())),
                preferred_element_type=jnp.float32,
            )
            for (row, block), weight in zip(inside, weights)
        ]
        for (row, _), top, weight, term in zip(inside, tops, weights, terms):
            before = highest[row]
            after = jnp.maximum(before, top)
            old, new = jnp.exp(before - after), jnp.exp(top - after)
            highest[row] = after
            sums[row] = sums[row] * old + sum(lane_tiles(weight)) * new
            for at in range(0, rank, LANES):
                summed[row, :, at : at + LANES] = (
                    summed[row, :, at : at + LANES] * old + term[:, at : at + LANES] * new
                )

    def visit_group(group, _):
        visit(group * GROUP, GROUP)
        return 0

    whole = items // GROUP
    lax.fori_loop(0, whole, visit_group, 0)
    pl.when((items & 2) != 0)(lambda: visit(whole * GROUP, 2))
    pl.when((items & 1) != 0)(lambda: visit(items - 1, 1))
    for row in range(own_rows):
        latent = summed[row] * (1.0 / jnp.sum(sums[row], axis=1, keepdims=True))
        for device in range(devices):
            staged[device, row * own_heads : (row + 1) * own_heads, :] = latent[
                device * own_heads : (device + 1) * own_heads
            ]
    latent_ref[...] = staged[...].astype(latent_ref.dtype)


def attend(queries, cache, cache_len, devices, rank):
    own_rows, depth, heads = queries.shape
    blocks = cache.shape[2] // BLOCK
    packed = own_rows * heads // devices
    listed = own_rows * blocks
    return pl.pallas_call(
        attend_kernel,
        out_shape=jax.ShapeDtypeStruct((devices, packed, rank), jnp.bfloat16),
        in_specs=[pl.BlockSpec(memory_space=pl.ANY)] * 3,
        out_specs=pl.BlockSpec(memory_space=pltpu.VMEM),
        scratch_shapes=[
            pltpu.SMEM((own_rows,), jnp.int32),
            pltpu.VMEM((own_rows, heads, depth), jnp.bfloat16),
            pltpu.VMEM((own_rows, blocks, depth, BLOCK), jnp.bfloat16),
            pltpu.VMEM((own_rows, heads, rank), jnp.float32),
            pltpu.VMEM((own_rows, heads, LANES), jnp.float32),
            pltpu.VMEM((own_rows, heads, LANES), jnp.float32),
            pltpu.VMEM((devices, packed, rank), jnp.float32),
            pltpu.SMEM((listed,), jnp.int32),
            pltpu.SMEM((listed,), jnp.int32),
            pltpu.SemaphoreType.DMA,
            pltpu.SemaphoreType.DMA,
            pltpu.SemaphoreType.DMA((own_rows, blocks)),
        ],
        compiler_params=pltpu.CompilerParams(vmem_limit_bytes=55 * MIB),
        cost_estimate=pl.CostEstimate(
            flops=own_rows * heads * cache.shape[2] * (depth + rank),
            bytes_accessed=cache.size,
            transcendentals=own_rows * heads * cache.shape[2],
        ),
        name="attend",
    )(cache_len, jnp.swapaxes(queries, 1, 2), cache)


def store_term(term, at, refs):
    rows = term.shape[0] // len(refs)
    for piece, ref in enumerate(refs):
        ref[:, at : at + TILE] = term[piece * rows : (piece + 1) * rows].astype(ref.dtype)


def term_shapes(rows, width):
    return tuple(
        jax.ShapeDtypeStruct((rows, width), kind)
        for kind in (jnp.float32, jnp.bfloat16)
        for _ in range(PIECES)
    )


def project_kernel(own_rows, far, joined_ref, residual_ref, absorb_ref, w_ref, *pieces):
    own_heads = absorb_ref.shape[0]
    width = w_ref.shape[1]
    shape = (len(pieces) * pieces[0].shape[0], joined_ref.shape[0])
    row = lax.broadcasted_iota(jnp.int32, shape, 0)
    place = lax.broadcasted_iota(jnp.int32, shape, 1)
    turn = own_rows.bit_length() - 1
    far_bits = far.bit_length() - 1
    request, slot = row & (own_rows - 1), row >> turn
    far_at, slot = slot & (far - 1), slot >> far_bits
    distance = (far_at << 3) + ((4 - (slot & 3) & 3) << 1) + (slot >> 2)
    device = distance ^ lax.axis_index("experts")
    values = []
    for head in range(own_heads):
        wanted = ((device << turn) + request) * own_heads + head
        choice = (place == wanted).astype(jnp.float32).astype(jnp.bfloat16)
        latent = jnp.dot(choice, joined_ref[...], preferred_element_type=jnp.float32)
        value = jnp.dot(
            latent.astype(jnp.bfloat16), absorb_ref[head], preferred_element_type=jnp.float32
        )
        values.append(value.astype(jnp.bfloat16))
    values = jnp.concatenate(values, axis=1)
    for at in range(0, width, TILE):
        term = jnp.dot(values, w_ref[:, at : at + TILE], preferred_element_type=jnp.float32)
        store_term(term, at, pieces)
    residual = residual_ref[...].astype(jnp.float32)
    pieces[0][:own_rows, :] = pieces[0][:own_rows, :] + residual


def project(joined, w_absorb, residual_in, w_out, rows, far):
    depth, width = w_out.shape
    own_rows = residual_in.shape[0]
    return pl.pallas_call(
        functools.partial(project_kernel, own_rows, far),
        out_shape=term_shapes(rows // (2 * PIECES), width),
        in_specs=[pl.BlockSpec(memory_space=pltpu.VMEM)] * 4,
        out_specs=(pl.BlockSpec(memory_space=pltpu.VMEM),) * (2 * PIECES),
        compiler_params=pltpu.CompilerParams(vmem_limit_bytes=24 * MIB),
        cost_estimate=pl.CostEstimate(
            flops=2 * rows * depth * width, bytes_accessed=2 * depth * width, transcendentals=0
        ),
        name="project",
    )(joined, residual_in, w_absorb, w_out)


def expert_kernel(*refs):
    streams, (gain_ref, gate_ref, up_ref, down_ref), pieces = refs[:8], refs[8:12], refs[12:]
    width = gain_ref.shape[1]
    depth = width // PARTS
    inverses = []
    for stream in streams:
        squares = 0.0
        for at in range(0, width, depth):
            piece = stream[:, at : at + depth].astype(jnp.float32)
            squares = squares + sum(lane_tiles(piece * piece))
        mean = jnp.sum(squares, axis=1, keepdims=True) / width
        inverses.append(lax.rsqrt(mean + 1e-06))
    gate, up = 0.0, 0.0
    for at in range(0, width, depth):
        gain = gain_ref[:, at : at + depth]
        tokens = jnp.concatenate(
            [
                stream[:, at : at + depth].astype(jnp.float32) * inverse * gain
                for stream, inverse in zip(streams, inverses)
            ],
            axis=0,
        ).astype(jnp.bfloat16)
        gate = gate + jnp.dot(
            tokens, gate_ref[at : at + depth, :], preferred_element_type=jnp.float32
        )
        up = up + jnp.dot(
            tokens, up_ref[at : at + depth, :], preferred_element_type=jnp.float32
        )
    active = (gate / (1.0 + jnp.exp(-gate)) * up).astype(jnp.bfloat16)
    for at in range(0, width, TILE):
        term = jnp.dot(active, down_ref[:, at : at + TILE], preferred_element_type=jnp.float32)
        store_term(term, at, pieces)


def run_expert(streams, norm_gain, w_gate, w_up, w_down):
    rows, width = streams[0].shape
    hidden = w_gate.shape[1]
    return pl.pallas_call(
        expert_kernel,
        out_shape=term_shapes(rows, width),
        in_specs=[pl.BlockSpec(memory_space=pltpu.VMEM)] * (2 * PIECES + 4),
        out_specs=(pl.BlockSpec(memory_space=pltpu.VMEM),) * (2 * PIECES),
        compiler_params=pltpu.CompilerParams(vmem_limit_bytes=24 * MIB),
        cost_estimate=pl.CostEstimate(
            flops=12 * PIECES * rows * hidden * width,
            bytes_accessed=6 * hidden * width,
            transcendentals=2 * PIECES * rows * hidden,
        ),
        name="expert",
    )(*streams, norm_gain[None], w_gate, w_up, w_down)


def swap(array, distance):
    pairs = [(at, at ^ distance) for at in range(lax.axis_size("experts"))]
    return lax.ppermute(array, "experts", pairs)


def wide(array):
    return array.astype(jnp.float32)


def collect(terms):
    keeps, sends = terms[:PIECES], terms[PIECES:]
    total = 0.0
    for piece in (1, 2, 3, 0):
        part = keeps[piece] + wide(swap(sends[piece], 1))
        if piece:
            part = wide(swap(part.astype(jnp.bfloat16), SQUARE[piece]))
        total = total + part
    return total


def exchange(total, far):
    own_rows = total.shape[0] // far
    sent = total.astype(jnp.bfloat16)
    for at in range(1, far):
        block = swap(sent, 8 * at)
        total = total + wide(
            jnp.concatenate(
                [block[(to ^ at) * own_rows : ((to ^ at) + 1) * own_rows] for to in range(far)]
            )
        )
    return total.astype(jnp.bfloat16)


def spread(stream):
    own = [swap(stream, distance) if distance else stream for distance in SQUARE]
    return own + [swap(piece, 1) for piece in own]


def shards(
    queries,
    cache,
    cache_len,
    residual_in,
    w_absorb,
    w_out,
    norm_gain,
    expert_ids,
    route_gates,
    w_gate,
    w_up,
    w_down,
):
    devices = lax.axis_size("experts")
    rank_here = lax.axis_index("experts")
    own_rows = queries.shape[0]
    all_rows = expert_ids.shape[0]
    far = devices // 8
    split_ways = FF // w_gate.shape[1]
    assert split_ways == 8

    latent = attend(queries, cache, cache_len, devices, w_absorb.shape[1])
    joined = lax.all_to_all(latent, "experts", split_axis=0, concat_axis=0, tiled=True)
    joined = joined.reshape(-1, joined.shape[-1])
    terms = project(joined, w_absorb, residual_in, w_out, all_rows, far)
    stream = exchange(collect(terms), far)
    attended = stream[:own_rows]

    total = collect(run_expert(spread(stream), norm_gain, w_gate, w_up, w_down))
    own_ids = lax.dynamic_slice_in_dim(expert_ids, rank_here * own_rows, own_rows, 0)
    expert_out = 0.0
    for at in range(far):
        block = total[at * own_rows : (at + 1) * own_rows]
        block = wide(swap(block.astype(jnp.bfloat16), 8 * at)) if at else block
        expert = (rank_here ^ (8 * at)) // split_ways
        mixing = jnp.sum(
            route_gates * (own_ids == expert).astype(jnp.float32), axis=1, keepdims=True
        )
        expert_out = expert_out + mixing * block
    return (attended, expert_out.astype(jnp.bfloat16))


def solution(mesh):
    placed = (
        P(("groups", "experts"), None, None),
        P(("groups", "experts"), None, None),
        P(("groups", "experts")),
        P(("groups", "experts"), None),
        P("experts", None, None),
        P("experts", None),
        P(),
        P("groups", None),
        P(("groups", "experts"), None),
        P(None, "experts"),
        P(None, "experts"),
        P("experts", None),
    )
    return jax.shard_map(
        shards,
        mesh=mesh,
        in_specs=placed,
        out_specs=(P(("groups", "experts"), None), P(("groups", "experts"), None)),
        check_vma=False,
    )
```

```python
import functools

import jax
import jax.numpy as jnp
from jax import lax
from jax.experimental import pallas as pl
from jax.experimental.pallas import tpu as pltpu
from jax.sharding import PartitionSpec as P

QK = 192
FF = 2048
BLOCK = 512
LOWEST = -3e38
GROUP = 4
LANES = 128
TILE = 256
PARTS = 4
SQUARE = (0, 6, 4, 2)
PIECES = len(SQUARE)
SIDES = 2
MIB = 2**20


def lane_tiles(array):
    return [array[:, at : at + LANES] for at in range(0, array.shape[1], LANES)]


def attend_kernel(
    len_ref,
    queries_ref,
    cache_ref,
    latent_ref,
    length,
    queries,
    held,
    summed,
    highest,
    sums,
    staged,
    item_row,
    item_block,
    length_arrived,
    queries_arrived,
    arrived,
):
    own_rows, heads, _ = queries.shape
    devices, _, rank = staged.shape
    own_heads = heads // devices
    blocks = held.shape[1]

    length_copy = pltpu.make_async_copy(len_ref, length, length_arrived)
    length_copy.start()
    queries_copy = pltpu.make_async_copy(queries_ref, queries, queries_arrived)
    queries_copy.start()

    def block_copy(row, block):
        return pltpu.make_async_copy(
            cache_ref.at[row, :, pl.ds(pl.multiple_of(block * BLOCK, BLOCK), BLOCK)],
            held.at[row, block],
            arrived.at[row, block],
        )

    for row in range(own_rows):
        block_copy(row, 0).start()
        item_row[row] = row
        item_block[row] = 0
    highest[...] = jnp.full_like(highest, LOWEST)
    sums[...] = jnp.zeros_like(sums)
    summed[...] = jnp.zeros_like(summed)
    length_copy.wait()
    items = own_rows
    for row in range(own_rows):
        count = (length[row] + BLOCK - 1) // BLOCK

        def begin(block, first, row=row):
            block_copy(row, block).start()
            item_row[first + block] = row
            item_block[first + block] = block
            return first

        lax.fori_loop(1, count, begin, items - 1)
        items = items + count - 1
    queries_copy.wait()
    column = lax.broadcasted_iota(jnp.int32, (heads, BLOCK), 1)

    def visit(first, many):
        inside = [(item_row[first + at], item_block[first + at]) for at in range(many)]
        for row, block in inside:
            block_copy(row, block).wait()
        found = []
        for row, block in inside:
            score = jnp.dot(
                queries[row], held[row, block], preferred_element_type=jnp.float32
            ) * QK ** (-0.5)
            found.append(
                jnp.where(column + block * BLOCK < length[row], score, -jnp.inf)
            )
        tops = [
            jnp.max(functools.reduce(jnp.maximum, lane_tiles(score)), axis=1, keepdims=True)
            for score in found
        ]
        weights = [jnp.exp(score - top) for score, top in zip(found, tops)]
        terms = [
            lax.dot_general(
                weight.astype(jnp.bfloat16),
                held[row, block, :rank, :],
                (((1,), (1,)), ((), ())),
                preferred_element_type=jnp.float32,
            )
            for (row, block), weight in zip(inside, weights)
        ]
        for (row, _), top, weight, term in zip(inside, tops, weights, terms):
            before = highest[row]
            after = jnp.maximum(before, top)
            old, new = jnp.exp(before - after), jnp.exp(top - after)
            highest[row] = after
            sums[row] = sums[row] * old + sum(lane_tiles(weight)) * new
            for at in range(0, rank, LANES):
                summed[row, :, at : at + LANES] = (
                    summed[row, :, at : at + LANES] * old + term[:, at : at + LANES] * new
                )

    def visit_group(group, _):
        visit(group * GROUP, GROUP)
        return 0

    whole = items // GROUP
    lax.fori_loop(0, whole, visit_group, 0)
    pl.when((items & 2) != 0)(lambda: visit(whole * GROUP, 2))
    pl.when((items & 1) != 0)(lambda: visit(items - 1, 1))
    for row in range(own_rows):
        latent = summed[row] * (1.0 / jnp.sum(sums[row], axis=1, keepdims=True))
        for device in range(devices):
            staged[device, row * own_heads : (row + 1) * own_heads, :] = latent[
                device * own_heads : (device + 1) * own_heads
            ]
    latent_ref[...] = staged[...].astype(latent_ref.dtype)


def attend(queries, cache, cache_len, devices, rank):
    own_rows, depth, heads = queries.shape
    blocks = cache.shape[2] // BLOCK
    packed = own_rows * heads // devices
    listed = own_rows * blocks
    return pl.pallas_call(
        attend_kernel,
        out_shape=jax.ShapeDtypeStruct((devices, packed, rank), jnp.bfloat16),
        in_specs=[pl.BlockSpec(memory_space=pl.ANY)] * 3,
        out_specs=pl.BlockSpec(memory_space=pltpu.VMEM),
        scratch_shapes=[
            pltpu.SMEM((own_rows,), jnp.int32),
            pltpu.VMEM((own_rows, heads, depth), jnp.bfloat16),
            pltpu.VMEM((own_rows, blocks, depth, BLOCK), jnp.bfloat16),
            pltpu.VMEM((own_rows, heads, rank), jnp.float32),
            pltpu.VMEM((own_rows, heads, LANES), jnp.float32),
            pltpu.VMEM((own_rows, heads, LANES), jnp.float32),
            pltpu.VMEM((devices, packed, rank), jnp.float32),
            pltpu.SMEM((listed,), jnp.int32),
            pltpu.SMEM((listed,), jnp.int32),
            pltpu.SemaphoreType.DMA,
            pltpu.SemaphoreType.DMA,
            pltpu.SemaphoreType.DMA((own_rows, blocks)),
        ],
        compiler_params=pltpu.CompilerParams(vmem_limit_bytes=55 * MIB),
        cost_estimate=pl.CostEstimate(
            flops=own_rows * heads * cache.shape[2] * (depth + rank),
            bytes_accessed=cache.size,
            transcendentals=own_rows * heads * cache.shape[2],
        ),
        name="attend",
    )(cache_len, jnp.swapaxes(queries, 1, 2), cache)


def store_term(term, at, refs):
    rows = term.shape[0] // len(refs)
    for piece, ref in enumerate(refs):
        ref[:, at : at + TILE] = term[piece * rows : (piece + 1) * rows].astype(ref.dtype)


def term_shapes(rows, width):
    return tuple(
        jax.ShapeDtypeStruct((rows, width), kind)
        for kind in (jnp.float32, jnp.bfloat16)
        for _ in range(PIECES)
    )


def project_kernel(own_rows, far, joined_ref, residual_ref, absorb_ref, w_ref, *pieces):
    own_heads = absorb_ref.shape[0]
    width = w_ref.shape[1]
    shape = (len(pieces) * pieces[0].shape[0], joined_ref.shape[0])
    row = lax.broadcasted_iota(jnp.int32, shape, 0)
    place = lax.broadcasted_iota(jnp.int32, shape, 1)
    turn = own_rows.bit_length() - 1
    far_bits = far.bit_length() - 1
    request, slot = row & (own_rows - 1), row >> turn
    far_at, slot = slot & (far - 1), slot >> far_bits
    distance = (far_at << 3) + ((4 - (slot & 3) & 3) << 1) + (slot >> 2)
    device = distance ^ lax.axis_index("experts")
    choices = []
    for head in range(own_heads):
        wanted = ((device << turn) + request) * own_heads + head
        choices.append((place == wanted).astype(jnp.float32))
    latents = jnp.dot(
        jnp.concatenate(choices, axis=0).astype(jnp.bfloat16),
        joined_ref[...],
        preferred_element_type=jnp.float32,
    ).astype(jnp.bfloat16)
    values = [
        jnp.dot(
            latents[head * shape[0] : (head + 1) * shape[0]],
            absorb_ref[head],
            preferred_element_type=jnp.float32,
        ).astype(jnp.bfloat16)
        for head in range(own_heads)
    ]
    values = jnp.concatenate(values, axis=1)
    for at in range(0, width, TILE):
        term = jnp.dot(values, w_ref[:, at : at + TILE], preferred_element_type=jnp.float32)
        store_term(term, at, pieces)
    residual = residual_ref[...].astype(jnp.float32)
    pieces[0][:own_rows, :] = pieces[0][:own_rows, :] + residual


def project(joined, w_absorb, residual_in, w_out, rows, far):
    depth, width = w_out.shape
    own_rows = residual_in.shape[0]
    return pl.pallas_call(
        functools.partial(project_kernel, own_rows, far),
        out_shape=term_shapes(rows // (2 * PIECES), width),
        in_specs=[pl.BlockSpec(memory_space=pltpu.VMEM)] * 4,
        out_specs=(pl.BlockSpec(memory_space=pltpu.VMEM),) * (2 * PIECES),
        compiler_params=pltpu.CompilerParams(vmem_limit_bytes=24 * MIB),
        cost_estimate=pl.CostEstimate(
            flops=2 * rows * depth * width, bytes_accessed=2 * depth * width, transcendentals=0
        ),
        name="project",
    )(joined, residual_in, w_absorb, w_out)


def expert_kernel(*refs):
    count = 2 * PIECES * SIDES
    streams, (gain_ref, gate_ref, up_ref, down_ref) = refs[:count], refs[count : count + 4]
    pieces = refs[count + 4 :]
    streams = [streams[at :: 2 * PIECES] for at in range(2 * PIECES)]
    width = gain_ref.shape[1]
    side = width // SIDES
    depth = width // PARTS
    inverses = []
    for stream in streams:
        squares = 0.0
        for ref in stream:
            for at in range(0, side, depth):
                piece = ref[:, at : at + depth].astype(jnp.float32)
                squares = squares + sum(lane_tiles(piece * piece))
        mean = jnp.sum(squares, axis=1, keepdims=True) / width
        inverses.append(lax.rsqrt(mean + 1e-06))
    gate, up = 0.0, 0.0
    for at in range(0, width, depth):
        gain = gain_ref[:, at : at + depth]
        place = at % side
        tokens = jnp.concatenate(
            [
                stream[at // side][:, place : place + depth].astype(jnp.float32)
                * inverse
                * gain
                for stream, inverse in zip(streams, inverses)
            ],
            axis=0,
        ).astype(jnp.bfloat16)
        gate = gate + jnp.dot(
            tokens, gate_ref[at : at + depth, :], preferred_element_type=jnp.float32
        )
        up = up + jnp.dot(
            tokens, up_ref[at : at + depth, :], preferred_element_type=jnp.float32
        )
    active = (gate / (1.0 + jnp.exp(-gate)) * up).astype(jnp.bfloat16)
    for at in range(0, width, TILE):
        term = jnp.dot(active, down_ref[:, at : at + TILE], preferred_element_type=jnp.float32)
        store_term(term, at, pieces)


def run_expert(streams, norm_gain, w_gate, w_up, w_down):
    rows = streams[0].shape[0]
    width, hidden = w_gate.shape
    return pl.pallas_call(
        expert_kernel,
        out_shape=term_shapes(rows, width),
        in_specs=[pl.BlockSpec(memory_space=pltpu.VMEM)] * (2 * PIECES * SIDES + 4),
        out_specs=(pl.BlockSpec(memory_space=pltpu.VMEM),) * (2 * PIECES),
        compiler_params=pltpu.CompilerParams(vmem_limit_bytes=24 * MIB),
        cost_estimate=pl.CostEstimate(
            flops=12 * PIECES * rows * hidden * width,
            bytes_accessed=6 * hidden * width,
            transcendentals=2 * PIECES * rows * hidden,
        ),
        name="expert",
    )(*streams, norm_gain[None], w_gate, w_up, w_down)


def swap(array, distance):
    pairs = [(at, at ^ distance) for at in range(lax.axis_size("experts"))]
    return lax.ppermute(array, "experts", pairs)


def wide(array):
    return array.astype(jnp.float32)


def collect(terms):
    keeps, sends = terms[:PIECES], terms[PIECES:]
    total = 0.0
    for piece in (1, 2, 3, 0):
        part = keeps[piece] + wide(swap(sends[piece], 1))
        if piece:
            part = wide(swap(part.astype(jnp.bfloat16), SQUARE[piece]))
        total = total + part
    return total


def exchange(total, far):
    own_rows = total.shape[0] // far
    sent = total.astype(jnp.bfloat16)
    for at in range(1, far):
        block = swap(sent, 8 * at)
        total = total + wide(
            jnp.concatenate(
                [block[(to ^ at) * own_rows : ((to ^ at) + 1) * own_rows] for to in range(far)]
            )
        )
    return total.astype(jnp.bfloat16)


def spread(stream):
    own = [swap(stream, distance) if distance else stream for distance in SQUARE]
    return own + [swap(piece, 1) for piece in own]


def shards(
    queries,
    cache,
    cache_len,
    residual_in,
    w_absorb,
    w_out,
    norm_gain,
    expert_ids,
    route_gates,
    w_gate,
    w_up,
    w_down,
):
    devices = lax.axis_size("experts")
    rank_here = lax.axis_index("experts")
    own_rows = queries.shape[0]
    all_rows = expert_ids.shape[0]
    far = devices // 8
    split_ways = FF // w_gate.shape[1]
    assert split_ways == 8

    latent = attend(queries, cache, cache_len, devices, w_absorb.shape[1])
    joined = lax.all_to_all(latent, "experts", split_axis=0, concat_axis=0, tiled=True)
    joined = joined.reshape(-1, joined.shape[-1])
    terms = project(joined, w_absorb, residual_in, w_out, all_rows, far)
    total = collect(terms)
    side = total.shape[1] // SIDES
    totals = lax.optimization_barrier(
        [total[:, at * side : (at + 1) * side] for at in range(SIDES)]
    )
    attended, streams = [], []
    for total in totals:
        stream = exchange(total, far)
        attended.append(stream[:own_rows])
        streams.extend(spread(stream))
    attended = jnp.concatenate(attended, axis=1)

    total = collect(run_expert(streams, norm_gain, w_gate, w_up, w_down))
    own_ids = lax.dynamic_slice_in_dim(expert_ids, rank_here * own_rows, own_rows, 0)
    expert_out = 0.0
    for at in range(far):
        block = total[at * own_rows : (at + 1) * own_rows]
        block = wide(swap(block.astype(jnp.bfloat16), 8 * at)) if at else block
        expert = (rank_here ^ (8 * at)) // split_ways
        mixing = jnp.sum(
            route_gates * (own_ids == expert).astype(jnp.float32), axis=1, keepdims=True
        )
        expert_out = expert_out + mixing * block
    return (attended, expert_out.astype(jnp.bfloat16))


def solution(mesh):
    placed = (
        P(("groups", "experts"), None, None),
        P(("groups", "experts"), None, None),
        P(("groups", "experts")),
        P(("groups", "experts"), None),
        P("experts", None, None),
        P("experts", None),
        P(),
        P("groups", None),
        P(("groups", "experts"), None),
        P(None, "experts"),
        P(None, "experts"),
        P("experts", None),
    )
    return jax.shard_map(
        shards,
        mesh=mesh,
        in_specs=placed,
        out_specs=(P(("groups", "experts"), None), P(("groups", "experts"), None)),
        check_vma=False,
    )
```

```python
import functools

import jax
import jax.numpy as jnp
from jax import lax
from jax.experimental import pallas as pl
from jax.experimental.pallas import tpu as pltpu
from jax.sharding import PartitionSpec as P

QK = 192
FF = 2048
BLOCK = 512
GROUP = 4
LANES = 128
TILE = 256
PARTS = 4
SQUARE = (0, 6, 4, 2)
PIECES = len(SQUARE)
MIB = 2**20


def lane_tiles(array):
    return [array[:, at : at + LANES] for at in range(0, array.shape[1], LANES)]


def attend_kernel(
    len_ref,
    queries_ref,
    cache_ref,
    latent_ref,
    length,
    queries,
    held,
    summed,
    highest,
    sums,
    staged,
    item_row,
    item_block,
    length_arrived,
    queries_arrived,
    arrived,
):
    own_rows, heads, _ = queries.shape
    devices, _, rank = staged.shape
    own_heads = heads // devices
    blocks = held.shape[1]

    length_copy = pltpu.make_async_copy(len_ref, length, length_arrived)
    length_copy.start()
    queries_copy = pltpu.make_async_copy(queries_ref, queries, queries_arrived)
    queries_copy.start()

    def block_copy(row, block):
        return pltpu.make_async_copy(
            cache_ref.at[row, :, pl.ds(pl.multiple_of(block * BLOCK, BLOCK), BLOCK)],
            held.at[row, block],
            arrived.at[row, block],
        )

    for row in range(own_rows):
        block_copy(row, 0).start()
        item_row[row] = row
        item_block[row] = 0
    length_copy.wait()
    items = own_rows
    for row in range(own_rows):
        count = (length[row] + BLOCK - 1) // BLOCK

        def begin(block, first, row=row):
            block_copy(row, block).start()
            item_row[first + block] = row
            item_block[first + block] = block
            return first

        lax.fori_loop(1, count, begin, items - 1)
        items = items + count - 1
    queries_copy.wait()
    column = lax.broadcasted_iota(jnp.int32, (heads, BLOCK), 1)

    def visit(inside, new):
        found = []
        for row, block in inside:
            if new:
                block_copy(row, block).wait()
            score = jnp.dot(
                queries[row], held[row, block], preferred_element_type=jnp.float32
            ) * QK ** (-0.5)
            found.append(
                jnp.where(column + block * BLOCK < length[row], score, -jnp.inf)
            )
        tops = [
            jnp.max(functools.reduce(jnp.maximum, lane_tiles(score)), axis=1, keepdims=True)
            for score in found
        ]
        weights = [jnp.exp(score - top) for score, top in zip(found, tops)]
        terms = [
            lax.dot_general(
                weight.astype(jnp.bfloat16),
                held[row, block, :rank, :],
                (((1,), (1,)), ((), ())),
                preferred_element_type=jnp.float32,
            )
            for (row, block), weight in zip(inside, weights)
        ]
        for (row, _), top, weight, term in zip(inside, tops, weights, terms):
            if new:
                highest[row] = jnp.broadcast_to(top, (heads, LANES))
                sums[row] = sum(lane_tiles(weight))
                summed[row] = term
                continue
            before = highest[row]
            after = jnp.maximum(before, top)
            ours, theirs = jnp.exp(before - after), jnp.exp(top - after)
            highest[row] = after
            sums[row] = sums[row] * ours + sum(lane_tiles(weight)) * theirs
            for at in range(0, rank, LANES):
                summed[row, :, at : at + LANES] = (
                    summed[row, :, at : at + LANES] * ours
                    + term[:, at : at + LANES] * theirs
                )

    def visit_items(first, many):
        inside = [(item_row[first + at], item_block[first + at]) for at in range(many)]
        for row, block in inside:
            block_copy(row, block).wait()
        visit(inside, False)

    def visit_group(group, _):
        visit_items(own_rows + group * GROUP, GROUP)
        return 0

    visit([(row, 0) for row in range(own_rows)], True)
    rest = items - own_rows
    whole = rest // GROUP
    lax.fori_loop(0, whole, visit_group, 0)
    pl.when((rest & 2) != 0)(lambda: visit_items(own_rows + whole * GROUP, 2))
    pl.when((rest & 1) != 0)(lambda: visit_items(items - 1, 1))
    for row in range(own_rows):
        latent = summed[row] * (1.0 / jnp.sum(sums[row], axis=1, keepdims=True))
        for device in range(devices):
            staged[device, row * own_heads : (row + 1) * own_heads, :] = latent[
                device * own_heads : (device + 1) * own_heads
            ]
    latent_ref[...] = staged[...].astype(latent_ref.dtype)


def attend(queries, cache, cache_len, devices, rank):
    own_rows, depth, heads = queries.shape
    blocks = cache.shape[2] // BLOCK
    packed = own_rows * heads // devices
    listed = own_rows * blocks
    return pl.pallas_call(
        attend_kernel,
        out_shape=jax.ShapeDtypeStruct((devices, packed, rank), jnp.bfloat16),
        in_specs=[pl.BlockSpec(memory_space=pl.ANY)] * 3,
        out_specs=pl.BlockSpec(memory_space=pltpu.VMEM),
        scratch_shapes=[
            pltpu.SMEM((own_rows,), jnp.int32),
            pltpu.VMEM((own_rows, heads, depth), jnp.bfloat16),
            pltpu.VMEM((own_rows, blocks, depth, BLOCK), jnp.bfloat16),
            pltpu.VMEM((own_rows, heads, rank), jnp.float32),
            pltpu.VMEM((own_rows, heads, LANES), jnp.float32),
            pltpu.VMEM((own_rows, heads, LANES), jnp.float32),
            pltpu.VMEM((devices, packed, rank), jnp.float32),
            pltpu.SMEM((listed,), jnp.int32),
            pltpu.SMEM((listed,), jnp.int32),
            pltpu.SemaphoreType.DMA,
            pltpu.SemaphoreType.DMA,
            pltpu.SemaphoreType.DMA((own_rows, blocks)),
        ],
        compiler_params=pltpu.CompilerParams(vmem_limit_bytes=55 * MIB),
        cost_estimate=pl.CostEstimate(
            flops=own_rows * heads * cache.shape[2] * (depth + rank),
            bytes_accessed=cache.size,
            transcendentals=own_rows * heads * cache.shape[2],
        ),
        name="attend",
    )(cache_len, jnp.swapaxes(queries, 1, 2), cache)


def store_term(term, at, refs):
    rows = term.shape[0] // len(refs)
    for piece, ref in enumerate(refs):
        ref[:, at : at + TILE] = term[piece * rows : (piece + 1) * rows].astype(ref.dtype)


def term_shapes(rows, width):
    return tuple(
        jax.ShapeDtypeStruct((rows, width), kind)
        for kind in (jnp.float32, jnp.bfloat16)
        for _ in range(PIECES)
    )


def project_kernel(own_rows, far, joined_ref, residual_ref, absorb_ref, w_ref, *pieces):
    own_heads = absorb_ref.shape[0]
    width = w_ref.shape[1]
    shape = (len(pieces) * pieces[0].shape[0], joined_ref.shape[0])
    row = lax.broadcasted_iota(jnp.int32, shape, 0)
    place = lax.broadcasted_iota(jnp.int32, shape, 1)
    turn = own_rows.bit_length() - 1
    far_bits = far.bit_length() - 1
    request, slot = row & (own_rows - 1), row >> turn
    far_at, slot = slot & (far - 1), slot >> far_bits
    distance = (far_at << 3) + ((4 - (slot & 3) & 3) << 1) + (slot >> 2)
    device = distance ^ lax.axis_index("experts")
    choices = []
    for head in range(own_heads):
        wanted = ((device << turn) + request) * own_heads + head
        choices.append((place == wanted).astype(jnp.float32))
    latents = jnp.dot(
        jnp.concatenate(choices, axis=0).astype(jnp.bfloat16),
        joined_ref[...],
        preferred_element_type=jnp.float32,
    ).astype(jnp.bfloat16)
    values = [
        jnp.dot(
            latents[head * shape[0] : (head + 1) * shape[0]],
            absorb_ref[head],
            preferred_element_type=jnp.float32,
        ).astype(jnp.bfloat16)
        for head in range(own_heads)
    ]
    values = jnp.concatenate(values, axis=1)
    for at in range(0, width, TILE):
        term = jnp.dot(values, w_ref[:, at : at + TILE], preferred_element_type=jnp.float32)
        store_term(term, at, pieces)
    residual = residual_ref[...].astype(jnp.float32)
    pieces[0][:own_rows, :] = pieces[0][:own_rows, :] + residual


def project(joined, w_absorb, residual_in, w_out, rows, far):
    depth, width = w_out.shape
    own_rows = residual_in.shape[0]
    return pl.pallas_call(
        functools.partial(project_kernel, own_rows, far),
        out_shape=term_shapes(rows // (2 * PIECES), width),
        in_specs=[pl.BlockSpec(memory_space=pltpu.VMEM)] * 4,
        out_specs=(pl.BlockSpec(memory_space=pltpu.VMEM),) * (2 * PIECES),
        compiler_params=pltpu.CompilerParams(vmem_limit_bytes=24 * MIB),
        cost_estimate=pl.CostEstimate(
            flops=2 * rows * depth * width, bytes_accessed=2 * depth * width, transcendentals=0
        ),
        name="project",
    )(joined, residual_in, w_absorb, w_out)


def expert_kernel(*refs):
    streams, (gain_ref, gate_ref, up_ref, down_ref), pieces = refs[:8], refs[8:12], refs[12:]
    width = gain_ref.shape[1]
    depth = width // PARTS
    inverses = []
    for stream in streams:
        squares = 0.0
        for at in range(0, width, depth):
            piece = stream[:, at : at + depth].astype(jnp.float32)
            squares = squares + sum(lane_tiles(piece * piece))
        mean = jnp.sum(squares, axis=1, keepdims=True) / width
        inverses.append(lax.rsqrt(mean + 1e-06))
    gate, up = 0.0, 0.0
    for at in range(0, width, depth):
        gain = gain_ref[:, at : at + depth]
        tokens = jnp.concatenate(
            [
                stream[:, at : at + depth].astype(jnp.float32) * inverse * gain
                for stream, inverse in zip(streams, inverses)
            ],
            axis=0,
        ).astype(jnp.bfloat16)
        gate = gate + jnp.dot(
            tokens, gate_ref[at : at + depth, :], preferred_element_type=jnp.float32
        )
        up = up + jnp.dot(
            tokens, up_ref[at : at + depth, :], preferred_element_type=jnp.float32
        )
    active = (gate / (1.0 + jnp.exp(-gate)) * up).astype(jnp.bfloat16)
    for at in range(0, width, TILE):
        term = jnp.dot(active, down_ref[:, at : at + TILE], preferred_element_type=jnp.float32)
        store_term(term, at, pieces)


def run_expert(streams, norm_gain, w_gate, w_up, w_down):
    rows, width = streams[0].shape
    hidden = w_gate.shape[1]
    return pl.pallas_call(
        expert_kernel,
        out_shape=term_shapes(rows, width),
        in_specs=[pl.BlockSpec(memory_space=pltpu.VMEM)] * (2 * PIECES + 4),
        out_specs=(pl.BlockSpec(memory_space=pltpu.VMEM),) * (2 * PIECES),
        compiler_params=pltpu.CompilerParams(vmem_limit_bytes=24 * MIB),
        cost_estimate=pl.CostEstimate(
            flops=12 * PIECES * rows * hidden * width,
            bytes_accessed=6 * hidden * width,
            transcendentals=2 * PIECES * rows * hidden,
        ),
        name="expert",
    )(*streams, norm_gain[None], w_gate, w_up, w_down)


def swap(array, distance):
    pairs = [(at, at ^ distance) for at in range(lax.axis_size("experts"))]
    return lax.ppermute(array, "experts", pairs)


def wide(array):
    return array.astype(jnp.float32)


def collect(terms):
    keeps, sends = terms[:PIECES], terms[PIECES:]
    total = 0.0
    for piece in (1, 2, 3, 0):
        part = keeps[piece] + wide(swap(sends[piece], 1))
        if piece:
            part = wide(swap(part.astype(jnp.bfloat16), SQUARE[piece]))
        total = total + part
    return total


def exchange(total, far):
    own_rows = total.shape[0] // far
    sent = total.astype(jnp.bfloat16)
    for at in range(1, far):
        block = swap(sent, 8 * at)
        total = total + wide(
            jnp.concatenate(
                [block[(to ^ at) * own_rows : ((to ^ at) + 1) * own_rows] for to in range(far)]
            )
        )
    return total.astype(jnp.bfloat16)


def spread(stream):
    own = [swap(stream, distance) if distance else stream for distance in SQUARE]
    return own + [swap(piece, 1) for piece in own]


def shards(
    queries,
    cache,
    cache_len,
    residual_in,
    w_absorb,
    w_out,
    norm_gain,
    expert_ids,
    route_gates,
    w_gate,
    w_up,
    w_down,
):
    devices = lax.axis_size("experts")
    rank_here = lax.axis_index("experts")
    own_rows = queries.shape[0]
    all_rows = expert_ids.shape[0]
    far = devices // 8
    split_ways = FF // w_gate.shape[1]
    assert split_ways == 8

    latent = attend(queries, cache, cache_len, devices, w_absorb.shape[1])
    joined = lax.all_to_all(latent, "experts", split_axis=0, concat_axis=0, tiled=True)
    joined = joined.reshape(-1, joined.shape[-1])
    terms = project(joined, w_absorb, residual_in, w_out, all_rows, far)
    stream = exchange(collect(terms), far)
    attended = stream[:own_rows]

    total = collect(run_expert(spread(stream), norm_gain, w_gate, w_up, w_down))
    own_ids = lax.dynamic_slice_in_dim(expert_ids, rank_here * own_rows, own_rows, 0)
    expert_out = 0.0
    for at in range(far):
        block = total[at * own_rows : (at + 1) * own_rows]
        block = wide(swap(block.astype(jnp.bfloat16), 8 * at)) if at else block
        expert = (rank_here ^ (8 * at)) // split_ways
        mixing = jnp.sum(
            route_gates * (own_ids == expert).astype(jnp.float32), axis=1, keepdims=True
        )
        expert_out = expert_out + mixing * block
    return (attended, expert_out.astype(jnp.bfloat16))


def solution(mesh):
    placed = (
        P(("groups", "experts"), None, None),
        P(("groups", "experts"), None, None),
        P(("groups", "experts")),
        P(("groups", "experts"), None),
        P("experts", None, None),
        P("experts", None),
        P(),
        P("groups", None),
        P(("groups", "experts"), None),
        P(None, "experts"),
        P(None, "experts"),
        P("experts", None),
    )
    return jax.shard_map(
        shards,
        mesh=mesh,
        in_specs=placed,
        out_specs=(P(("groups", "experts"), None), P(("groups", "experts"), None)),
        check_vma=False,
    )
```

```python
import functools

import jax
import jax.numpy as jnp
from jax import lax
from jax.experimental import pallas as pl
from jax.experimental.pallas import tpu as pltpu
from jax.sharding import PartitionSpec as P

QK = 192
FF = 2048
BLOCK = 512
LOWEST = -3e38
GROUP = 4
LANES = 128
TILE = 256
PARTS = 4
SQUARE = (6, 4, 2, 0)
PIECES = len(SQUARE)
MIB = 2**20


def lane_tiles(array):
    return [array[:, at : at + LANES] for at in range(0, array.shape[1], LANES)]


def attend_kernel(
    len_ref,
    queries_ref,
    cache_ref,
    latent_ref,
    length,
    queries,
    held,
    summed,
    highest,
    sums,
    staged,
    item_row,
    item_block,
    length_arrived,
    queries_arrived,
    arrived,
):
    own_rows, heads, _ = queries.shape
    devices, _, rank = staged.shape
    own_heads = heads // devices
    blocks = held.shape[1]

    length_copy = pltpu.make_async_copy(len_ref, length, length_arrived)
    length_copy.start()
    queries_copy = pltpu.make_async_copy(queries_ref, queries, queries_arrived)
    queries_copy.start()

    def block_copy(row, block):
        return pltpu.make_async_copy(
            cache_ref.at[row, :, pl.ds(pl.multiple_of(block * BLOCK, BLOCK), BLOCK)],
            held.at[row, block],
            arrived.at[row, block],
        )

    for row in range(own_rows):
        block_copy(row, 0).start()
        item_row[row] = row
        item_block[row] = 0
    highest[...] = jnp.full_like(highest, LOWEST)
    sums[...] = jnp.zeros_like(sums)
    summed[...] = jnp.zeros_like(summed)
    length_copy.wait()
    items = own_rows
    for row in range(own_rows):
        count = (length[row] + BLOCK - 1) // BLOCK

        def begin(block, first, row=row):
            block_copy(row, block).start()
            item_row[first + block] = row
            item_block[first + block] = block
            return first

        lax.fori_loop(1, count, begin, items - 1)
        items = items + count - 1
    queries_copy.wait()
    column = lax.broadcasted_iota(jnp.int32, (heads, BLOCK), 1)

    def visit(first, many):
        inside = [(item_row[first + at], item_block[first + at]) for at in range(many)]
        for row, block in inside:
            block_copy(row, block).wait()
        found = []
        for row, block in inside:
            score = jnp.dot(
                queries[row], held[row, block], preferred_element_type=jnp.float32
            ) * QK ** (-0.5)
            found.append(
                jnp.where(column + block * BLOCK < length[row], score, -jnp.inf)
            )
        tops = [
            jnp.max(functools.reduce(jnp.maximum, lane_tiles(score)), axis=1, keepdims=True)
            for score in found
        ]
        weights = [jnp.exp(score - top) for score, top in zip(found, tops)]
        terms = [
            lax.dot_general(
                weight.astype(jnp.bfloat16),
                held[row, block, :rank, :],
                (((1,), (1,)), ((), ())),
                preferred_element_type=jnp.float32,
            )
            for (row, block), weight in zip(inside, weights)
        ]
        for (row, _), top, weight, term in zip(inside, tops, weights, terms):
            before = highest[row]
            after = jnp.maximum(before, top)
            old, new = jnp.exp(before - after), jnp.exp(top - after)
            highest[row] = after
            sums[row] = sums[row] * old + sum(lane_tiles(weight)) * new
            for at in range(0, rank, LANES):
                summed[row, :, at : at + LANES] = (
                    summed[row, :, at : at + LANES] * old + term[:, at : at + LANES] * new
                )

    def visit_group(group, _):
        visit(group * GROUP, GROUP)
        return 0

    whole = items // GROUP
    lax.fori_loop(0, whole, visit_group, 0)
    pl.when((items & 2) != 0)(lambda: visit(whole * GROUP, 2))
    pl.when((items & 1) != 0)(lambda: visit(items - 1, 1))
    for row in range(own_rows):
        latent = summed[row] * (1.0 / jnp.sum(sums[row], axis=1, keepdims=True))
        for device in range(devices):
            staged[device, row * own_heads : (row + 1) * own_heads, :] = latent[
                device * own_heads : (device + 1) * own_heads
            ]
    latent_ref[...] = staged[...].astype(latent_ref.dtype)


def attend(queries, cache, cache_len, devices, rank):
    own_rows, depth, heads = queries.shape
    blocks = cache.shape[2] // BLOCK
    packed = own_rows * heads // devices
    listed = own_rows * blocks
    return pl.pallas_call(
        attend_kernel,
        out_shape=jax.ShapeDtypeStruct((devices, packed, rank), jnp.bfloat16),
        in_specs=[pl.BlockSpec(memory_space=pl.ANY)] * 3,
        out_specs=pl.BlockSpec(memory_space=pltpu.VMEM),
        scratch_shapes=[
            pltpu.SMEM((own_rows,), jnp.int32),
            pltpu.VMEM((own_rows, heads, depth), jnp.bfloat16),
            pltpu.VMEM((own_rows, blocks, depth, BLOCK), jnp.bfloat16),
            pltpu.VMEM((own_rows, heads, rank), jnp.float32),
            pltpu.VMEM((own_rows, heads, LANES), jnp.float32),
            pltpu.VMEM((own_rows, heads, LANES), jnp.float32),
            pltpu.VMEM((devices, packed, rank), jnp.float32),
            pltpu.SMEM((listed,), jnp.int32),
            pltpu.SMEM((listed,), jnp.int32),
            pltpu.SemaphoreType.DMA,
            pltpu.SemaphoreType.DMA,
            pltpu.SemaphoreType.DMA((own_rows, blocks)),
        ],
        compiler_params=pltpu.CompilerParams(vmem_limit_bytes=55 * MIB),
        cost_estimate=pl.CostEstimate(
            flops=own_rows * heads * cache.shape[2] * (depth + rank),
            bytes_accessed=cache.size,
            transcendentals=own_rows * heads * cache.shape[2],
        ),
        name="attend",
    )(cache_len, jnp.swapaxes(queries, 1, 2), cache)


def store_term(term, at, refs):
    first = 0
    for ref in refs:
        rows = ref.shape[0]
        ref[:, at : at + TILE] = term[first : first + rows].astype(ref.dtype)
        first += rows


def term_shapes(rows, width):
    kept = [jax.ShapeDtypeStruct((rows, width), jnp.float32)] * PIECES
    sent = [jax.ShapeDtypeStruct((many * rows, width), jnp.bfloat16) for many in (1, PIECES - 1)]
    return kept + sent


def project_kernel(own_rows, far, joined_ref, residual_ref, absorb_ref, w_ref, *pieces):
    own_heads = absorb_ref.shape[0]
    width = w_ref.shape[1]
    shape = (2 * PIECES * pieces[0].shape[0], joined_ref.shape[0])
    row = lax.broadcasted_iota(jnp.int32, shape, 0)
    place = lax.broadcasted_iota(jnp.int32, shape, 1)
    turn = own_rows.bit_length() - 1
    far_bits = far.bit_length() - 1
    request, slot = row & (own_rows - 1), row >> turn
    far_at, slot = slot & (far - 1), slot >> far_bits
    distance = (far_at << 3) + ((3 - (slot & 3)) << 1) + (slot >> 2)
    device = distance ^ lax.axis_index("experts")
    choices = []
    for head in range(own_heads):
        wanted = ((device << turn) + request) * own_heads + head
        choices.append((place == wanted).astype(jnp.float32))
    latents = jnp.dot(
        jnp.concatenate(choices, axis=0).astype(jnp.bfloat16),
        joined_ref[...],
        preferred_element_type=jnp.float32,
    ).astype(jnp.bfloat16)
    values = [
        jnp.dot(
            latents[head * shape[0] : (head + 1) * shape[0]],
            absorb_ref[head],
            preferred_element_type=jnp.float32,
        ).astype(jnp.bfloat16)
        for head in range(own_heads)
    ]
    values = jnp.concatenate(values, axis=1)
    for at in range(0, width, TILE):
        term = jnp.dot(values, w_ref[:, at : at + TILE], preferred_element_type=jnp.float32)
        store_term(term, at, pieces)
    residual = residual_ref[...].astype(jnp.float32)
    stays = pieces[PIECES - 1]
    stays[:own_rows, :] = stays[:own_rows, :] + residual


def project(joined, w_absorb, residual_in, w_out, rows, far):
    depth, width = w_out.shape
    own_rows = residual_in.shape[0]
    return pl.pallas_call(
        functools.partial(project_kernel, own_rows, far),
        out_shape=term_shapes(rows // (2 * PIECES), width),
        in_specs=[pl.BlockSpec(memory_space=pltpu.VMEM)] * 4,
        out_specs=[pl.BlockSpec(memory_space=pltpu.VMEM)] * (PIECES + 2),
        compiler_params=pltpu.CompilerParams(vmem_limit_bytes=24 * MIB),
        cost_estimate=pl.CostEstimate(
            flops=2 * rows * depth * width, bytes_accessed=2 * depth * width, transcendentals=0
        ),
        name="project",
    )(joined, residual_in, w_absorb, w_out)


def expert_kernel(*refs):
    count = 2 * PIECES
    streams, (gain_ref, gate_ref, up_ref, down_ref) = refs[:count], refs[count : count + 4]
    pieces = refs[count + 4 :]
    streams = streams[1:PIECES] + streams[:1] + streams[PIECES + 1 :] + streams[PIECES : PIECES + 1]
    width = gain_ref.shape[1]
    depth = width // PARTS
    inverses = []
    for stream in streams:
        squares = 0.0
        for at in range(0, width, depth):
            piece = stream[:, at : at + depth].astype(jnp.float32)
            squares = squares + sum(lane_tiles(piece * piece))
        mean = jnp.sum(squares, axis=1, keepdims=True) / width
        inverses.append(lax.rsqrt(mean + 1e-06))
    gate, up = 0.0, 0.0
    for at in range(0, width, depth):
        gain = gain_ref[:, at : at + depth]
        tokens = jnp.concatenate(
            [
                stream[:, at : at + depth].astype(jnp.float32) * inverse * gain
                for stream, inverse in zip(streams, inverses)
            ],
            axis=0,
        ).astype(jnp.bfloat16)
        gate = gate + jnp.dot(
            tokens, gate_ref[at : at + depth, :], preferred_element_type=jnp.float32
        )
        up = up + jnp.dot(
            tokens, up_ref[at : at + depth, :], preferred_element_type=jnp.float32
        )
    active = (gate / (1.0 + jnp.exp(-gate)) * up).astype(jnp.bfloat16)
    for at in range(0, width, TILE):
        term = jnp.dot(active, down_ref[:, at : at + TILE], preferred_element_type=jnp.float32)
        store_term(term, at, pieces)


def run_expert(streams, norm_gain, w_gate, w_up, w_down):
    rows, width = streams[0].shape
    hidden = w_gate.shape[1]
    return pl.pallas_call(
        expert_kernel,
        out_shape=term_shapes(rows, width),
        in_specs=[pl.BlockSpec(memory_space=pltpu.VMEM)] * (2 * PIECES + 4),
        out_specs=[pl.BlockSpec(memory_space=pltpu.VMEM)] * (PIECES + 2),
        compiler_params=pltpu.CompilerParams(vmem_limit_bytes=24 * MIB),
        cost_estimate=pl.CostEstimate(
            flops=12 * PIECES * rows * hidden * width,
            bytes_accessed=6 * hidden * width,
            transcendentals=2 * PIECES * rows * hidden,
        ),
        name="expert",
    )(*streams, norm_gain[None], w_gate, w_up, w_down)


def swap(array, distance):
    pairs = [(at, at ^ distance) for at in range(lax.axis_size("experts"))]
    return lax.ppermute(array, "experts", pairs)


def wide(array):
    return array.astype(jnp.float32)


def collect(terms):
    *keeps, first, rest = terms
    rows = first.shape[0]
    rest = swap(rest, 1)
    others = [swap(first, 1)] + [
        rest[at * rows : (at + 1) * rows] for at in range(PIECES - 1)
    ]
    total = 0.0
    for keep, other, distance in zip(keeps, others, SQUARE):
        part = keep + wide(other)
        if distance:
            part = wide(swap(part.astype(jnp.bfloat16), distance))
        total = total + part
    return total


def exchange(total, far):
    own_rows = total.shape[0] // far
    sent = total.astype(jnp.bfloat16)
    for at in range(1, far):
        block = swap(sent, 8 * at)
        total = total + wide(
            jnp.concatenate(
                [block[(to ^ at) * own_rows : ((to ^ at) + 1) * own_rows] for to in range(far)]
            )
        )
    return total.astype(jnp.bfloat16)


def spread(stream):
    own = [stream] + [swap(stream, distance) for distance in SQUARE if distance]
    return own + [swap(piece, 1) for piece in own]


def shards(
    queries,
    cache,
    cache_len,
    residual_in,
    w_absorb,
    w_out,
    norm_gain,
    expert_ids,
    route_gates,
    w_gate,
    w_up,
    w_down,
):
    devices = lax.axis_size("experts")
    rank_here = lax.axis_index("experts")
    own_rows = queries.shape[0]
    all_rows = expert_ids.shape[0]
    far = devices // 8
    split_ways = FF // w_gate.shape[1]
    assert split_ways == 8

    latent = attend(queries, cache, cache_len, devices, w_absorb.shape[1])
    joined = lax.all_to_all(latent, "experts", split_axis=0, concat_axis=0, tiled=True)
    joined = joined.reshape(-1, joined.shape[-1])
    terms = project(joined, w_absorb, residual_in, w_out, all_rows, far)
    stream = exchange(collect(terms), far)
    attended = stream[:own_rows]

    total = collect(run_expert(spread(stream), norm_gain, w_gate, w_up, w_down))
    own_ids = lax.dynamic_slice_in_dim(expert_ids, rank_here * own_rows, own_rows, 0)
    mixings = []
    for at in range(far):
        expert = (rank_here ^ (8 * at)) // split_ways
        mixings.append(
            jnp.sum(
                route_gates * (own_ids == expert).astype(jnp.float32), axis=1, keepdims=True
            )
        )
    expert_out = lax.optimization_barrier(mixings[0] * total[:own_rows])
    for at in range(1, far):
        block = total[at * own_rows : (at + 1) * own_rows].astype(jnp.bfloat16)
        expert_out = expert_out + mixings[at] * wide(swap(block, 8 * at))
    return (attended, expert_out.astype(jnp.bfloat16))


def solution(mesh):
    placed = (
        P(("groups", "experts"), None, None),
        P(("groups", "experts"), None, None),
        P(("groups", "experts")),
        P(("groups", "experts"), None),
        P("experts", None, None),
        P("experts", None),
        P(),
        P("groups", None),
        P(("groups", "experts"), None),
        P(None, "experts"),
        P(None, "experts"),
        P("experts", None),
    )
    return jax.shard_map(
        shards,
        mesh=mesh,
        in_specs=placed,
        out_specs=(P(("groups", "experts"), None), P(("groups", "experts"), None)),
        check_vma=False,
    )
```

```python
import functools

import jax
import jax.numpy as jnp
from jax import lax
from jax.experimental import pallas as pl
from jax.experimental.pallas import tpu as pltpu
from jax.sharding import PartitionSpec as P

QK = 192
FF = 2048
BLOCK = 256
LOWEST = -3e38
GROUP = 8
LANES = 128
TILE = 256
PARTS = 4
SQUARE = (6, 4, 2, 0)
PIECES = len(SQUARE)
MIB = 2**20


def lane_tiles(array):
    return [array[:, at : at + LANES] for at in range(0, array.shape[1], LANES)]


def attend_kernel(
    len_ref,
    queries_ref,
    cache_ref,
    latent_ref,
    length,
    queries,
    held,
    summed,
    highest,
    sums,
    staged,
    item_row,
    item_block,
    length_arrived,
    queries_arrived,
    arrived,
):
    own_rows, heads, _ = queries.shape
    devices, _, rank = staged.shape
    own_heads = heads // devices
    blocks = held.shape[1]

    length_copy = pltpu.make_async_copy(len_ref, length, length_arrived)
    length_copy.start()
    queries_copy = pltpu.make_async_copy(queries_ref, queries, queries_arrived)
    queries_copy.start()

    def block_copy(row, block):
        return pltpu.make_async_copy(
            cache_ref.at[row, :, pl.ds(pl.multiple_of(block * BLOCK, BLOCK), BLOCK)],
            held.at[row, block],
            arrived.at[row, block],
        )

    for row in range(own_rows):
        block_copy(row, 0).start()
        item_row[row] = row
        item_block[row] = 0
    highest[...] = jnp.full_like(highest, LOWEST)
    sums[...] = jnp.zeros_like(sums)
    summed[...] = jnp.zeros_like(summed)
    length_copy.wait()
    items = own_rows
    for row in range(own_rows):
        count = (length[row] + BLOCK - 1) // BLOCK

        def begin(block, first, row=row):
            block_copy(row, block).start()
            item_row[first + block] = row
            item_block[first + block] = block
            return first

        lax.fori_loop(1, count, begin, items - 1)
        items = items + count - 1
    queries_copy.wait()
    column = lax.broadcasted_iota(jnp.int32, (heads, BLOCK), 1)

    def visit(first, many):
        inside = [(item_row[first + at], item_block[first + at]) for at in range(many)]
        for row, block in inside:
            block_copy(row, block).wait()
        found = []
        for row, block in inside:
            score = jnp.dot(
                queries[row], held[row, block], preferred_element_type=jnp.float32
            ) * QK ** (-0.5)
            found.append(
                jnp.where(column + block * BLOCK < length[row], score, -jnp.inf)
            )
        tops = [
            jnp.max(functools.reduce(jnp.maximum, lane_tiles(score)), axis=1, keepdims=True)
            for score in found
        ]
        weights = [jnp.exp(score - top) for score, top in zip(found, tops)]
        terms = [
            lax.dot_general(
                weight.astype(jnp.bfloat16),
                held[row, block, :rank, :],
                (((1,), (1,)), ((), ())),
                preferred_element_type=jnp.float32,
            )
            for (row, block), weight in zip(inside, weights)
        ]
        for (row, _), top, weight, term in zip(inside, tops, weights, terms):
            before = highest[row]
            after = jnp.maximum(before, top)
            old, new = jnp.exp(before - after), jnp.exp(top - after)
            highest[row] = after
            sums[row] = sums[row] * old + sum(lane_tiles(weight)) * new
            for at in range(0, rank, LANES):
                summed[row, :, at : at + LANES] = (
                    summed[row, :, at : at + LANES] * old + term[:, at : at + LANES] * new
                )

    def visit_group(group, _):
        visit(own_rows + group * GROUP, GROUP)
        return 0

    visit(0, own_rows)
    rest = items - own_rows
    lax.fori_loop(0, rest // GROUP, visit_group, 0)
    many = GROUP // 2
    while many:
        first = own_rows + rest // (2 * many) * (2 * many)
        pl.when((rest & many) != 0)(functools.partial(visit, first, many))
        many //= 2
    for row in range(own_rows):
        latent = summed[row] * (1.0 / jnp.sum(sums[row], axis=1, keepdims=True))
        for device in range(devices):
            staged[device, row * own_heads : (row + 1) * own_heads, :] = latent[
                device * own_heads : (device + 1) * own_heads
            ]
    latent_ref[...] = staged[...].astype(latent_ref.dtype)


def attend(queries, cache, cache_len, devices, rank):
    own_rows, depth, heads = queries.shape
    blocks = cache.shape[2] // BLOCK
    packed = own_rows * heads // devices
    listed = own_rows * blocks
    return pl.pallas_call(
        attend_kernel,
        out_shape=jax.ShapeDtypeStruct((devices, packed, rank), jnp.bfloat16),
        in_specs=[pl.BlockSpec(memory_space=pl.ANY)] * 3,
        out_specs=pl.BlockSpec(memory_space=pltpu.VMEM),
        scratch_shapes=[
            pltpu.SMEM((own_rows,), jnp.int32),
            pltpu.VMEM((own_rows, heads, depth), jnp.bfloat16),
            pltpu.VMEM((own_rows, blocks, depth, BLOCK), jnp.bfloat16),
            pltpu.VMEM((own_rows, heads, rank), jnp.float32),
            pltpu.VMEM((own_rows, heads, LANES), jnp.float32),
            pltpu.VMEM((own_rows, heads, LANES), jnp.float32),
            pltpu.VMEM((devices, packed, rank), jnp.float32),
            pltpu.SMEM((listed,), jnp.int32),
            pltpu.SMEM((listed,), jnp.int32),
            pltpu.SemaphoreType.DMA,
            pltpu.SemaphoreType.DMA,
            pltpu.SemaphoreType.DMA((own_rows, blocks)),
        ],
        compiler_params=pltpu.CompilerParams(vmem_limit_bytes=55 * MIB),
        cost_estimate=pl.CostEstimate(
            flops=own_rows * heads * cache.shape[2] * (depth + rank),
            bytes_accessed=cache.size,
            transcendentals=own_rows * heads * cache.shape[2],
        ),
        name="attend",
    )(cache_len, jnp.swapaxes(queries, 1, 2), cache)


def store_term(term, at, refs):
    first = 0
    for ref in refs:
        rows = ref.shape[0]
        ref[:, at : at + TILE] = term[first : first + rows].astype(ref.dtype)
        first += rows


def term_shapes(rows, width):
    kept = [jax.ShapeDtypeStruct((rows, width), jnp.float32)] * PIECES
    sent = [jax.ShapeDtypeStruct((many * rows, width), jnp.bfloat16) for many in (1, PIECES - 1)]
    return kept + sent


def project_kernel(own_rows, far, joined_ref, residual_ref, absorb_ref, w_ref, *pieces):
    own_heads = absorb_ref.shape[0]
    width = w_ref.shape[1]
    shape = (2 * PIECES * pieces[0].shape[0], joined_ref.shape[0])
    row = lax.broadcasted_iota(jnp.int32, shape, 0)
    place = lax.broadcasted_iota(jnp.int32, shape, 1)
    turn = own_rows.bit_length() - 1
    far_bits = far.bit_length() - 1
    request, slot = row & (own_rows - 1), row >> turn
    far_at, slot = slot & (far - 1), slot >> far_bits
    distance = (far_at << 3) + ((3 - (slot & 3)) << 1) + (slot >> 2)
    device = distance ^ lax.axis_index("experts")
    choices = []
    for head in range(own_heads):
        wanted = ((device << turn) + request) * own_heads + head
        choices.append((place == wanted).astype(jnp.float32))
    latents = jnp.dot(
        jnp.concatenate(choices, axis=0).astype(jnp.bfloat16),
        joined_ref[...],
        preferred_element_type=jnp.float32,
    ).astype(jnp.bfloat16)
    values = [
        jnp.dot(
            latents[head * shape[0] : (head + 1) * shape[0]],
            absorb_ref[head],
            preferred_element_type=jnp.float32,
        ).astype(jnp.bfloat16)
        for head in range(own_heads)
    ]
    values = jnp.concatenate(values, axis=1)
    for at in range(0, width, TILE):
        term = jnp.dot(values, w_ref[:, at : at + TILE], preferred_element_type=jnp.float32)
        store_term(term, at, pieces)
    residual = residual_ref[...].astype(jnp.float32)
    stays = pieces[PIECES - 1]
    stays[:own_rows, :] = stays[:own_rows, :] + residual


def project(joined, w_absorb, residual_in, w_out, rows, far):
    depth, width = w_out.shape
    own_rows = residual_in.shape[0]
    return pl.pallas_call(
        functools.partial(project_kernel, own_rows, far),
        out_shape=term_shapes(rows // (2 * PIECES), width),
        in_specs=[pl.BlockSpec(memory_space=pltpu.VMEM)] * 4,
        out_specs=[pl.BlockSpec(memory_space=pltpu.VMEM)] * (PIECES + 2),
        compiler_params=pltpu.CompilerParams(vmem_limit_bytes=24 * MIB),
        cost_estimate=pl.CostEstimate(
            flops=2 * rows * depth * width, bytes_accessed=2 * depth * width, transcendentals=0
        ),
        name="project",
    )(joined, residual_in, w_absorb, w_out)


def expert_kernel(*refs):
    count = 2 * PIECES
    streams, (gain_ref, gate_ref, up_ref, down_ref) = refs[:count], refs[count : count + 4]
    pieces = refs[count + 4 :]
    streams = streams[1:PIECES] + streams[:1] + streams[PIECES + 1 :] + streams[PIECES : PIECES + 1]
    width = gain_ref.shape[1]
    depth = width // PARTS
    inverses = []
    for stream in streams:
        squares = 0.0
        for at in range(0, width, depth):
            piece = stream[:, at : at + depth].astype(jnp.float32)
            squares = squares + sum(lane_tiles(piece * piece))
        mean = jnp.sum(squares, axis=1, keepdims=True) / width
        inverses.append(lax.rsqrt(mean + 1e-06))
    gate, up = 0.0, 0.0
    for at in range(0, width, depth):
        gain = gain_ref[:, at : at + depth]
        tokens = jnp.concatenate(
            [
                stream[:, at : at + depth].astype(jnp.float32) * inverse * gain
                for stream, inverse in zip(streams, inverses)
            ],
            axis=0,
        ).astype(jnp.bfloat16)
        gate = gate + jnp.dot(
            tokens, gate_ref[at : at + depth, :], preferred_element_type=jnp.float32
        )
        up = up + jnp.dot(
            tokens, up_ref[at : at + depth, :], preferred_element_type=jnp.float32
        )
    active = (gate / (1.0 + jnp.exp(-gate)) * up).astype(jnp.bfloat16)
    for at in range(0, width, TILE):
        term = jnp.dot(active, down_ref[:, at : at + TILE], preferred_element_type=jnp.float32)
        store_term(term, at, pieces)


def run_expert(streams, norm_gain, w_gate, w_up, w_down):
    rows, width = streams[0].shape
    hidden = w_gate.shape[1]
    return pl.pallas_call(
        expert_kernel,
        out_shape=term_shapes(rows, width),
        in_specs=[pl.BlockSpec(memory_space=pltpu.VMEM)] * (2 * PIECES + 4),
        out_specs=[pl.BlockSpec(memory_space=pltpu.VMEM)] * (PIECES + 2),
        compiler_params=pltpu.CompilerParams(vmem_limit_bytes=24 * MIB),
        cost_estimate=pl.CostEstimate(
            flops=12 * PIECES * rows * hidden * width,
            bytes_accessed=6 * hidden * width,
            transcendentals=2 * PIECES * rows * hidden,
        ),
        name="expert",
    )(*streams, norm_gain[None], w_gate, w_up, w_down)


def swap(array, distance):
    pairs = [(at, at ^ distance) for at in range(lax.axis_size("experts"))]
    return lax.ppermute(array, "experts", pairs)


def wide(array):
    return array.astype(jnp.float32)


def collect(terms):
    *keeps, first, rest = terms
    rows = first.shape[0]
    rest = swap(rest, 1)
    others = [swap(first, 1)] + [
        rest[at * rows : (at + 1) * rows] for at in range(PIECES - 1)
    ]
    total = 0.0
    for keep, other, distance in zip(keeps, others, SQUARE):
        part = keep + wide(other)
        if distance:
            part = wide(swap(part.astype(jnp.bfloat16), distance))
        total = total + part
    return total


def exchange(total, far):
    own_rows = total.shape[0] // far
    sent = total.astype(jnp.bfloat16)
    for at in range(1, far):
        block = swap(sent, 8 * at)
        total = total + wide(
            jnp.concatenate(
                [block[(to ^ at) * own_rows : ((to ^ at) + 1) * own_rows] for to in range(far)]
            )
        )
    return total.astype(jnp.bfloat16)


def spread(stream):
    own = [stream] + [swap(stream, distance) for distance in SQUARE if distance]
    return own + [swap(piece, 1) for piece in own]


def shards(
    queries,
    cache,
    cache_len,
    residual_in,
    w_absorb,
    w_out,
    norm_gain,
    expert_ids,
    route_gates,
    w_gate,
    w_up,
    w_down,
):
    devices = lax.axis_size("experts")
    rank_here = lax.axis_index("experts")
    own_rows = queries.shape[0]
    all_rows = expert_ids.shape[0]
    far = devices // 8
    split_ways = FF // w_gate.shape[1]
    assert split_ways == 8

    latent = attend(queries, cache, cache_len, devices, w_absorb.shape[1])
    joined = lax.all_to_all(latent, "experts", split_axis=0, concat_axis=0, tiled=True)
    joined = joined.reshape(-1, joined.shape[-1])
    terms = project(joined, w_absorb, residual_in, w_out, all_rows, far)
    stream = exchange(collect(terms), far)
    attended = stream[:own_rows]

    total = collect(run_expert(spread(stream), norm_gain, w_gate, w_up, w_down))
    own_ids = lax.dynamic_slice_in_dim(expert_ids, rank_here * own_rows, own_rows, 0)
    mixings = []
    for at in range(far):
        expert = (rank_here ^ (8 * at)) // split_ways
        mixings.append(
            jnp.sum(
                route_gates * (own_ids == expert).astype(jnp.float32), axis=1, keepdims=True
            )
        )
    expert_out = lax.optimization_barrier(mixings[0] * total[:own_rows])
    for at in range(1, far):
        block = total[at * own_rows : (at + 1) * own_rows].astype(jnp.bfloat16)
        expert_out = expert_out + mixings[at] * wide(swap(block, 8 * at))
    return (attended, expert_out.astype(jnp.bfloat16))


def solution(mesh):
    placed = (
        P(("groups", "experts"), None, None),
        P(("groups", "experts"), None, None),
        P(("groups", "experts")),
        P(("groups", "experts"), None),
        P("experts", None, None),
        P("experts", None),
        P(),
        P("groups", None),
        P(("groups", "experts"), None),
        P(None, "experts"),
        P(None, "experts"),
        P("experts", None),
    )
    return jax.shard_map(
        shards,
        mesh=mesh,
        in_specs=placed,
        out_specs=(P(("groups", "experts"), None), P(("groups", "experts"), None)),
        check_vma=False,
    )
```

```python
import functools

import jax
import jax.numpy as jnp
from jax import lax
from jax.experimental import pallas as pl
from jax.experimental.pallas import tpu as pltpu
from jax.sharding import PartitionSpec as P

QK = 192
FF = 2048
BLOCK = 512
LOWEST = -3e38
GROUP = 8
LANES = 128
TILE = 256
PARTS = 4
SQUARE = (6, 4, 2, 0)
PIECES = len(SQUARE)
MIB = 2**20


def lane_tiles(array):
    return [array[:, at : at + LANES] for at in range(0, array.shape[1], LANES)]


def attend_kernel(
    len_ref,
    queries_ref,
    cache_ref,
    latent_ref,
    length,
    queries,
    held,
    summed,
    highest,
    sums,
    staged,
    item_row,
    item_block,
    length_arrived,
    queries_arrived,
    arrived,
):
    own_rows, heads, _ = queries.shape
    devices, _, rank = staged.shape
    own_heads = heads // devices
    blocks = held.shape[1]

    length_copy = pltpu.make_async_copy(len_ref, length, length_arrived)
    length_copy.start()
    queries_copy = pltpu.make_async_copy(queries_ref, queries, queries_arrived)
    queries_copy.start()

    def block_copy(row, block):
        return pltpu.make_async_copy(
            cache_ref.at[row, :, pl.ds(pl.multiple_of(block * BLOCK, BLOCK), BLOCK)],
            held.at[row, block],
            arrived.at[row, block],
        )

    for row in range(own_rows):
        block_copy(row, 0).start()
        item_row[row] = row
        item_block[row] = 0
    highest[...] = jnp.full_like(highest, LOWEST)
    sums[...] = jnp.zeros_like(sums)
    summed[...] = jnp.zeros_like(summed)
    length_copy.wait()
    items = own_rows
    for row in range(own_rows):
        count = (length[row] + BLOCK - 1) // BLOCK

        def begin(block, first, row=row):
            block_copy(row, block).start()
            item_row[first + block] = row
            item_block[first + block] = block
            return first

        lax.fori_loop(1, count, begin, items - 1)
        items = items + count - 1
    queries_copy.wait()
    column = lax.broadcasted_iota(jnp.int32, (heads, BLOCK), 1)

    def visit(first, many):
        inside = [(item_row[first + at], item_block[first + at]) for at in range(many)]
        for row, block in inside:
            block_copy(row, block).wait()
        found = []
        for row, block in inside:
            score = jnp.dot(
                queries[row], held[row, block], preferred_element_type=jnp.float32
            ) * QK ** (-0.5)
            found.append(
                jnp.where(column + block * BLOCK < length[row], score, -jnp.inf)
            )
        tops = [
            jnp.max(functools.reduce(jnp.maximum, lane_tiles(score)), axis=1, keepdims=True)
            for score in found
        ]
        weights = [jnp.exp(score - top) for score, top in zip(found, tops)]
        terms = [
            lax.dot_general(
                weight.astype(jnp.bfloat16),
                held[row, block, :rank, :],
                (((1,), (1,)), ((), ())),
                preferred_element_type=jnp.float32,
            )
            for (row, block), weight in zip(inside, weights)
        ]
        for (row, _), top, weight, term in zip(inside, tops, weights, terms):
            before = highest[row]
            after = jnp.maximum(before, top)
            old, new = jnp.exp(before - after), jnp.exp(top - after)
            highest[row] = after
            sums[row] = sums[row] * old + sum(lane_tiles(weight)) * new
            for at in range(0, rank, LANES):
                summed[row, :, at : at + LANES] = (
                    summed[row, :, at : at + LANES] * old + term[:, at : at + LANES] * new
                )

    def visit_group(group, _):
        visit(own_rows + group * GROUP, GROUP)
        return 0

    visit(0, own_rows)
    rest = items - own_rows
    lax.fori_loop(0, rest // GROUP, visit_group, 0)
    many = GROUP // 2
    while many:
        first = own_rows + rest // (2 * many) * (2 * many)
        pl.when((rest & many) != 0)(functools.partial(visit, first, many))
        many //= 2
    for row in range(own_rows):
        latent = summed[row] * (1.0 / jnp.sum(sums[row], axis=1, keepdims=True))
        for device in range(devices):
            staged[device, row * own_heads : (row + 1) * own_heads, :] = latent[
                device * own_heads : (device + 1) * own_heads
            ]
    latent_ref[...] = staged[...].astype(latent_ref.dtype)


def attend(queries, cache, cache_len, devices, rank):
    own_rows, depth, heads = queries.shape
    blocks = cache.shape[2] // BLOCK
    packed = own_rows * heads // devices
    listed = own_rows * blocks
    return pl.pallas_call(
        attend_kernel,
        out_shape=jax.ShapeDtypeStruct((devices, packed, rank), jnp.bfloat16),
        in_specs=[pl.BlockSpec(memory_space=pl.ANY)] * 3,
        out_specs=pl.BlockSpec(memory_space=pltpu.VMEM),
        scratch_shapes=[
            pltpu.SMEM((own_rows,), jnp.int32),
            pltpu.VMEM((own_rows, heads, depth), jnp.bfloat16),
            pltpu.VMEM((own_rows, blocks, depth, BLOCK), jnp.bfloat16),
            pltpu.VMEM((own_rows, heads, rank), jnp.float32),
            pltpu.VMEM((own_rows, heads, LANES), jnp.float32),
            pltpu.VMEM((own_rows, heads, LANES), jnp.float32),
            pltpu.VMEM((devices, packed, rank), jnp.float32),
            pltpu.SMEM((listed,), jnp.int32),
            pltpu.SMEM((listed,), jnp.int32),
            pltpu.SemaphoreType.DMA,
            pltpu.SemaphoreType.DMA,
            pltpu.SemaphoreType.DMA((own_rows, blocks)),
        ],
        compiler_params=pltpu.CompilerParams(vmem_limit_bytes=55 * MIB),
        cost_estimate=pl.CostEstimate(
            flops=own_rows * heads * cache.shape[2] * (depth + rank),
            bytes_accessed=cache.size,
            transcendentals=own_rows * heads * cache.shape[2],
        ),
        name="attend",
    )(cache_len, jnp.swapaxes(queries, 1, 2), cache)


def store_term(term, at, refs):
    first = 0
    for ref in refs:
        rows = ref.shape[0]
        ref[:, at : at + TILE] = term[first : first + rows].astype(ref.dtype)
        first += rows


def term_shapes(rows, width):
    kept = [jax.ShapeDtypeStruct((rows, width), jnp.float32)] * PIECES
    sent = [jax.ShapeDtypeStruct((many * rows, width), jnp.bfloat16) for many in (1, PIECES - 1)]
    return kept + sent


def project_kernel(own_rows, far, joined_ref, residual_ref, absorb_ref, w_ref, *pieces):
    own_heads = absorb_ref.shape[0]
    width = w_ref.shape[1]
    shape = (2 * PIECES * pieces[0].shape[0], joined_ref.shape[0])
    row = lax.broadcasted_iota(jnp.int32, shape, 0)
    place = lax.broadcasted_iota(jnp.int32, shape, 1)
    turn = own_rows.bit_length() - 1
    far_bits = far.bit_length() - 1
    request, slot = row & (own_rows - 1), row >> turn
    far_at, slot = slot & (far - 1), slot >> far_bits
    distance = (far_at << 3) + ((3 - (slot & 3)) << 1) + (slot >> 2)
    device = distance ^ lax.axis_index("experts")
    choices = []
    for head in range(own_heads):
        wanted = ((device << turn) + request) * own_heads + head
        choices.append((place == wanted).astype(jnp.float32))
    latents = jnp.dot(
        jnp.concatenate(choices, axis=0).astype(jnp.bfloat16),
        joined_ref[...],
        preferred_element_type=jnp.float32,
    ).astype(jnp.bfloat16)
    values = [
        jnp.dot(
            latents[head * shape[0] : (head + 1) * shape[0]],
            absorb_ref[head],
            preferred_element_type=jnp.float32,
        ).astype(jnp.bfloat16)
        for head in range(own_heads)
    ]
    values = jnp.concatenate(values, axis=1)
    for at in range(0, width, TILE):
        term = jnp.dot(values, w_ref[:, at : at + TILE], preferred_element_type=jnp.float32)
        store_term(term, at, pieces)
    residual = residual_ref[...].astype(jnp.float32)
    stays = pieces[PIECES - 1]
    stays[:own_rows, :] = stays[:own_rows, :] + residual


def project(joined, w_absorb, residual_in, w_out, rows, far):
    depth, width = w_out.shape
    own_rows = residual_in.shape[0]
    return pl.pallas_call(
        functools.partial(project_kernel, own_rows, far),
        out_shape=term_shapes(rows // (2 * PIECES), width),
        in_specs=[pl.BlockSpec(memory_space=pltpu.VMEM)] * 4,
        out_specs=[pl.BlockSpec(memory_space=pltpu.VMEM)] * (PIECES + 2),
        compiler_params=pltpu.CompilerParams(vmem_limit_bytes=24 * MIB),
        cost_estimate=pl.CostEstimate(
            flops=2 * rows * depth * width, bytes_accessed=2 * depth * width, transcendentals=0
        ),
        name="project",
    )(joined, residual_in, w_absorb, w_out)


def expert_kernel(*refs):
    count = 2 * PIECES
    streams, (gain_ref, gate_ref, up_ref, down_ref) = refs[:count], refs[count : count + 4]
    pieces = refs[count + 4 :]
    streams = streams[1:PIECES] + streams[:1] + streams[PIECES + 1 :] + streams[PIECES : PIECES + 1]
    width = gain_ref.shape[1]
    depth = width // PARTS
    inverses = []
    for stream in streams:
        squares = 0.0
        for at in range(0, width, depth):
            piece = stream[:, at : at + depth].astype(jnp.float32)
            squares = squares + sum(lane_tiles(piece * piece))
        mean = jnp.sum(squares, axis=1, keepdims=True) / width
        inverses.append(lax.rsqrt(mean + 1e-06))
    gate, up = 0.0, 0.0
    for at in range(0, width, depth):
        gain = gain_ref[:, at : at + depth]
        tokens = jnp.concatenate(
            [
                stream[:, at : at + depth].astype(jnp.float32) * inverse * gain
                for stream, inverse in zip(streams, inverses)
            ],
            axis=0,
        ).astype(jnp.bfloat16)
        gate = gate + jnp.dot(
            tokens, gate_ref[at : at + depth, :], preferred_element_type=jnp.float32
        )
        up = up + jnp.dot(
            tokens, up_ref[at : at + depth, :], preferred_element_type=jnp.float32
        )
    active = (gate / (1.0 + jnp.exp(-gate)) * up).astype(jnp.bfloat16)
    for at in range(0, width, TILE):
        term = jnp.dot(active, down_ref[:, at : at + TILE], preferred_element_type=jnp.float32)
        store_term(term, at, pieces)


def run_expert(streams, norm_gain, w_gate, w_up, w_down):
    rows, width = streams[0].shape
    hidden = w_gate.shape[1]
    return pl.pallas_call(
        expert_kernel,
        out_shape=term_shapes(rows, width),
        in_specs=[pl.BlockSpec(memory_space=pltpu.VMEM)] * (2 * PIECES + 4),
        out_specs=[pl.BlockSpec(memory_space=pltpu.VMEM)] * (PIECES + 2),
        compiler_params=pltpu.CompilerParams(vmem_limit_bytes=24 * MIB),
        cost_estimate=pl.CostEstimate(
            flops=12 * PIECES * rows * hidden * width,
            bytes_accessed=6 * hidden * width,
            transcendentals=2 * PIECES * rows * hidden,
        ),
        name="expert",
    )(*streams, norm_gain[None], w_gate, w_up, w_down)


def swap(array, distance):
    pairs = [(at, at ^ distance) for at in range(lax.axis_size("experts"))]
    return lax.ppermute(array, "experts", pairs)


def wide(array):
    return array.astype(jnp.float32)


def collect(terms):
    *keeps, first, rest = terms
    rows = first.shape[0]
    rest = swap(rest, 1)
    others = [swap(first, 1)] + [
        rest[at * rows : (at + 1) * rows] for at in range(PIECES - 1)
    ]
    found = []
    for keep, other, distance in zip(keeps, others, SQUARE):
        part = keep + wide(other)
        if distance:
            part = swap(part.astype(jnp.bfloat16), distance)
        found.append(part)
    return found


def exchange(total, far):
    own_rows = total.shape[0] // far
    sent = total.astype(jnp.bfloat16)
    for at in range(1, far):
        block = swap(sent, 8 * at)
        total = total + wide(
            jnp.concatenate(
                [block[(to ^ at) * own_rows : ((to ^ at) + 1) * own_rows] for to in range(far)]
            )
        )
    return total.astype(jnp.bfloat16)


def spread(stream):
    own = [stream] + [swap(stream, distance) for distance in SQUARE if distance]
    return own + [swap(piece, 1) for piece in own]


def shards(
    queries,
    cache,
    cache_len,
    residual_in,
    w_absorb,
    w_out,
    norm_gain,
    expert_ids,
    route_gates,
    w_gate,
    w_up,
    w_down,
):
    devices = lax.axis_size("experts")
    rank_here = lax.axis_index("experts")
    own_rows = queries.shape[0]
    all_rows = expert_ids.shape[0]
    far = devices // 8
    split_ways = FF // w_gate.shape[1]
    assert split_ways == 8

    latent = attend(queries, cache, cache_len, devices, w_absorb.shape[1])
    joined = lax.all_to_all(latent, "experts", split_axis=0, concat_axis=0, tiled=True)
    joined = joined.reshape(-1, joined.shape[-1])
    terms = project(joined, w_absorb, residual_in, w_out, all_rows, far)
    stream = exchange(sum(wide(part) for part in collect(terms)), far)
    attended = stream[:own_rows]

    parts = collect(run_expert(spread(stream), norm_gain, w_gate, w_up, w_down))
    sent = [
        sum(wide(part[at * own_rows : (at + 1) * own_rows]) for part in parts).astype(
            jnp.bfloat16
        )
        for at in range(1, far)
    ]
    *sent, parts = lax.optimization_barrier((*sent, parts))
    own_ids = lax.dynamic_slice_in_dim(expert_ids, rank_here * own_rows, own_rows, 0)
    mixings = []
    for at in range(far):
        expert = (rank_here ^ (8 * at)) // split_ways
        mixings.append(
            jnp.sum(
                route_gates * (own_ids == expert).astype(jnp.float32), axis=1, keepdims=True
            )
        )
    kept = sum(wide(part[:own_rows]) for part in parts)
    expert_out = lax.optimization_barrier(mixings[0] * kept)
    for at in range(1, far):
        expert_out = expert_out + mixings[at] * wide(swap(sent[at - 1], 8 * at))
    return (attended, expert_out.astype(jnp.bfloat16))


def solution(mesh):
    placed = (
        P(("groups", "experts"), None, None),
        P(("groups", "experts"), None, None),
        P(("groups", "experts")),
        P(("groups", "experts"), None),
        P("experts", None, None),
        P("experts", None),
        P(),
        P("groups", None),
        P(("groups", "experts"), None),
        P(None, "experts"),
        P(None, "experts"),
        P("experts", None),
    )
    return jax.shard_map(
        shards,
        mesh=mesh,
        in_specs=placed,
        out_specs=(P(("groups", "experts"), None), P(("groups", "experts"), None)),
        check_vma=False,
    )
```

```python
import functools

import jax
import jax.numpy as jnp
from jax import lax
from jax.experimental import pallas as pl
from jax.experimental.pallas import tpu as pltpu
from jax.sharding import PartitionSpec as P

QK = 192
FF = 2048
BLOCK = 512
LOWEST = -3e38
GROUP = 8
LANES = 128
TILE = 256
PARTS = 4
SQUARE = (6, 4, 2, 0)
PIECES = len(SQUARE)
MIB = 2**20


def lane_tiles(array):
    return [array[:, at : at + LANES] for at in range(0, array.shape[1], LANES)]


def attend_kernel(
    len_ref,
    queries_ref,
    cache_ref,
    latent_ref,
    length,
    queries,
    held,
    summed,
    highest,
    sums,
    staged,
    item_row,
    item_block,
    length_arrived,
    queries_arrived,
    arrived,
):
    own_rows, heads, _ = queries.shape
    devices, _, rank = staged.shape
    own_heads = heads // devices
    blocks = held.shape[1]

    length_copy = pltpu.make_async_copy(len_ref, length, length_arrived)
    length_copy.start()
    queries_copy = pltpu.make_async_copy(queries_ref, queries, queries_arrived)
    queries_copy.start()

    def block_copy(row, block):
        return pltpu.make_async_copy(
            cache_ref.at[row, :, pl.ds(pl.multiple_of(block * BLOCK, BLOCK), BLOCK)],
            held.at[row, block],
            arrived.at[row, block],
        )

    for row in range(own_rows):
        block_copy(row, 0).start()
        item_row[row] = row
        item_block[row] = 0
    highest[...] = jnp.full_like(highest, LOWEST)
    sums[...] = jnp.zeros_like(sums)
    summed[...] = jnp.zeros_like(summed)
    length_copy.wait()
    items = own_rows
    for row in range(own_rows):
        count = (length[row] + BLOCK - 1) // BLOCK

        def begin(block, first, row=row):
            block_copy(row, block).start()
            item_row[first + block] = row
            item_block[first + block] = block
            return first

        lax.fori_loop(1, count, begin, items - 1)
        items = items + count - 1
    queries_copy.wait()
    column = lax.broadcasted_iota(jnp.int32, (heads, BLOCK), 1)

    def visit(first, many):
        inside = [(item_row[first + at], item_block[first + at]) for at in range(many)]
        for row, block in inside:
            block_copy(row, block).wait()
        found = []
        for row, block in inside:
            score = jnp.dot(
                queries[row], held[row, block], preferred_element_type=jnp.float32
            ) * QK ** (-0.5)
            found.append(
                jnp.where(column + block * BLOCK < length[row], score, -jnp.inf)
            )
        tops = [
            jnp.max(functools.reduce(jnp.maximum, lane_tiles(score)), axis=1, keepdims=True)
            for score in found
        ]
        weights = [jnp.exp(score - top) for score, top in zip(found, tops)]
        terms = [
            lax.dot_general(
                weight.astype(jnp.bfloat16),
                held[row, block, :rank, :],
                (((1,), (1,)), ((), ())),
                preferred_element_type=jnp.float32,
            )
            for (row, block), weight in zip(inside, weights)
        ]
        for (row, _), top, weight, term in zip(inside, tops, weights, terms):
            before = highest[row]
            after = jnp.maximum(before, top)
            old, new = jnp.exp(before - after), jnp.exp(top - after)
            highest[row] = after
            sums[row] = sums[row] * old + sum(lane_tiles(weight)) * new
            for at in range(0, rank, LANES):
                summed[row, :, at : at + LANES] = (
                    summed[row, :, at : at + LANES] * old + term[:, at : at + LANES] * new
                )

    def visit_group(group, _):
        visit(own_rows + group * GROUP, GROUP)
        return 0

    visit(0, own_rows)
    rest = items - own_rows
    lax.fori_loop(0, rest // GROUP, visit_group, 0)
    left = rest % GROUP
    for many in range(1, GROUP):
        pl.when(left == many)(functools.partial(visit, items - many, many))
    for row in range(own_rows):
        latent = summed[row] * (1.0 / jnp.sum(sums[row], axis=1, keepdims=True))
        for device in range(devices):
            staged[device, row * own_heads : (row + 1) * own_heads, :] = latent[
                device * own_heads : (device + 1) * own_heads
            ]
    latent_ref[...] = staged[...].astype(latent_ref.dtype)


def attend(queries, cache, cache_len, devices, rank):
    own_rows, depth, heads = queries.shape
    blocks = cache.shape[2] // BLOCK
    packed = own_rows * heads // devices
    listed = own_rows * blocks
    return pl.pallas_call(
        attend_kernel,
        out_shape=jax.ShapeDtypeStruct((devices, packed, rank), jnp.bfloat16),
        in_specs=[pl.BlockSpec(memory_space=pl.ANY)] * 3,
        out_specs=pl.BlockSpec(memory_space=pltpu.VMEM),
        scratch_shapes=[
            pltpu.SMEM((own_rows,), jnp.int32),
            pltpu.VMEM((own_rows, heads, depth), jnp.bfloat16),
            pltpu.VMEM((own_rows, blocks, depth, BLOCK), jnp.bfloat16),
            pltpu.VMEM((own_rows, heads, rank), jnp.float32),
            pltpu.VMEM((own_rows, heads, LANES), jnp.float32),
            pltpu.VMEM((own_rows, heads, LANES), jnp.float32),
            pltpu.VMEM((devices, packed, rank), jnp.float32),
            pltpu.SMEM((listed,), jnp.int32),
            pltpu.SMEM((listed,), jnp.int32),
            pltpu.SemaphoreType.DMA,
            pltpu.SemaphoreType.DMA,
            pltpu.SemaphoreType.DMA((own_rows, blocks)),
        ],
        compiler_params=pltpu.CompilerParams(vmem_limit_bytes=55 * MIB),
        cost_estimate=pl.CostEstimate(
            flops=own_rows * heads * cache.shape[2] * (depth + rank),
            bytes_accessed=cache.size,
            transcendentals=own_rows * heads * cache.shape[2],
        ),
        name="attend",
    )(cache_len, jnp.swapaxes(queries, 1, 2), cache)


def store_term(term, at, refs):
    first = 0
    for ref in refs:
        rows = ref.shape[0]
        ref[:, at : at + TILE] = term[first : first + rows].astype(ref.dtype)
        first += rows


def term_shapes(rows, width):
    kept = [jax.ShapeDtypeStruct((rows, width), jnp.float32)] * PIECES
    sent = [jax.ShapeDtypeStruct((many * rows, width), jnp.bfloat16) for many in (1, PIECES - 1)]
    return kept + sent


def project_kernel(own_rows, far, joined_ref, residual_ref, absorb_ref, w_ref, *pieces):
    own_heads = absorb_ref.shape[0]
    width = w_ref.shape[1]
    shape = (2 * PIECES * pieces[0].shape[0], joined_ref.shape[0])
    row = lax.broadcasted_iota(jnp.int32, shape, 0)
    place = lax.broadcasted_iota(jnp.int32, shape, 1)
    turn = own_rows.bit_length() - 1
    far_bits = far.bit_length() - 1
    request, slot = row & (own_rows - 1), row >> turn
    far_at, slot = slot & (far - 1), slot >> far_bits
    distance = (far_at << 3) + ((3 - (slot & 3)) << 1) + (slot >> 2)
    device = distance ^ lax.axis_index("experts")
    choices = []
    for head in range(own_heads):
        wanted = ((device << turn) + request) * own_heads + head
        choices.append((place == wanted).astype(jnp.float32))
    latents = jnp.dot(
        jnp.concatenate(choices, axis=0).astype(jnp.bfloat16),
        joined_ref[...],
        preferred_element_type=jnp.float32,
    ).astype(jnp.bfloat16)
    values = [
        jnp.dot(
            latents[head * shape[0] : (head + 1) * shape[0]],
            absorb_ref[head],
            preferred_element_type=jnp.float32,
        ).astype(jnp.bfloat16)
        for head in range(own_heads)
    ]
    values = jnp.concatenate(values, axis=1)
    for at in range(0, width, TILE):
        term = jnp.dot(values, w_ref[:, at : at + TILE], preferred_element_type=jnp.float32)
        store_term(term, at, pieces)
    residual = residual_ref[...].astype(jnp.float32)
    stays = pieces[PIECES - 1]
    stays[:own_rows, :] = stays[:own_rows, :] + residual


def project(joined, w_absorb, residual_in, w_out, rows, far):
    depth, width = w_out.shape
    own_rows = residual_in.shape[0]
    return pl.pallas_call(
        functools.partial(project_kernel, own_rows, far),
        out_shape=term_shapes(rows // (2 * PIECES), width),
        in_specs=[pl.BlockSpec(memory_space=pltpu.VMEM)] * 4,
        out_specs=[pl.BlockSpec(memory_space=pltpu.VMEM)] * (PIECES + 2),
        compiler_params=pltpu.CompilerParams(vmem_limit_bytes=24 * MIB),
        cost_estimate=pl.CostEstimate(
            flops=2 * rows * depth * width, bytes_accessed=2 * depth * width, transcendentals=0
        ),
        name="project",
    )(joined, residual_in, w_absorb, w_out)


def expert_kernel(*refs):
    count = 2 * PIECES
    streams, (gain_ref, gate_ref, up_ref, down_ref) = refs[:count], refs[count : count + 4]
    pieces = refs[count + 4 :]
    streams = streams[1:PIECES] + streams[:1] + streams[PIECES + 1 :] + streams[PIECES : PIECES + 1]
    width = gain_ref.shape[1]
    depth = width // PARTS
    inverses = []
    for stream in streams:
        squares = 0.0
        for at in range(0, width, depth):
            piece = stream[:, at : at + depth].astype(jnp.float32)
            squares = squares + sum(lane_tiles(piece * piece))
        mean = jnp.sum(squares, axis=1, keepdims=True) / width
        inverses.append(lax.rsqrt(mean + 1e-06))
    gate, up = 0.0, 0.0
    for at in range(0, width, depth):
        gain = gain_ref[:, at : at + depth]
        tokens = jnp.concatenate(
            [
                stream[:, at : at + depth].astype(jnp.float32) * inverse * gain
                for stream, inverse in zip(streams, inverses)
            ],
            axis=0,
        ).astype(jnp.bfloat16)
        gate = gate + jnp.dot(
            tokens, gate_ref[at : at + depth, :], preferred_element_type=jnp.float32
        )
        up = up + jnp.dot(
            tokens, up_ref[at : at + depth, :], preferred_element_type=jnp.float32
        )
    active = (gate / (1.0 + jnp.exp(-gate)) * up).astype(jnp.bfloat16)
    for at in range(0, width, TILE):
        term = jnp.dot(active, down_ref[:, at : at + TILE], preferred_element_type=jnp.float32)
        store_term(term, at, pieces)


def run_expert(streams, norm_gain, w_gate, w_up, w_down):
    rows, width = streams[0].shape
    hidden = w_gate.shape[1]
    return pl.pallas_call(
        expert_kernel,
        out_shape=term_shapes(rows, width),
        in_specs=[pl.BlockSpec(memory_space=pltpu.VMEM)] * (2 * PIECES + 4),
        out_specs=[pl.BlockSpec(memory_space=pltpu.VMEM)] * (PIECES + 2),
        compiler_params=pltpu.CompilerParams(vmem_limit_bytes=24 * MIB),
        cost_estimate=pl.CostEstimate(
            flops=12 * PIECES * rows * hidden * width,
            bytes_accessed=6 * hidden * width,
            transcendentals=2 * PIECES * rows * hidden,
        ),
        name="expert",
    )(*streams, norm_gain[None], w_gate, w_up, w_down)


def swap(array, distance):
    pairs = [(at, at ^ distance) for at in range(lax.axis_size("experts"))]
    return lax.ppermute(array, "experts", pairs)


def wide(array):
    return array.astype(jnp.float32)


def collect(terms):
    *keeps, first, rest = terms
    rows = first.shape[0]
    rest = swap(rest, 1)
    others = [swap(first, 1)] + [
        rest[at * rows : (at + 1) * rows] for at in range(PIECES - 1)
    ]
    found = []
    for keep, other, distance in zip(keeps, others, SQUARE):
        part = keep + wide(other)
        if distance:
            part = swap(part.astype(jnp.bfloat16), distance)
        found.append(part)
    return found


def exchange(total, far):
    own_rows = total.shape[0] // far
    sent = total.astype(jnp.bfloat16)
    for at in range(1, far):
        block = swap(sent, 8 * at)
        total = total + wide(
            jnp.concatenate(
                [block[(to ^ at) * own_rows : ((to ^ at) + 1) * own_rows] for to in range(far)]
            )
        )
    return total.astype(jnp.bfloat16)


def spread(stream):
    own = [stream] + [swap(stream, distance) for distance in SQUARE if distance]
    return own + [swap(piece, 1) for piece in own]


def shards(
    queries,
    cache,
    cache_len,
    residual_in,
    w_absorb,
    w_out,
    norm_gain,
    expert_ids,
    route_gates,
    w_gate,
    w_up,
    w_down,
):
    devices = lax.axis_size("experts")
    rank_here = lax.axis_index("experts")
    own_rows = queries.shape[0]
    all_rows = expert_ids.shape[0]
    far = devices // 8
    split_ways = FF // w_gate.shape[1]
    assert split_ways == 8

    latent = attend(queries, cache, cache_len, devices, w_absorb.shape[1])
    joined = lax.all_to_all(latent, "experts", split_axis=0, concat_axis=0, tiled=True)
    joined = joined.reshape(-1, joined.shape[-1])
    terms = project(joined, w_absorb, residual_in, w_out, all_rows, far)
    stream = exchange(sum(wide(part) for part in collect(terms)), far)
    attended = stream[:own_rows]

    parts = collect(run_expert(spread(stream), norm_gain, w_gate, w_up, w_down))
    sent = [
        sum(wide(part[at * own_rows : (at + 1) * own_rows]) for part in parts).astype(
            jnp.bfloat16
        )
        for at in range(1, far)
    ]
    *sent, parts = lax.optimization_barrier((*sent, parts))
    own_ids = lax.dynamic_slice_in_dim(expert_ids, rank_here * own_rows, own_rows, 0)
    mixings = []
    for at in range(far):
        expert = (rank_here ^ (8 * at)) // split_ways
        mixings.append(
            jnp.sum(
                route_gates * (own_ids == expert).astype(jnp.float32), axis=1, keepdims=True
            )
        )
    kept = sum(wide(part[:own_rows]) for part in parts)
    expert_out = lax.optimization_barrier(mixings[0] * kept)
    for at in range(1, far):
        expert_out = expert_out + mixings[at] * wide(swap(sent[at - 1], 8 * at))
    return (attended, expert_out.astype(jnp.bfloat16))


def solution(mesh):
    placed = (
        P(("groups", "experts"), None, None),
        P(("groups", "experts"), None, None),
        P(("groups", "experts")),
        P(("groups", "experts"), None),
        P("experts", None, None),
        P("experts", None),
        P(),
        P("groups", None),
        P(("groups", "experts"), None),
        P(None, "experts"),
        P(None, "experts"),
        P("experts", None),
    )
    return jax.shard_map(
        shards,
        mesh=mesh,
        in_specs=placed,
        out_specs=(P(("groups", "experts"), None), P(("groups", "experts"), None)),
        check_vma=False,
    )
```

```python
import functools

import jax
import jax.numpy as jnp
from jax import lax
from jax.experimental import pallas as pl
from jax.experimental.pallas import tpu as pltpu
from jax.sharding import PartitionSpec as P

QK = 192
FF = 2048
BLOCK = 512
LOWEST = -3e38
GROUP = 4
LANES = 128
TILE = 256
PARTS = 4
SQUARE = (6, 4, 2, 0)
PIECES = len(SQUARE)
MIB = 2**20


def lane_tiles(array):
    return [array[:, at : at + LANES] for at in range(0, array.shape[1], LANES)]


def attend_kernel(
    len_ref,
    queries_ref,
    cache_ref,
    latent_ref,
    length,
    queries,
    held,
    summed,
    highest,
    sums,
    staged,
    item_row,
    item_block,
    length_arrived,
    queries_arrived,
    arrived,
):
    own_rows, heads, _ = queries.shape
    devices, _, rank = staged.shape
    own_heads = heads // devices
    blocks = held.shape[1]

    length_copy = pltpu.make_async_copy(len_ref, length, length_arrived)
    length_copy.start()
    queries_copy = pltpu.make_async_copy(queries_ref, queries, queries_arrived)
    queries_copy.start()

    def block_copy(row, block):
        return pltpu.make_async_copy(
            cache_ref.at[row, :, pl.ds(pl.multiple_of(block * BLOCK, BLOCK), BLOCK)],
            held.at[row, block],
            arrived.at[row, block],
        )

    for row in range(own_rows):
        block_copy(row, 0).start()
        item_row[row] = row
        item_block[row] = 0
    highest[...] = jnp.full_like(highest, LOWEST)
    sums[...] = jnp.zeros_like(sums)
    summed[...] = jnp.zeros_like(summed)
    length_copy.wait()
    items = own_rows
    for row in range(own_rows):
        count = (length[row] + BLOCK - 1) // BLOCK

        def begin(block, first, row=row):
            block_copy(row, block).start()
            item_row[first + block] = row
            item_block[first + block] = block
            return first

        lax.fori_loop(1, count, begin, items - 1)
        items = items + count - 1
    queries_copy.wait()
    column = lax.broadcasted_iota(jnp.int32, (heads, BLOCK), 1)

    def visit(first, many):
        inside = [(item_row[first + at], item_block[first + at]) for at in range(many)]
        for row, block in inside:
            block_copy(row, block).wait()
        found = []
        for row, block in inside:
            score = jnp.dot(
                queries[row], held[row, block], preferred_element_type=jnp.float32
            ) * QK ** (-0.5)
            found.append(
                jnp.where(column + block * BLOCK < length[row], score, -jnp.inf)
            )
        tops = [
            jnp.max(functools.reduce(jnp.maximum, lane_tiles(score)), axis=1, keepdims=True)
            for score in found
        ]
        weights = [jnp.exp(score - top) for score, top in zip(found, tops)]
        terms = [
            lax.dot_general(
                weight.astype(jnp.bfloat16),
                held[row, block, :rank, :],
                (((1,), (1,)), ((), ())),
                preferred_element_type=jnp.float32,
            )
            for (row, block), weight in zip(inside, weights)
        ]
        for (row, _), top, weight, term in zip(inside, tops, weights, terms):
            before = highest[row]
            after = jnp.maximum(before, top)
            old, new = jnp.exp(before - after), jnp.exp(top - after)
            highest[row] = after
            sums[row] = sums[row] * old + sum(lane_tiles(weight)) * new
            for at in range(0, rank, LANES):
                summed[row, :, at : at + LANES] = (
                    summed[row, :, at : at + LANES] * old + term[:, at : at + LANES] * new
                )

    def visit_group(group, _):
        visit(own_rows + group * GROUP, GROUP)
        return 0

    visit(0, own_rows)
    rest = items - own_rows
    lax.fori_loop(0, rest // GROUP, visit_group, 0)
    left = rest % GROUP
    for many in range(1, GROUP):
        pl.when(left == many)(functools.partial(visit, items - many, many))
    for row in range(own_rows):
        latent = summed[row] * (1.0 / jnp.sum(sums[row], axis=1, keepdims=True))
        for device in range(devices):
            staged[device, row * own_heads : (row + 1) * own_heads, :] = latent[
                device * own_heads : (device + 1) * own_heads
            ]
    latent_ref[...] = staged[...].astype(latent_ref.dtype)


def attend(queries, cache, cache_len, devices, rank):
    own_rows, depth, heads = queries.shape
    blocks = cache.shape[2] // BLOCK
    packed = own_rows * heads // devices
    listed = own_rows * blocks
    return pl.pallas_call(
        attend_kernel,
        out_shape=jax.ShapeDtypeStruct((devices, packed, rank), jnp.bfloat16),
        in_specs=[pl.BlockSpec(memory_space=pl.ANY)] * 3,
        out_specs=pl.BlockSpec(memory_space=pltpu.VMEM),
        scratch_shapes=[
            pltpu.SMEM((own_rows,), jnp.int32),
            pltpu.VMEM((own_rows, heads, depth), jnp.bfloat16),
            pltpu.VMEM((own_rows, blocks, depth, BLOCK), jnp.bfloat16),
            pltpu.VMEM((own_rows, heads, rank), jnp.float32),
            pltpu.VMEM((own_rows, heads, LANES), jnp.float32),
            pltpu.VMEM((own_rows, heads, LANES), jnp.float32),
            pltpu.VMEM((devices, packed, rank), jnp.float32),
            pltpu.SMEM((listed,), jnp.int32),
            pltpu.SMEM((listed,), jnp.int32),
            pltpu.SemaphoreType.DMA,
            pltpu.SemaphoreType.DMA,
            pltpu.SemaphoreType.DMA((own_rows, blocks)),
        ],
        compiler_params=pltpu.CompilerParams(vmem_limit_bytes=55 * MIB),
        cost_estimate=pl.CostEstimate(
            flops=own_rows * heads * cache.shape[2] * (depth + rank),
            bytes_accessed=cache.size,
            transcendentals=own_rows * heads * cache.shape[2],
        ),
        name="attend",
    )(cache_len, jnp.swapaxes(queries, 1, 2), cache)


def store_term(term, at, refs):
    first = 0
    for ref in refs:
        rows = ref.shape[0]
        ref[:, at : at + TILE] = term[first : first + rows].astype(ref.dtype)
        first += rows


def term_shapes(rows, width):
    kept = [jax.ShapeDtypeStruct((rows, width), jnp.float32)] * PIECES
    sent = [jax.ShapeDtypeStruct((many * rows, width), jnp.bfloat16) for many in (1, PIECES - 1)]
    return kept + sent


def project_kernel(own_rows, far, joined_ref, residual_ref, absorb_ref, w_ref, *pieces):
    own_heads = absorb_ref.shape[0]
    width = w_ref.shape[1]
    shape = (2 * PIECES * pieces[0].shape[0], joined_ref.shape[0])
    row = lax.broadcasted_iota(jnp.int32, shape, 0)
    place = lax.broadcasted_iota(jnp.int32, shape, 1)
    turn = own_rows.bit_length() - 1
    far_bits = far.bit_length() - 1
    request, slot = row & (own_rows - 1), row >> turn
    far_at, slot = slot & (far - 1), slot >> far_bits
    distance = (far_at << 3) + ((3 - (slot & 3)) << 1) + (slot >> 2)
    device = distance ^ lax.axis_index("experts")
    choices = []
    for head in range(own_heads):
        wanted = ((device << turn) + request) * own_heads + head
        choices.append((place == wanted).astype(jnp.float32))
    latents = jnp.dot(
        jnp.concatenate(choices, axis=0).astype(jnp.bfloat16),
        joined_ref[...],
        preferred_element_type=jnp.float32,
    ).astype(jnp.bfloat16)
    values = [
        jnp.dot(
            latents[head * shape[0] : (head + 1) * shape[0]],
            absorb_ref[head],
            preferred_element_type=jnp.float32,
        ).astype(jnp.bfloat16)
        for head in range(own_heads)
    ]
    values = jnp.concatenate(values, axis=1)
    for at in range(0, width, TILE):
        term = jnp.dot(values, w_ref[:, at : at + TILE], preferred_element_type=jnp.float32)
        store_term(term, at, pieces)
    residual = residual_ref[...].astype(jnp.float32)
    stays = pieces[PIECES - 1]
    stays[:own_rows, :] = stays[:own_rows, :] + residual


def project(joined, w_absorb, residual_in, w_out, rows, far):
    depth, width = w_out.shape
    own_rows = residual_in.shape[0]
    return pl.pallas_call(
        functools.partial(project_kernel, own_rows, far),
        out_shape=term_shapes(rows // (2 * PIECES), width),
        in_specs=[pl.BlockSpec(memory_space=pltpu.VMEM)] * 4,
        out_specs=[pl.BlockSpec(memory_space=pltpu.VMEM)] * (PIECES + 2),
        compiler_params=pltpu.CompilerParams(vmem_limit_bytes=24 * MIB),
        cost_estimate=pl.CostEstimate(
            flops=2 * rows * depth * width, bytes_accessed=2 * depth * width, transcendentals=0
        ),
        name="project",
    )(joined, residual_in, w_absorb, w_out)


def expert_kernel(*refs):
    count = 2 * PIECES
    streams, (gain_ref, gate_ref, up_ref, down_ref) = refs[:count], refs[count : count + 4]
    pieces = refs[count + 4 :]
    streams = streams[1:PIECES] + streams[:1] + streams[PIECES + 1 :] + streams[PIECES : PIECES + 1]
    width = gain_ref.shape[1]
    depth = width // PARTS
    inverses = []
    for stream in streams:
        squares = 0.0
        for at in range(0, width, depth):
            piece = stream[:, at : at + depth].astype(jnp.float32)
            squares = squares + sum(lane_tiles(piece * piece))
        mean = jnp.sum(squares, axis=1, keepdims=True) / width
        inverses.append(lax.rsqrt(mean + 1e-06))
    gate, up = 0.0, 0.0
    for at in range(0, width, depth):
        gain = gain_ref[:, at : at + depth]
        tokens = jnp.concatenate(
            [
                stream[:, at : at + depth].astype(jnp.float32) * inverse * gain
                for stream, inverse in zip(streams, inverses)
            ],
            axis=0,
        ).astype(jnp.bfloat16)
        gate = gate + jnp.dot(
            tokens, gate_ref[at : at + depth, :], preferred_element_type=jnp.float32
        )
        up = up + jnp.dot(
            tokens, up_ref[at : at + depth, :], preferred_element_type=jnp.float32
        )
    active = (gate / (1.0 + jnp.exp(-gate)) * up).astype(jnp.bfloat16)
    for at in range(0, width, TILE):
        term = jnp.dot(active, down_ref[:, at : at + TILE], preferred_element_type=jnp.float32)
        store_term(term, at, pieces)


def run_expert(streams, norm_gain, w_gate, w_up, w_down):
    rows, width = streams[0].shape
    hidden = w_gate.shape[1]
    return pl.pallas_call(
        expert_kernel,
        out_shape=term_shapes(rows, width),
        in_specs=[pl.BlockSpec(memory_space=pltpu.VMEM)] * (2 * PIECES + 4),
        out_specs=[pl.BlockSpec(memory_space=pltpu.VMEM)] * (PIECES + 2),
        compiler_params=pltpu.CompilerParams(vmem_limit_bytes=24 * MIB),
        cost_estimate=pl.CostEstimate(
            flops=12 * PIECES * rows * hidden * width,
            bytes_accessed=6 * hidden * width,
            transcendentals=2 * PIECES * rows * hidden,
        ),
        name="expert",
    )(*streams, norm_gain[None], w_gate, w_up, w_down)


def swap(array, distance):
    pairs = [(at, at ^ distance) for at in range(lax.axis_size("experts"))]
    return lax.ppermute(array, "experts", pairs)


def wide(array):
    return array.astype(jnp.float32)


def collect(terms):
    *keeps, first, rest = terms
    rows = first.shape[0]
    rest = swap(rest, 1)
    others = [swap(first, 1)] + [
        rest[at * rows : (at + 1) * rows] for at in range(PIECES - 1)
    ]
    found = []
    for keep, other, distance in zip(keeps, others, SQUARE):
        part = keep + wide(other)
        if distance:
            part = swap(part.astype(jnp.bfloat16), distance)
        found.append(part)
    return found


def exchange(total, far):
    own_rows = total.shape[0] // far
    sent = total.astype(jnp.bfloat16)
    for at in range(1, far):
        block = swap(sent, 8 * at)
        total = total + wide(
            jnp.concatenate(
                [block[(to ^ at) * own_rows : ((to ^ at) + 1) * own_rows] for to in range(far)]
            )
        )
    return total.astype(jnp.bfloat16)


def spread(stream):
    own = [stream] + [swap(stream, distance) for distance in SQUARE if distance]
    return own + [swap(piece, 1) for piece in own]


def shards(
    queries,
    cache,
    cache_len,
    residual_in,
    w_absorb,
    w_out,
    norm_gain,
    expert_ids,
    route_gates,
    w_gate,
    w_up,
    w_down,
):
    devices = lax.axis_size("experts")
    rank_here = lax.axis_index("experts")
    own_rows = queries.shape[0]
    all_rows = expert_ids.shape[0]
    far = devices // 8
    split_ways = FF // w_gate.shape[1]
    assert split_ways == 8

    latent = attend(queries, cache, cache_len, devices, w_absorb.shape[1])
    joined = lax.all_to_all(latent, "experts", split_axis=0, concat_axis=0, tiled=True)
    joined = joined.reshape(-1, joined.shape[-1])
    terms = project(joined, w_absorb, residual_in, w_out, all_rows, far)
    stream = exchange(sum(wide(part) for part in collect(terms)), far)
    attended = stream[:own_rows]

    parts = collect(run_expert(spread(stream), norm_gain, w_gate, w_up, w_down))
    sent = [
        sum(wide(part[at * own_rows : (at + 1) * own_rows]) for part in parts).astype(
            jnp.bfloat16
        )
        for at in range(1, far)
    ]
    *sent, parts = lax.optimization_barrier((*sent, parts))
    own_ids = lax.dynamic_slice_in_dim(expert_ids, rank_here * own_rows, own_rows, 0)
    mixings = []
    for at in range(far):
        expert = (rank_here ^ (8 * at)) // split_ways
        mixings.append(
            jnp.sum(
                route_gates * (own_ids == expert).astype(jnp.float32), axis=1, keepdims=True
            )
        )
    kept = sum(wide(part[:own_rows]) for part in parts)
    expert_out = lax.optimization_barrier(mixings[0] * kept)
    for at in range(1, far):
        expert_out = expert_out + mixings[at] * wide(swap(sent[at - 1], 8 * at))
    return (attended, expert_out.astype(jnp.bfloat16))


def solution(mesh):
    placed = (
        P(("groups", "experts"), None, None),
        P(("groups", "experts"), None, None),
        P(("groups", "experts")),
        P(("groups", "experts"), None),
        P("experts", None, None),
        P("experts", None),
        P(),
        P("groups", None),
        P(("groups", "experts"), None),
        P(None, "experts"),
        P(None, "experts"),
        P("experts", None),
    )
    return jax.shard_map(
        shards,
        mesh=mesh,
        in_specs=placed,
        out_specs=(P(("groups", "experts"), None), P(("groups", "experts"), None)),
        check_vma=False,
    )
```

```python
import functools

import jax
import jax.numpy as jnp
from jax import lax
from jax.experimental import pallas as pl
from jax.experimental.pallas import tpu as pltpu
from jax.sharding import PartitionSpec as P

QK = 192
FF = 2048
BLOCK = 512
LOWEST = -3e38
GROUP = 4
LANES = 128
TILE = 256
PARTS = 4
SQUARE = (6, 4, 2, 0)
PIECES = len(SQUARE)
MIB = 2**20


def lane_tiles(array):
    return [array[:, at : at + LANES] for at in range(0, array.shape[1], LANES)]


def attend_kernel(
    len_ref,
    queries_ref,
    cache_ref,
    latent_ref,
    length,
    queries,
    held,
    summed,
    highest,
    sums,
    staged,
    item_row,
    item_block,
    length_arrived,
    queries_arrived,
    arrived,
):
    own_rows, heads, _ = queries.shape
    devices, _, rank = staged.shape
    own_heads = heads // devices
    blocks = held.shape[1]

    length_copy = pltpu.make_async_copy(len_ref, length, length_arrived)
    length_copy.start()
    queries_copy = pltpu.make_async_copy(queries_ref, queries, queries_arrived)
    queries_copy.start()

    def block_copy(row, block):
        return pltpu.make_async_copy(
            cache_ref.at[row, :, pl.ds(pl.multiple_of(block * BLOCK, BLOCK), BLOCK)],
            held.at[row, block],
            arrived.at[row, block],
        )

    for row in range(own_rows):
        block_copy(row, 0).start()
        item_row[row] = row
        item_block[row] = 0
    highest[...] = jnp.full_like(highest, LOWEST)
    sums[...] = jnp.zeros_like(sums)
    summed[...] = jnp.zeros_like(summed)
    length_copy.wait()
    items = own_rows
    for row in range(own_rows):
        count = (length[row] + BLOCK - 1) // BLOCK

        def begin(block, first, row=row):
            block_copy(row, block).start()
            item_row[first + block] = row
            item_block[first + block] = block
            return first

        lax.fori_loop(1, count, begin, items - 1)
        items = items + count - 1
    queries_copy.wait()
    column = lax.broadcasted_iota(jnp.int32, (heads, BLOCK), 1)

    def visit(first, many):
        inside = [(item_row[first + at], item_block[first + at]) for at in range(many)]
        for row, block in inside:
            block_copy(row, block).wait()
        found = []
        for row, block in inside:
            score = jnp.dot(
                queries[row], held[row, block], preferred_element_type=jnp.float32
            ) * QK ** (-0.5)
            found.append(
                jnp.where(column + block * BLOCK < length[row], score, -jnp.inf)
            )
        tops = [
            jnp.max(functools.reduce(jnp.maximum, lane_tiles(score)), axis=1, keepdims=True)
            for score in found
        ]
        weights = [jnp.exp(score - top) for score, top in zip(found, tops)]
        terms = [
            lax.dot_general(
                weight.astype(jnp.bfloat16),
                held[row, block, :rank, :],
                (((1,), (1,)), ((), ())),
                preferred_element_type=jnp.float32,
            )
            for (row, block), weight in zip(inside, weights)
        ]
        for (row, _), top, weight, term in zip(inside, tops, weights, terms):
            before = highest[row]
            after = jnp.maximum(before, top)
            old, new = jnp.exp(before - after), jnp.exp(top - after)
            highest[row] = after
            sums[row] = sums[row] * old + sum(lane_tiles(weight)) * new
            for at in range(0, rank, LANES):
                summed[row, :, at : at + LANES] = (
                    summed[row, :, at : at + LANES] * old + term[:, at : at + LANES] * new
                )

    def visit_group(group, _):
        visit(own_rows + group * GROUP, GROUP)
        return 0

    visit(0, own_rows)
    rest = items - own_rows
    lax.fori_loop(0, rest // GROUP, visit_group, 0)
    left = rest % GROUP
    for many in range(1, GROUP):
        pl.when(left == many)(functools.partial(visit, items - many, many))
    for row in range(own_rows):
        latent = summed[row] * (1.0 / jnp.sum(sums[row], axis=1, keepdims=True))
        for device in range(devices):
            staged[device, row * own_heads : (row + 1) * own_heads, :] = latent[
                device * own_heads : (device + 1) * own_heads
            ]
    latent_ref[...] = staged[...].astype(latent_ref.dtype)


def attend(queries, cache, cache_len, devices, rank):
    own_rows, depth, heads = queries.shape
    blocks = cache.shape[2] // BLOCK
    packed = own_rows * heads // devices
    listed = own_rows * blocks
    return pl.pallas_call(
        attend_kernel,
        out_shape=jax.ShapeDtypeStruct((devices, packed, rank), jnp.bfloat16),
        in_specs=[pl.BlockSpec(memory_space=pl.ANY)] * 3,
        out_specs=pl.BlockSpec(memory_space=pltpu.VMEM),
        scratch_shapes=[
            pltpu.SMEM((own_rows,), jnp.int32),
            pltpu.VMEM((own_rows, heads, depth), jnp.bfloat16),
            pltpu.VMEM((own_rows, blocks, depth, BLOCK), jnp.bfloat16),
            pltpu.VMEM((own_rows, heads, rank), jnp.float32),
            pltpu.VMEM((own_rows, heads, LANES), jnp.float32),
            pltpu.VMEM((own_rows, heads, LANES), jnp.float32),
            pltpu.VMEM((devices, packed, rank), jnp.float32),
            pltpu.SMEM((listed,), jnp.int32),
            pltpu.SMEM((listed,), jnp.int32),
            pltpu.SemaphoreType.DMA,
            pltpu.SemaphoreType.DMA,
            pltpu.SemaphoreType.DMA((own_rows, blocks)),
        ],
        compiler_params=pltpu.CompilerParams(vmem_limit_bytes=107 * MIB // 2),
        cost_estimate=pl.CostEstimate(
            flops=own_rows * heads * cache.shape[2] * (depth + rank),
            bytes_accessed=cache.size,
            transcendentals=own_rows * heads * cache.shape[2],
        ),
        name="attend",
    )(cache_len, jnp.swapaxes(queries, 1, 2), cache)


def store_term(term, at, refs):
    first = 0
    for ref in refs:
        rows = ref.shape[0]
        ref[:, at : at + TILE] = term[first : first + rows].astype(ref.dtype)
        first += rows


def term_shapes(rows, width):
    kept = [jax.ShapeDtypeStruct((rows, width), jnp.float32)] * PIECES
    sent = [jax.ShapeDtypeStruct((many * rows, width), jnp.bfloat16) for many in (1, PIECES - 1)]
    return kept + sent


def project_kernel(own_rows, far, joined_ref, residual_ref, absorb_ref, w_ref, *pieces):
    own_heads = absorb_ref.shape[0]
    width = w_ref.shape[1]
    shape = (2 * PIECES * pieces[0].shape[0], joined_ref.shape[0])
    row = lax.broadcasted_iota(jnp.int32, shape, 0)
    place = lax.broadcasted_iota(jnp.int32, shape, 1)
    turn = own_rows.bit_length() - 1
    far_bits = far.bit_length() - 1
    request, slot = row & (own_rows - 1), row >> turn
    far_at, slot = slot & (far - 1), slot >> far_bits
    distance = (far_at << 3) + ((3 - (slot & 3)) << 1) + (slot >> 2)
    device = distance ^ lax.axis_index("experts")
    choices = []
    for head in range(own_heads):
        wanted = ((device << turn) + request) * own_heads + head
        choices.append((place == wanted).astype(jnp.float32))
    latents = jnp.dot(
        jnp.concatenate(choices, axis=0).astype(jnp.bfloat16),
        joined_ref[...],
        preferred_element_type=jnp.float32,
    ).astype(jnp.bfloat16)
    values = [
        jnp.dot(
            latents[head * shape[0] : (head + 1) * shape[0]],
            absorb_ref[head],
            preferred_element_type=jnp.float32,
        ).astype(jnp.bfloat16)
        for head in range(own_heads)
    ]
    values = jnp.concatenate(values, axis=1)
    for at in range(0, width, TILE):
        term = jnp.dot(values, w_ref[:, at : at + TILE], preferred_element_type=jnp.float32)
        store_term(term, at, pieces)
    residual = residual_ref[...].astype(jnp.float32)
    stays = pieces[PIECES - 1]
    stays[:own_rows, :] = stays[:own_rows, :] + residual


def project(joined, w_absorb, residual_in, w_out, rows, far):
    depth, width = w_out.shape
    own_rows = residual_in.shape[0]
    return pl.pallas_call(
        functools.partial(project_kernel, own_rows, far),
        out_shape=term_shapes(rows // (2 * PIECES), width),
        in_specs=[pl.BlockSpec(memory_space=pltpu.VMEM)] * 4,
        out_specs=[pl.BlockSpec(memory_space=pltpu.VMEM)] * (PIECES + 2),
        compiler_params=pltpu.CompilerParams(vmem_limit_bytes=24 * MIB),
        cost_estimate=pl.CostEstimate(
            flops=2 * rows * depth * width, bytes_accessed=2 * depth * width, transcendentals=0
        ),
        name="project",
    )(joined, residual_in, w_absorb, w_out)


def expert_kernel(*refs):
    count = 2 * PIECES
    streams, (gain_ref, gate_ref, up_ref, down_ref) = refs[:count], refs[count : count + 4]
    pieces = refs[count + 4 :]
    streams = streams[1:PIECES] + streams[:1] + streams[PIECES + 1 :] + streams[PIECES : PIECES + 1]
    width = gain_ref.shape[1]
    depth = width // PARTS
    inverses = []
    for stream in streams:
        squares = 0.0
        for at in range(0, width, depth):
            piece = stream[:, at : at + depth].astype(jnp.float32)
            squares = squares + sum(lane_tiles(piece * piece))
        mean = jnp.sum(squares, axis=1, keepdims=True) / width
        inverses.append(lax.rsqrt(mean + 1e-06))
    gate, up = 0.0, 0.0
    for at in range(0, width, depth):
        gain = gain_ref[:, at : at + depth]
        tokens = jnp.concatenate(
            [
                stream[:, at : at + depth].astype(jnp.float32) * inverse * gain
                for stream, inverse in zip(streams, inverses)
            ],
            axis=0,
        ).astype(jnp.bfloat16)
        gate = gate + jnp.dot(
            tokens, gate_ref[at : at + depth, :], preferred_element_type=jnp.float32
        )
        up = up + jnp.dot(
            tokens, up_ref[at : at + depth, :], preferred_element_type=jnp.float32
        )
    active = (gate / (1.0 + jnp.exp(-gate)) * up).astype(jnp.bfloat16)
    for at in range(0, width, TILE):
        term = jnp.dot(active, down_ref[:, at : at + TILE], preferred_element_type=jnp.float32)
        store_term(term, at, pieces)


def run_expert(streams, norm_gain, w_gate, w_up, w_down):
    rows, width = streams[0].shape
    hidden = w_gate.shape[1]
    return pl.pallas_call(
        expert_kernel,
        out_shape=term_shapes(rows, width),
        in_specs=[pl.BlockSpec(memory_space=pltpu.VMEM)] * (2 * PIECES + 4),
        out_specs=[pl.BlockSpec(memory_space=pltpu.VMEM)] * (PIECES + 2),
        compiler_params=pltpu.CompilerParams(vmem_limit_bytes=24 * MIB),
        cost_estimate=pl.CostEstimate(
            flops=12 * PIECES * rows * hidden * width,
            bytes_accessed=6 * hidden * width,
            transcendentals=2 * PIECES * rows * hidden,
        ),
        name="expert",
    )(*streams, norm_gain[None], w_gate, w_up, w_down)


def swap(array, distance):
    pairs = [(at, at ^ distance) for at in range(lax.axis_size("experts"))]
    return lax.ppermute(array, "experts", pairs)


def wide(array):
    return array.astype(jnp.float32)


def collect(terms):
    *keeps, first, rest = terms
    rows = first.shape[0]
    rest = swap(rest, 1)
    others = [swap(first, 1)] + [
        rest[at * rows : (at + 1) * rows] for at in range(PIECES - 1)
    ]
    found = []
    for keep, other, distance in zip(keeps, others, SQUARE):
        part = keep + wide(other)
        if distance:
            part = swap(part.astype(jnp.bfloat16), distance)
        found.append(part)
    return found


def exchange(total, far):
    own_rows = total.shape[0] // far
    sent = total.astype(jnp.bfloat16)
    for at in range(1, far):
        block = swap(sent, 8 * at)
        total = total + wide(
            jnp.concatenate(
                [block[(to ^ at) * own_rows : ((to ^ at) + 1) * own_rows] for to in range(far)]
            )
        )
    return total.astype(jnp.bfloat16)


def spread(stream):
    own = [stream] + [swap(stream, distance) for distance in SQUARE if distance]
    return own + [swap(piece, 1) for piece in own]


def shards(
    queries,
    cache,
    cache_len,
    residual_in,
    w_absorb,
    w_out,
    norm_gain,
    expert_ids,
    route_gates,
    w_gate,
    w_up,
    w_down,
):
    devices = lax.axis_size("experts")
    rank_here = lax.axis_index("experts")
    own_rows = queries.shape[0]
    all_rows = expert_ids.shape[0]
    far = devices // 8
    split_ways = FF // w_gate.shape[1]
    assert split_ways == 8

    latent = attend(queries, cache, cache_len, devices, w_absorb.shape[1])
    joined = lax.all_to_all(latent, "experts", split_axis=0, concat_axis=0, tiled=True)
    joined = joined.reshape(-1, joined.shape[-1])
    terms = project(joined, w_absorb, residual_in, w_out, all_rows, far)
    stream = exchange(sum(wide(part) for part in collect(terms)), far)
    attended = stream[:own_rows]

    parts = collect(run_expert(spread(stream), norm_gain, w_gate, w_up, w_down))
    sent = [
        sum(wide(part[at * own_rows : (at + 1) * own_rows]) for part in parts).astype(
            jnp.bfloat16
        )
        for at in range(1, far)
    ]
    *sent, parts = lax.optimization_barrier((*sent, parts))
    own_ids = lax.dynamic_slice_in_dim(expert_ids, rank_here * own_rows, own_rows, 0)
    mixings = []
    for at in range(far):
        expert = (rank_here ^ (8 * at)) // split_ways
        mixings.append(
            jnp.sum(
                route_gates * (own_ids == expert).astype(jnp.float32), axis=1, keepdims=True
            )
        )
    kept = sum(wide(part[:own_rows]) for part in parts)
    expert_out = lax.optimization_barrier(mixings[0] * kept)
    for at in range(1, far):
        expert_out = expert_out + mixings[at] * wide(swap(sent[at - 1], 8 * at))
    return (attended, expert_out.astype(jnp.bfloat16))


def solution(mesh):
    placed = (
        P(("groups", "experts"), None, None),
        P(("groups", "experts"), None, None),
        P(("groups", "experts")),
        P(("groups", "experts"), None),
        P("experts", None, None),
        P("experts", None),
        P(),
        P("groups", None),
        P(("groups", "experts"), None),
        P(None, "experts"),
        P(None, "experts"),
        P("experts", None),
    )
    return jax.shard_map(
        shards,
        mesh=mesh,
        in_specs=placed,
        out_specs=(P(("groups", "experts"), None), P(("groups", "experts"), None)),
        check_vma=False,
    )
```

```python
import functools

import jax
import jax.numpy as jnp
from jax import lax
from jax.experimental import pallas as pl
from jax.experimental.pallas import tpu as pltpu
from jax.sharding import PartitionSpec as P

QK = 192
FF = 2048
BLOCK = 512
LOWEST = -3e38
GROUP = 4
LANES = 128
TILE = 256
PARTS = 4
SQUARE = (6, 4, 2, 0)
PIECES = len(SQUARE)
MIB = 2**20


def lane_tiles(array):
    return [array[:, at : at + LANES] for at in range(0, array.shape[1], LANES)]


def attend_kernel(
    len_ref,
    queries_ref,
    cache_ref,
    latent_ref,
    length,
    queries,
    held,
    summed,
    highest,
    sums,
    staged,
    item_row,
    item_block,
    length_arrived,
    queries_arrived,
    arrived,
):
    own_rows, heads, _ = queries.shape
    devices, _, rank = staged.shape
    own_heads = heads // devices
    blocks = held.shape[1]

    length_copy = pltpu.make_async_copy(len_ref, length, length_arrived)
    length_copy.start()
    queries_copy = pltpu.make_async_copy(queries_ref, queries, queries_arrived)
    queries_copy.start()

    def block_copy(row, block):
        return pltpu.make_async_copy(
            cache_ref.at[row, :, pl.ds(pl.multiple_of(block * BLOCK, BLOCK), BLOCK)],
            held.at[row, block],
            arrived.at[row, block],
        )

    for row in range(own_rows):
        block_copy(row, 0).start()
        item_row[row] = row
        item_block[row] = 0
    highest[...] = jnp.full_like(highest, LOWEST)
    sums[...] = jnp.zeros_like(sums)
    summed[...] = jnp.zeros_like(summed)
    length_copy.wait()
    items = own_rows
    for row in range(own_rows):
        count = (length[row] + BLOCK - 1) // BLOCK

        def begin(block, first, row=row):
            block_copy(row, block).start()
            item_row[first + block] = row
            item_block[first + block] = block
            return first

        lax.fori_loop(1, count, begin, items - 1)
        items = items + count - 1
    queries_copy.wait()
    column = lax.broadcasted_iota(jnp.int32, (heads, BLOCK), 1)

    def visit(first, many):
        inside = [(item_row[first + at], item_block[first + at]) for at in range(many)]
        for row, block in inside:
            block_copy(row, block).wait()
        found = []
        for row, block in inside:
            score = jnp.dot(
                queries[row], held[row, block], preferred_element_type=jnp.float32
            ) * QK ** (-0.5)
            found.append(
                jnp.where(column + block * BLOCK < length[row], score, -jnp.inf)
            )
        tops = [
            jnp.max(functools.reduce(jnp.maximum, lane_tiles(score)), axis=1, keepdims=True)
            for score in found
        ]
        weights = [jnp.exp(score - top) for score, top in zip(found, tops)]
        terms = [
            lax.dot_general(
                weight.astype(jnp.bfloat16),
                held[row, block, :rank, :],
                (((1,), (1,)), ((), ())),
                preferred_element_type=jnp.float32,
            )
            for (row, block), weight in zip(inside, weights)
        ]
        for (row, _), top, weight, term in zip(inside, tops, weights, terms):
            before = highest[row]
            after = jnp.maximum(before, top)
            old, new = jnp.exp(before - after), jnp.exp(top - after)
            highest[row] = after
            sums[row] = sums[row] * old + sum(lane_tiles(weight)) * new
            for at in range(0, rank, LANES):
                summed[row, :, at : at + LANES] = (
                    summed[row, :, at : at + LANES] * old + term[:, at : at + LANES] * new
                )

    def visit_group(group, _):
        visit(own_rows + group * GROUP, GROUP)
        return 0

    visit(0, own_rows)
    rest = items - own_rows
    lax.fori_loop(0, rest // GROUP, visit_group, 0)
    left = rest % GROUP
    for many in range(1, GROUP):
        pl.when(left == many)(functools.partial(visit, items - many, many))
    for row in range(own_rows):
        latent = summed[row] * (1.0 / jnp.sum(sums[row], axis=1, keepdims=True))
        for device in range(devices):
            staged[device, row * own_heads : (row + 1) * own_heads, :] = latent[
                device * own_heads : (device + 1) * own_heads
            ]
    latent_ref[...] = staged[...].astype(latent_ref.dtype)


def attend(queries, cache, cache_len, devices, rank):
    own_rows, depth, heads = queries.shape
    blocks = cache.shape[2] // BLOCK
    packed = own_rows * heads // devices
    listed = own_rows * blocks
    return pl.pallas_call(
        attend_kernel,
        out_shape=jax.ShapeDtypeStruct((devices, packed, rank), jnp.bfloat16),
        in_specs=[pl.BlockSpec(memory_space=pl.ANY)] * 3,
        out_specs=pl.BlockSpec(memory_space=pltpu.VMEM),
        scratch_shapes=[
            pltpu.SMEM((own_rows,), jnp.int32),
            pltpu.VMEM((own_rows, heads, depth), jnp.bfloat16),
            pltpu.VMEM((own_rows, blocks, depth, BLOCK), jnp.bfloat16),
            pltpu.VMEM((own_rows, heads, rank), jnp.float32),
            pltpu.VMEM((own_rows, heads, LANES), jnp.float32),
            pltpu.VMEM((own_rows, heads, LANES), jnp.float32),
            pltpu.VMEM((devices, packed, rank), jnp.float32),
            pltpu.SMEM((listed,), jnp.int32),
            pltpu.SMEM((listed,), jnp.int32),
            pltpu.SemaphoreType.DMA,
            pltpu.SemaphoreType.DMA,
            pltpu.SemaphoreType.DMA((own_rows, blocks)),
        ],
        compiler_params=pltpu.CompilerParams(vmem_limit_bytes=55 * MIB),
        cost_estimate=pl.CostEstimate(
            flops=own_rows * heads * cache.shape[2] * (depth + rank),
            bytes_accessed=cache.size,
            transcendentals=own_rows * heads * cache.shape[2],
        ),
        name="attend",
    )(cache_len, jnp.swapaxes(queries, 1, 2), cache)


def store_term(term, at, refs):
    first = 0
    for ref in refs:
        rows = ref.shape[0]
        ref[:, at : at + TILE] = term[first : first + rows].astype(ref.dtype)
        first += rows


def term_shapes(rows, width):
    kept = [jax.ShapeDtypeStruct((rows, width), jnp.float32)] * PIECES
    sent = [jax.ShapeDtypeStruct((many * rows, width), jnp.bfloat16) for many in (1, PIECES - 1)]
    return kept + sent


def project_kernel(own_rows, far, joined_ref, residual_ref, absorb_ref, w_ref, *pieces):
    own_heads = absorb_ref.shape[0]
    width = w_ref.shape[1]
    shape = (2 * PIECES * pieces[0].shape[0], joined_ref.shape[0])
    row = lax.broadcasted_iota(jnp.int32, shape, 0)
    place = lax.broadcasted_iota(jnp.int32, shape, 1)
    turn = own_rows.bit_length() - 1
    far_bits = far.bit_length() - 1
    request, slot = row & (own_rows - 1), row >> turn
    far_at, slot = slot & (far - 1), slot >> far_bits
    distance = (far_at << 3) + ((3 - (slot & 3)) << 1) + (slot >> 2)
    device = distance ^ lax.axis_index("experts")
    choices = []
    for head in range(own_heads):
        wanted = ((device << turn) + request) * own_heads + head
        choices.append((place == wanted).astype(jnp.float32))
    latents = jnp.dot(
        jnp.concatenate(choices, axis=0).astype(jnp.bfloat16),
        joined_ref[...],
        preferred_element_type=jnp.float32,
    ).astype(jnp.bfloat16)
    values = [
        jnp.dot(
            latents[head * shape[0] : (head + 1) * shape[0]],
            absorb_ref[head],
            preferred_element_type=jnp.float32,
        ).astype(jnp.bfloat16)
        for head in range(own_heads)
    ]
    values = jnp.concatenate(values, axis=1)
    for at in range(0, width, TILE):
        term = jnp.dot(values, w_ref[:, at : at + TILE], preferred_element_type=jnp.float32)
        store_term(term, at, pieces)
    residual = residual_ref[...].astype(jnp.float32)
    stays = pieces[PIECES - 1]
    stays[:own_rows, :] = stays[:own_rows, :] + residual


def project(joined, w_absorb, residual_in, w_out, rows, far):
    depth, width = w_out.shape
    own_rows = residual_in.shape[0]
    return pl.pallas_call(
        functools.partial(project_kernel, own_rows, far),
        out_shape=term_shapes(rows // (2 * PIECES), width),
        in_specs=[pl.BlockSpec(memory_space=pltpu.VMEM)] * 4,
        out_specs=[pl.BlockSpec(memory_space=pltpu.VMEM)] * (PIECES + 2),
        compiler_params=pltpu.CompilerParams(vmem_limit_bytes=24 * MIB),
        cost_estimate=pl.CostEstimate(
            flops=2 * rows * depth * width, bytes_accessed=2 * depth * width, transcendentals=0
        ),
        name="project",
    )(joined, residual_in, w_absorb, w_out)


def expert_kernel(*refs):
    count = 2 * PIECES
    streams, (gain_ref, gate_ref, up_ref, down_ref) = refs[:count], refs[count : count + 4]
    pieces = refs[count + 4 :]
    streams = streams[1:PIECES] + streams[:1] + streams[PIECES + 1 :] + streams[PIECES : PIECES + 1]
    width = gain_ref.shape[1]
    depth = width // PARTS
    inverses = []
    for stream in streams:
        squares = 0.0
        for at in range(0, width, depth):
            piece = stream[:, at : at + depth].astype(jnp.float32)
            squares = squares + sum(lane_tiles(piece * piece))
        mean = jnp.sum(squares, axis=1, keepdims=True) / width
        inverses.append(lax.rsqrt(mean + 1e-06))
    gate, up = 0.0, 0.0
    for at in range(0, width, depth):
        gain = gain_ref[:, at : at + depth]
        tokens = jnp.concatenate(
            [
                stream[:, at : at + depth].astype(jnp.float32) * inverse * gain
                for stream, inverse in zip(streams, inverses)
            ],
            axis=0,
        ).astype(jnp.bfloat16)
        gate = gate + jnp.dot(
            tokens, gate_ref[at : at + depth, :], preferred_element_type=jnp.float32
        )
        up = up + jnp.dot(
            tokens, up_ref[at : at + depth, :], preferred_element_type=jnp.float32
        )
    active = (gate / (1.0 + jnp.exp(-gate)) * up).astype(jnp.bfloat16)
    for at in range(0, width, TILE):
        term = jnp.dot(active, down_ref[:, at : at + TILE], preferred_element_type=jnp.float32)
        store_term(term, at, pieces)


def run_expert(streams, norm_gain, w_gate, w_up, w_down):
    rows, width = streams[0].shape
    hidden = w_gate.shape[1]
    return pl.pallas_call(
        expert_kernel,
        out_shape=term_shapes(rows, width),
        in_specs=[pl.BlockSpec(memory_space=pltpu.VMEM)] * (2 * PIECES + 4),
        out_specs=[pl.BlockSpec(memory_space=pltpu.VMEM)] * (PIECES + 2),
        compiler_params=pltpu.CompilerParams(vmem_limit_bytes=24 * MIB),
        cost_estimate=pl.CostEstimate(
            flops=12 * PIECES * rows * hidden * width,
            bytes_accessed=6 * hidden * width,
            transcendentals=2 * PIECES * rows * hidden,
        ),
        name="expert",
    )(*streams, norm_gain[None], w_gate, w_up, w_down)


def swap(array, distance):
    pairs = [(at, at ^ distance) for at in range(lax.axis_size("experts"))]
    return lax.ppermute(array, "experts", pairs)


def wide(array):
    return array.astype(jnp.float32)


def collect(terms):
    *keeps, first, rest = terms
    rows = first.shape[0]
    rest = swap(rest, 1)
    others = [swap(first, 1)] + [
        rest[at * rows : (at + 1) * rows] for at in range(PIECES - 1)
    ]
    total = 0.0
    for keep, other, distance in zip(keeps, others, SQUARE):
        part = keep + wide(other)
        if distance:
            part = wide(swap(part.astype(jnp.bfloat16), distance))
        total = total + part
    return total


def exchange(total, far):
    own_rows = total.shape[0] // far
    sent = total.astype(jnp.bfloat16)
    for at in range(1, far):
        block = swap(sent, 8 * at)
        total = total + wide(
            jnp.concatenate(
                [block[(to ^ at) * own_rows : ((to ^ at) + 1) * own_rows] for to in range(far)]
            )
        )
    return total.astype(jnp.bfloat16)


def spread(stream):
    own = [stream] + [swap(stream, distance) for distance in SQUARE if distance]
    return own + [swap(piece, 1) for piece in own]


def shards(
    queries,
    cache,
    cache_len,
    residual_in,
    w_absorb,
    w_out,
    norm_gain,
    expert_ids,
    route_gates,
    w_gate,
    w_up,
    w_down,
):
    devices = lax.axis_size("experts")
    rank_here = lax.axis_index("experts")
    own_rows = queries.shape[0]
    all_rows = expert_ids.shape[0]
    far = devices // 8
    split_ways = FF // w_gate.shape[1]
    assert split_ways == 8

    latent = attend(queries, cache, cache_len, devices, w_absorb.shape[1])
    joined = lax.all_to_all(latent, "experts", split_axis=0, concat_axis=0, tiled=True)
    joined = joined.reshape(-1, joined.shape[-1])
    terms = project(joined, w_absorb, residual_in, w_out, all_rows, far)
    stream = exchange(collect(terms), far)
    attended = stream[:own_rows]

    total = collect(run_expert(spread(stream), norm_gain, w_gate, w_up, w_down))
    own_ids = lax.dynamic_slice_in_dim(expert_ids, rank_here * own_rows, own_rows, 0)
    mixings = []
    for at in range(far):
        expert = (rank_here ^ (8 * at)) // split_ways
        mixings.append(
            jnp.sum(
                route_gates * (own_ids == expert).astype(jnp.float32), axis=1, keepdims=True
            )
        )
    expert_out = lax.optimization_barrier(mixings[0] * total[:own_rows])
    for at in range(1, far):
        block = total[at * own_rows : (at + 1) * own_rows].astype(jnp.bfloat16)
        expert_out = expert_out + mixings[at] * wide(swap(block, 8 * at))
    return (attended, expert_out.astype(jnp.bfloat16))


def solution(mesh):
    placed = (
        P(("groups", "experts"), None, None),
        P(("groups", "experts"), None, None),
        P(("groups", "experts")),
        P(("groups", "experts"), None),
        P("experts", None, None),
        P("experts", None),
        P(),
        P("groups", None),
        P(("groups", "experts"), None),
        P(None, "experts"),
        P(None, "experts"),
        P("experts", None),
    )
    return jax.shard_map(
        shards,
        mesh=mesh,
        in_specs=placed,
        out_specs=(P(("groups", "experts"), None), P(("groups", "experts"), None)),
        check_vma=False,
    )
```

```python
import functools

import jax
import jax.numpy as jnp
from jax import lax
from jax.experimental import pallas as pl
from jax.experimental.pallas import tpu as pltpu
from jax.sharding import PartitionSpec as P

QK = 192
FF = 2048
BLOCK = 512
LOWEST = -3e38
GROUP = 4
LANES = 128
TILE = 256
PARTS = 4
SQUARE = (6, 4, 2, 0)
PIECES = len(SQUARE)
MIB = 2**20


def lane_tiles(array):
    return [array[:, at : at + LANES] for at in range(0, array.shape[1], LANES)]


def attend_kernel(
    len_ref,
    queries_ref,
    cache_ref,
    latent_ref,
    length,
    queries,
    held,
    summed,
    highest,
    sums,
    staged,
    item_row,
    item_block,
    length_arrived,
    queries_arrived,
    arrived,
):
    own_rows, heads, _ = queries.shape
    devices, _, rank = staged.shape
    own_heads = heads // devices
    blocks = held.shape[1]

    length_copy = pltpu.make_async_copy(len_ref, length, length_arrived)
    length_copy.start()
    queries_copy = pltpu.make_async_copy(queries_ref, queries, queries_arrived)
    queries_copy.start()

    def block_copy(row, block):
        return pltpu.make_async_copy(
            cache_ref.at[row, :, pl.ds(pl.multiple_of(block * BLOCK, BLOCK), BLOCK)],
            held.at[row, block],
            arrived.at[row, block],
        )

    for row in range(own_rows):
        block_copy(row, 0).start()
        item_row[row] = row
        item_block[row] = 0
    highest[...] = jnp.full_like(highest, LOWEST)
    sums[...] = jnp.zeros_like(sums)
    summed[...] = jnp.zeros_like(summed)
    length_copy.wait()
    items = own_rows
    for row in range(own_rows):
        count = (length[row] + BLOCK - 1) // BLOCK

        def begin(block, first, row=row):
            block_copy(row, block).start()
            item_row[first + block] = row
            item_block[first + block] = block
            return first

        lax.fori_loop(1, count, begin, items - 1)
        items = items + count - 1
    queries_copy.wait()
    column = lax.broadcasted_iota(jnp.int32, (heads, BLOCK), 1)

    def visit(first, many):
        inside = [(item_row[first + at], item_block[first + at]) for at in range(many)]
        for row, block in inside:
            block_copy(row, block).wait()
        found = []
        for row, block in inside:
            score = jnp.dot(
                queries[row], held[row, block], preferred_element_type=jnp.float32
            ) * QK ** (-0.5)
            found.append(
                jnp.where(column + block * BLOCK < length[row], score, -jnp.inf)
            )
        tops = [
            jnp.max(functools.reduce(jnp.maximum, lane_tiles(score)), axis=1, keepdims=True)
            for score in found
        ]
        weights = [jnp.exp(score - top) for score, top in zip(found, tops)]
        terms = [
            lax.dot_general(
                weight.astype(jnp.bfloat16),
                held[row, block, :rank, :],
                (((1,), (1,)), ((), ())),
                preferred_element_type=jnp.float32,
            )
            for (row, block), weight in zip(inside, weights)
        ]
        for (row, _), top, weight, term in zip(inside, tops, weights, terms):
            before = highest[row]
            after = jnp.maximum(before, top)
            old, new = jnp.exp(before - after), jnp.exp(top - after)
            highest[row] = after
            sums[row] = sums[row] * old + sum(lane_tiles(weight)) * new
            for at in range(0, rank, LANES):
                summed[row, :, at : at + LANES] = (
                    summed[row, :, at : at + LANES] * old + term[:, at : at + LANES] * new
                )

    def visit_group(group, _):
        visit(own_rows + group * GROUP, GROUP)
        return 0

    visit(0, own_rows // 2)
    visit(own_rows // 2, own_rows - own_rows // 2)
    rest = items - own_rows
    lax.fori_loop(0, rest // GROUP, visit_group, 0)
    left = rest % GROUP
    for many in range(1, GROUP):
        pl.when(left == many)(functools.partial(visit, items - many, many))
    for row in range(own_rows):
        latent = summed[row] * (1.0 / jnp.sum(sums[row], axis=1, keepdims=True))
        for device in range(devices):
            staged[device, row * own_heads : (row + 1) * own_heads, :] = latent[
                device * own_heads : (device + 1) * own_heads
            ]
    latent_ref[...] = staged[...].astype(latent_ref.dtype)


def attend(queries, cache, cache_len, devices, rank):
    own_rows, depth, heads = queries.shape
    blocks = cache.shape[2] // BLOCK
    packed = own_rows * heads // devices
    listed = own_rows * blocks
    return pl.pallas_call(
        attend_kernel,
        out_shape=jax.ShapeDtypeStruct((devices, packed, rank), jnp.bfloat16),
        in_specs=[pl.BlockSpec(memory_space=pl.ANY)] * 3,
        out_specs=pl.BlockSpec(memory_space=pltpu.VMEM),
        scratch_shapes=[
            pltpu.SMEM((own_rows,), jnp.int32),
            pltpu.VMEM((own_rows, heads, depth), jnp.bfloat16),
            pltpu.VMEM((own_rows, blocks, depth, BLOCK), jnp.bfloat16),
            pltpu.VMEM((own_rows, heads, rank), jnp.float32),
            pltpu.VMEM((own_rows, heads, LANES), jnp.float32),
            pltpu.VMEM((own_rows, heads, LANES), jnp.float32),
            pltpu.VMEM((devices, packed, rank), jnp.float32),
            pltpu.SMEM((listed,), jnp.int32),
            pltpu.SMEM((listed,), jnp.int32),
            pltpu.SemaphoreType.DMA,
            pltpu.SemaphoreType.DMA,
            pltpu.SemaphoreType.DMA((own_rows, blocks)),
        ],
        compiler_params=pltpu.CompilerParams(vmem_limit_bytes=55 * MIB),
        cost_estimate=pl.CostEstimate(
            flops=own_rows * heads * cache.shape[2] * (depth + rank),
            bytes_accessed=cache.size,
            transcendentals=own_rows * heads * cache.shape[2],
        ),
        name="attend",
    )(cache_len, jnp.swapaxes(queries, 1, 2), cache)


def store_term(term, at, refs):
    first = 0
    for ref in refs:
        rows = ref.shape[0]
        ref[:, at : at + TILE] = term[first : first + rows].astype(ref.dtype)
        first += rows


def term_shapes(rows, width):
    kept = [jax.ShapeDtypeStruct((rows, width), jnp.float32)] * PIECES
    sent = [jax.ShapeDtypeStruct((many * rows, width), jnp.bfloat16) for many in (1, PIECES - 1)]
    return kept + sent


def project_kernel(own_rows, far, joined_ref, residual_ref, absorb_ref, w_ref, *pieces):
    own_heads = absorb_ref.shape[0]
    width = w_ref.shape[1]
    shape = (2 * PIECES * pieces[0].shape[0], joined_ref.shape[0])
    row = lax.broadcasted_iota(jnp.int32, shape, 0)
    place = lax.broadcasted_iota(jnp.int32, shape, 1)
    turn = own_rows.bit_length() - 1
    far_bits = far.bit_length() - 1
    request, slot = row & (own_rows - 1), row >> turn
    far_at, slot = slot & (far - 1), slot >> far_bits
    distance = (far_at << 3) + ((3 - (slot & 3)) << 1) + (slot >> 2)
    device = distance ^ lax.axis_index("experts")
    choices = []
    for head in range(own_heads):
        wanted = ((device << turn) + request) * own_heads + head
        choices.append((place == wanted).astype(jnp.float32))
    latents = jnp.dot(
        jnp.concatenate(choices, axis=0).astype(jnp.bfloat16),
        joined_ref[...],
        preferred_element_type=jnp.float32,
    ).astype(jnp.bfloat16)
    values = [
        jnp.dot(
            latents[head * shape[0] : (head + 1) * shape[0]],
            absorb_ref[head],
            preferred_element_type=jnp.float32,
        ).astype(jnp.bfloat16)
        for head in range(own_heads)
    ]
    values = jnp.concatenate(values, axis=1)
    for at in range(0, width, TILE):
        term = jnp.dot(values, w_ref[:, at : at + TILE], preferred_element_type=jnp.float32)
        store_term(term, at, pieces)
    residual = residual_ref[...].astype(jnp.float32)
    stays = pieces[PIECES - 1]
    stays[:own_rows, :] = stays[:own_rows, :] + residual


def project(joined, w_absorb, residual_in, w_out, rows, far):
    depth, width = w_out.shape
    own_rows = residual_in.shape[0]
    return pl.pallas_call(
        functools.partial(project_kernel, own_rows, far),
        out_shape=term_shapes(rows // (2 * PIECES), width),
        in_specs=[pl.BlockSpec(memory_space=pltpu.VMEM)] * 4,
        out_specs=[pl.BlockSpec(memory_space=pltpu.VMEM)] * (PIECES + 2),
        compiler_params=pltpu.CompilerParams(vmem_limit_bytes=24 * MIB),
        cost_estimate=pl.CostEstimate(
            flops=2 * rows * depth * width, bytes_accessed=2 * depth * width, transcendentals=0
        ),
        name="project",
    )(joined, residual_in, w_absorb, w_out)


def expert_kernel(*refs):
    count = 2 * PIECES
    streams, (gain_ref, gate_ref, up_ref, down_ref) = refs[:count], refs[count : count + 4]
    pieces = refs[count + 4 :]
    streams = streams[1:PIECES] + streams[:1] + streams[PIECES + 1 :] + streams[PIECES : PIECES + 1]
    width = gain_ref.shape[1]
    depth = width // PARTS
    inverses = []
    for stream in streams:
        squares = 0.0
        for at in range(0, width, depth):
            piece = stream[:, at : at + depth].astype(jnp.float32)
            squares = squares + sum(lane_tiles(piece * piece))
        mean = jnp.sum(squares, axis=1, keepdims=True) / width
        inverses.append(lax.rsqrt(mean + 1e-06))
    gate, up = 0.0, 0.0
    for at in range(0, width, depth):
        gain = gain_ref[:, at : at + depth]
        tokens = jnp.concatenate(
            [
                stream[:, at : at + depth].astype(jnp.float32) * inverse * gain
                for stream, inverse in zip(streams, inverses)
            ],
            axis=0,
        ).astype(jnp.bfloat16)
        gate = gate + jnp.dot(
            tokens, gate_ref[at : at + depth, :], preferred_element_type=jnp.float32
        )
        up = up + jnp.dot(
            tokens, up_ref[at : at + depth, :], preferred_element_type=jnp.float32
        )
    active = (gate / (1.0 + jnp.exp(-gate)) * up).astype(jnp.bfloat16)
    for at in range(0, width, TILE):
        term = jnp.dot(active, down_ref[:, at : at + TILE], preferred_element_type=jnp.float32)
        store_term(term, at, pieces)


def run_expert(streams, norm_gain, w_gate, w_up, w_down):
    rows, width = streams[0].shape
    hidden = w_gate.shape[1]
    return pl.pallas_call(
        expert_kernel,
        out_shape=term_shapes(rows, width),
        in_specs=[pl.BlockSpec(memory_space=pltpu.VMEM)] * (2 * PIECES + 4),
        out_specs=[pl.BlockSpec(memory_space=pltpu.VMEM)] * (PIECES + 2),
        compiler_params=pltpu.CompilerParams(vmem_limit_bytes=24 * MIB),
        cost_estimate=pl.CostEstimate(
            flops=12 * PIECES * rows * hidden * width,
            bytes_accessed=6 * hidden * width,
            transcendentals=2 * PIECES * rows * hidden,
        ),
        name="expert",
    )(*streams, norm_gain[None], w_gate, w_up, w_down)


def swap(array, distance):
    pairs = [(at, at ^ distance) for at in range(lax.axis_size("experts"))]
    return lax.ppermute(array, "experts", pairs)


def wide(array):
    return array.astype(jnp.float32)


def collect(terms):
    *keeps, first, rest = terms
    rows = first.shape[0]
    rest = swap(rest, 1)
    others = [swap(first, 1)] + [
        rest[at * rows : (at + 1) * rows] for at in range(PIECES - 1)
    ]
    total = 0.0
    for keep, other, distance in zip(keeps, others, SQUARE):
        part = keep + wide(other)
        if distance:
            part = wide(swap(part.astype(jnp.bfloat16), distance))
        total = total + part
    return total


def exchange(total, far):
    own_rows = total.shape[0] // far
    sent = total.astype(jnp.bfloat16)
    for at in range(1, far):
        block = swap(sent, 8 * at)
        total = total + wide(
            jnp.concatenate(
                [block[(to ^ at) * own_rows : ((to ^ at) + 1) * own_rows] for to in range(far)]
            )
        )
    return total.astype(jnp.bfloat16)


def spread(stream):
    own = [stream] + [swap(stream, distance) for distance in SQUARE if distance]
    return own + [swap(piece, 1) for piece in own]


def shards(
    queries,
    cache,
    cache_len,
    residual_in,
    w_absorb,
    w_out,
    norm_gain,
    expert_ids,
    route_gates,
    w_gate,
    w_up,
    w_down,
):
    devices = lax.axis_size("experts")
    rank_here = lax.axis_index("experts")
    own_rows = queries.shape[0]
    all_rows = expert_ids.shape[0]
    far = devices // 8
    split_ways = FF // w_gate.shape[1]
    assert split_ways == 8

    latent = attend(queries, cache, cache_len, devices, w_absorb.shape[1])
    joined = lax.all_to_all(latent, "experts", split_axis=0, concat_axis=0, tiled=True)
    joined = joined.reshape(-1, joined.shape[-1])
    terms = project(joined, w_absorb, residual_in, w_out, all_rows, far)
    stream = exchange(collect(terms), far)
    attended = stream[:own_rows]

    total = collect(run_expert(spread(stream), norm_gain, w_gate, w_up, w_down))
    own_ids = lax.dynamic_slice_in_dim(expert_ids, rank_here * own_rows, own_rows, 0)
    mixings = []
    for at in range(far):
        expert = (rank_here ^ (8 * at)) // split_ways
        mixings.append(
            jnp.sum(
                route_gates * (own_ids == expert).astype(jnp.float32), axis=1, keepdims=True
            )
        )
    expert_out = lax.optimization_barrier(mixings[0] * total[:own_rows])
    for at in range(1, far):
        block = total[at * own_rows : (at + 1) * own_rows].astype(jnp.bfloat16)
        expert_out = expert_out + mixings[at] * wide(swap(block, 8 * at))
    return (attended, expert_out.astype(jnp.bfloat16))


def solution(mesh):
    placed = (
        P(("groups", "experts"), None, None),
        P(("groups", "experts"), None, None),
        P(("groups", "experts")),
        P(("groups", "experts"), None),
        P("experts", None, None),
        P("experts", None),
        P(),
        P("groups", None),
        P(("groups", "experts"), None),
        P(None, "experts"),
        P(None, "experts"),
        P("experts", None),
    )
    return jax.shard_map(
        shards,
        mesh=mesh,
        in_specs=placed,
        out_specs=(P(("groups", "experts"), None), P(("groups", "experts"), None)),
        check_vma=False,
    )
```

```python
import functools

import jax
import jax.numpy as jnp
from jax import lax
from jax.experimental import pallas as pl
from jax.experimental.pallas import tpu as pltpu
from jax.sharding import PartitionSpec as P

QK = 192
FF = 2048
BLOCK = 512
LOWEST = -3e38
GROUP = 4
LANES = 128
TILE = 256
PARTS = 4
SQUARE = (2, 4, 6, 0)
PIECES = len(SQUARE)
MIB = 2**20


def lane_tiles(array):
    return [array[:, at : at + LANES] for at in range(0, array.shape[1], LANES)]


def attend_kernel(
    len_ref,
    queries_ref,
    cache_ref,
    latent_ref,
    length,
    queries,
    held,
    summed,
    highest,
    sums,
    staged,
    item_row,
    item_block,
    length_arrived,
    queries_arrived,
    arrived,
):
    own_rows, heads, _ = queries.shape
    devices, _, rank = staged.shape
    own_heads = heads // devices
    blocks = held.shape[1]

    length_copy = pltpu.make_async_copy(len_ref, length, length_arrived)
    length_copy.start()
    queries_copy = pltpu.make_async_copy(queries_ref, queries, queries_arrived)
    queries_copy.start()

    def block_copy(row, block):
        return pltpu.make_async_copy(
            cache_ref.at[row, :, pl.ds(pl.multiple_of(block * BLOCK, BLOCK), BLOCK)],
            held.at[row, block],
            arrived.at[row, block],
        )

    for row in range(own_rows):
        block_copy(row, 0).start()
        item_row[row] = row
        item_block[row] = 0
    highest[...] = jnp.full_like(highest, LOWEST)
    sums[...] = jnp.zeros_like(sums)
    summed[...] = jnp.zeros_like(summed)
    length_copy.wait()
    items = own_rows
    for row in range(own_rows):
        count = (length[row] + BLOCK - 1) // BLOCK

        def begin(block, first, row=row):
            block_copy(row, block).start()
            item_row[first + block] = row
            item_block[first + block] = block
            return first

        lax.fori_loop(1, count, begin, items - 1)
        items = items + count - 1
    queries_copy.wait()
    column = lax.broadcasted_iota(jnp.int32, (heads, BLOCK), 1)

    def visit(first, many):
        inside = [(item_row[first + at], item_block[first + at]) for at in range(many)]
        for row, block in inside:
            block_copy(row, block).wait()
        found = []
        for row, block in inside:
            score = jnp.dot(
                queries[row], held[row, block], preferred_element_type=jnp.float32
            ) * QK ** (-0.5)
            found.append(
                jnp.where(column + block * BLOCK < length[row], score, -jnp.inf)
            )
        tops = [
            jnp.max(functools.reduce(jnp.maximum, lane_tiles(score)), axis=1, keepdims=True)
            for score in found
        ]
        weights = [jnp.exp(score - top) for score, top in zip(found, tops)]
        terms = [
            lax.dot_general(
                weight.astype(jnp.bfloat16),
                held[row, block, :rank, :],
                (((1,), (1,)), ((), ())),
                preferred_element_type=jnp.float32,
            )
            for (row, block), weight in zip(inside, weights)
        ]
        for (row, _), top, weight, term in zip(inside, tops, weights, terms):
            before = highest[row]
            after = jnp.maximum(before, top)
            old, new = jnp.exp(before - after), jnp.exp(top - after)
            highest[row] = after
            sums[row] = sums[row] * old + sum(lane_tiles(weight)) * new
            for at in range(0, rank, LANES):
                summed[row, :, at : at + LANES] = (
                    summed[row, :, at : at + LANES] * old + term[:, at : at + LANES] * new
                )

    def visit_group(group, _):
        visit(group * GROUP, GROUP)
        return 0

    whole = items // GROUP
    lax.fori_loop(0, whole, visit_group, 0)
    pl.when((items & 2) != 0)(lambda: visit(whole * GROUP, 2))
    pl.when((items & 1) != 0)(lambda: visit(items - 1, 1))
    for row in range(own_rows):
        latent = summed[row] * (1.0 / jnp.sum(sums[row], axis=1, keepdims=True))
        for device in range(devices):
            staged[device, row * own_heads : (row + 1) * own_heads, :] = latent[
                device * own_heads : (device + 1) * own_heads
            ]
    latent_ref[...] = staged[...].astype(latent_ref.dtype)


def attend(queries, cache, cache_len, devices, rank):
    own_rows, depth, heads = queries.shape
    blocks = cache.shape[2] // BLOCK
    packed = own_rows * heads // devices
    listed = own_rows * blocks
    return pl.pallas_call(
        attend_kernel,
        out_shape=jax.ShapeDtypeStruct((devices, packed, rank), jnp.bfloat16),
        in_specs=[pl.BlockSpec(memory_space=pl.ANY)] * 3,
        out_specs=pl.BlockSpec(memory_space=pltpu.VMEM),
        scratch_shapes=[
            pltpu.SMEM((own_rows,), jnp.int32),
            pltpu.VMEM((own_rows, heads, depth), jnp.bfloat16),
            pltpu.VMEM((own_rows, blocks, depth, BLOCK), jnp.bfloat16),
            pltpu.VMEM((own_rows, heads, rank), jnp.float32),
            pltpu.VMEM((own_rows, heads, LANES), jnp.float32),
            pltpu.VMEM((own_rows, heads, LANES), jnp.float32),
            pltpu.VMEM((devices, packed, rank), jnp.float32),
            pltpu.SMEM((listed,), jnp.int32),
            pltpu.SMEM((listed,), jnp.int32),
            pltpu.SemaphoreType.DMA,
            pltpu.SemaphoreType.DMA,
            pltpu.SemaphoreType.DMA((own_rows, blocks)),
        ],
        compiler_params=pltpu.CompilerParams(vmem_limit_bytes=55 * MIB),
        cost_estimate=pl.CostEstimate(
            flops=own_rows * heads * cache.shape[2] * (depth + rank),
            bytes_accessed=cache.size,
            transcendentals=own_rows * heads * cache.shape[2],
        ),
        name="attend",
    )(cache_len, jnp.swapaxes(queries, 1, 2), cache)


def store_term(term, at, refs):
    first = 0
    for ref in refs:
        rows = ref.shape[0]
        ref[:, at : at + TILE] = term[first : first + rows].astype(ref.dtype)
        first += rows


def term_shapes(rows, width):
    kept = [jax.ShapeDtypeStruct((rows, width), jnp.float32)] * PIECES
    sent = [jax.ShapeDtypeStruct((many * rows, width), jnp.bfloat16) for many in (1, PIECES - 1)]
    return kept + sent


def project_kernel(own_rows, far, joined_ref, residual_ref, absorb_ref, w_ref, *pieces):
    own_heads = absorb_ref.shape[0]
    width = w_ref.shape[1]
    shape = (2 * PIECES * pieces[0].shape[0], joined_ref.shape[0])
    row = lax.broadcasted_iota(jnp.int32, shape, 0)
    place = lax.broadcasted_iota(jnp.int32, shape, 1)
    turn = own_rows.bit_length() - 1
    far_bits = far.bit_length() - 1
    request, slot = row & (own_rows - 1), row >> turn
    far_at, slot = slot & (far - 1), slot >> far_bits
    distance = (far_at << 3) + ((slot + 1 & 3) << 1) + (slot >> 2)
    device = distance ^ lax.axis_index("experts")
    choices = []
    for head in range(own_heads):
        wanted = ((device << turn) + request) * own_heads + head
        choices.append((place == wanted).astype(jnp.float32))
    latents = jnp.dot(
        jnp.concatenate(choices, axis=0).astype(jnp.bfloat16),
        joined_ref[...],
        preferred_element_type=jnp.float32,
    ).astype(jnp.bfloat16)
    values = [
        jnp.dot(
            latents[head * shape[0] : (head + 1) * shape[0]],
            absorb_ref[head],
            preferred_element_type=jnp.float32,
        ).astype(jnp.bfloat16)
        for head in range(own_heads)
    ]
    values = jnp.concatenate(values, axis=1)
    for at in range(0, width, TILE):
        term = jnp.dot(values, w_ref[:, at : at + TILE], preferred_element_type=jnp.float32)
        store_term(term, at, pieces)
    residual = residual_ref[...].astype(jnp.float32)
    stays = pieces[PIECES - 1]
    stays[:own_rows, :] = stays[:own_rows, :] + residual


def project(joined, w_absorb, residual_in, w_out, rows, far):
    depth, width = w_out.shape
    own_rows = residual_in.shape[0]
    return pl.pallas_call(
        functools.partial(project_kernel, own_rows, far),
        out_shape=term_shapes(rows // (2 * PIECES), width),
        in_specs=[pl.BlockSpec(memory_space=pltpu.VMEM)] * 4,
        out_specs=[pl.BlockSpec(memory_space=pltpu.VMEM)] * (PIECES + 2),
        compiler_params=pltpu.CompilerParams(vmem_limit_bytes=24 * MIB),
        cost_estimate=pl.CostEstimate(
            flops=2 * rows * depth * width, bytes_accessed=2 * depth * width, transcendentals=0
        ),
        name="project",
    )(joined, residual_in, w_absorb, w_out)


def expert_kernel(*refs):
    count = 2 * PIECES
    streams, (gain_ref, gate_ref, up_ref, down_ref) = refs[:count], refs[count : count + 4]
    pieces = refs[count + 4 :]
    streams = streams[1:PIECES] + streams[:1] + streams[PIECES + 1 :] + streams[PIECES : PIECES + 1]
    width = gain_ref.shape[1]
    depth = width // PARTS
    inverses = []
    for stream in streams:
        squares = 0.0
        for at in range(0, width, depth):
            piece = stream[:, at : at + depth].astype(jnp.float32)
            squares = squares + sum(lane_tiles(piece * piece))
        mean = jnp.sum(squares, axis=1, keepdims=True) / width
        inverses.append(lax.rsqrt(mean + 1e-06))
    gate, up = 0.0, 0.0
    for at in range(0, width, depth):
        gain = gain_ref[:, at : at + depth]
        tokens = jnp.concatenate(
            [
                stream[:, at : at + depth].astype(jnp.float32) * inverse * gain
                for stream, inverse in zip(streams, inverses)
            ],
            axis=0,
        ).astype(jnp.bfloat16)
        gate = gate + jnp.dot(
            tokens, gate_ref[at : at + depth, :], preferred_element_type=jnp.float32
        )
        up = up + jnp.dot(
            tokens, up_ref[at : at + depth, :], preferred_element_type=jnp.float32
        )
    active = (gate / (1.0 + jnp.exp(-gate)) * up).astype(jnp.bfloat16)
    for at in range(0, width, TILE):
        term = jnp.dot(active, down_ref[:, at : at + TILE], preferred_element_type=jnp.float32)
        store_term(term, at, pieces)


def run_expert(streams, norm_gain, w_gate, w_up, w_down):
    rows, width = streams[0].shape
    hidden = w_gate.shape[1]
    return pl.pallas_call(
        expert_kernel,
        out_shape=term_shapes(rows, width),
        in_specs=[pl.BlockSpec(memory_space=pltpu.VMEM)] * (2 * PIECES + 4),
        out_specs=[pl.BlockSpec(memory_space=pltpu.VMEM)] * (PIECES + 2),
        compiler_params=pltpu.CompilerParams(vmem_limit_bytes=24 * MIB),
        cost_estimate=pl.CostEstimate(
            flops=12 * PIECES * rows * hidden * width,
            bytes_accessed=6 * hidden * width,
            transcendentals=2 * PIECES * rows * hidden,
        ),
        name="expert",
    )(*streams, norm_gain[None], w_gate, w_up, w_down)


def swap(array, distance):
    pairs = [(at, at ^ distance) for at in range(lax.axis_size("experts"))]
    return lax.ppermute(array, "experts", pairs)


def wide(array):
    return array.astype(jnp.float32)


def collect(terms):
    *keeps, first, rest = terms
    rows = first.shape[0]
    rest = swap(rest, 1)
    others = [swap(first, 1)] + [
        rest[at * rows : (at + 1) * rows] for at in range(PIECES - 1)
    ]
    total = 0.0
    for keep, other, distance in zip(keeps, others, SQUARE):
        part = keep + wide(other)
        if distance:
            part = wide(swap(part.astype(jnp.bfloat16), distance))
        total = total + part
    return total


def exchange(total, far):
    own_rows = total.shape[0] // far
    sent = total.astype(jnp.bfloat16)
    for at in range(1, far):
        block = swap(sent, 8 * at)
        total = total + wide(
            jnp.concatenate(
                [block[(to ^ at) * own_rows : ((to ^ at) + 1) * own_rows] for to in range(far)]
            )
        )
    return total.astype(jnp.bfloat16)


def spread(stream):
    own = [stream] + [swap(stream, distance) for distance in SQUARE if distance]
    return own + [swap(piece, 1) for piece in own]


def shards(
    queries,
    cache,
    cache_len,
    residual_in,
    w_absorb,
    w_out,
    norm_gain,
    expert_ids,
    route_gates,
    w_gate,
    w_up,
    w_down,
):
    devices = lax.axis_size("experts")
    rank_here = lax.axis_index("experts")
    own_rows = queries.shape[0]
    all_rows = expert_ids.shape[0]
    far = devices // 8
    split_ways = FF // w_gate.shape[1]
    assert split_ways == 8

    latent = attend(queries, cache, cache_len, devices, w_absorb.shape[1])
    joined = lax.all_to_all(latent, "experts", split_axis=0, concat_axis=0, tiled=True)
    joined = joined.reshape(-1, joined.shape[-1])
    terms = project(joined, w_absorb, residual_in, w_out, all_rows, far)
    stream = exchange(collect(terms), far)
    attended = stream[:own_rows]

    total = collect(run_expert(spread(stream), norm_gain, w_gate, w_up, w_down))
    own_ids = lax.dynamic_slice_in_dim(expert_ids, rank_here * own_rows, own_rows, 0)
    mixings = []
    for at in range(far):
        expert = (rank_here ^ (8 * at)) // split_ways
        mixings.append(
            jnp.sum(
                route_gates * (own_ids == expert).astype(jnp.float32), axis=1, keepdims=True
            )
        )
    expert_out = lax.optimization_barrier(mixings[0] * total[:own_rows])
    for at in range(1, far):
        block = total[at * own_rows : (at + 1) * own_rows].astype(jnp.bfloat16)
        expert_out = expert_out + mixings[at] * wide(swap(block, 8 * at))
    return (attended, expert_out.astype(jnp.bfloat16))


def solution(mesh):
    placed = (
        P(("groups", "experts"), None, None),
        P(("groups", "experts"), None, None),
        P(("groups", "experts")),
        P(("groups", "experts"), None),
        P("experts", None, None),
        P("experts", None),
        P(),
        P("groups", None),
        P(("groups", "experts"), None),
        P(None, "experts"),
        P(None, "experts"),
        P("experts", None),
    )
    return jax.shard_map(
        shards,
        mesh=mesh,
        in_specs=placed,
        out_specs=(P(("groups", "experts"), None), P(("groups", "experts"), None)),
        check_vma=False,
    )
```
